128 devices in a mesh: dp: 8 (over z_hi, y), tensor: 16 (over x, z_lo, core).
Axes of the slice: x: 4, y: 4, z: 4 (z_hi: 2, z_lo: 2; z = z_hi * 2 + z_lo), core: 2. Of those that a mesh axis runs over, the one named last changes fastest.
Arguments:
- tokens: bfloat16 [16, 1024, 2048], P('dp', 'tensor'), may hold values from -6 to 6
- attn_weight: bfloat16 [2048, 6144], P('dp', 'tensor'), may hold values from -0.125 to 0.125
- attn_bias: float32 [6144], P('tensor'), may hold values from -3 to 3
- dense_weight: bfloat16 [2048, 2048], P('tensor', 'dp'), may hold values from -0.75 to 0.75
- dense_bias: float32 [2048], replicated, may hold values from -3 to 3
- up_weight: bfloat16 [2048, 8192], P('dp', 'tensor'), may hold values from -0.125 to 0.125
- up_bias: float32 [8192], P('tensor'), may hold values from -3 to 3
- down_weight: bfloat16 [8192, 2048], P('tensor', 'dp'), may hold values from -0.0625 to 0.0625
- down_bias: float32 [2048], replicated, may hold values from -3 to 3
- norm_gain: float32 [2048], replicated, may hold values from 0.5 to 1.5
- norm_bias: float32 [2048], replicated, may hold values from -2 to 2
- cotangent: bfloat16 [16, 1024, 2048], P('dp', 'tensor'), may hold values from -6 to 6
Outputs:
- layer_out: bfloat16 [16, 1024, 2048], P('dp', 'tensor')
- grad_tokens: float32 [16, 1024, 2048], P('dp', 'tensor')
- attn_weight_grad: float32 [2048, 6144], P('dp', 'tensor')
- attn_bias_grad: float32 [6144], P('tensor')
- dense_weight_grad: float32 [2048, 2048], P('tensor', 'dp')
- dense_bias_grad: float32 [2048], replicated
- up_weight_grad: float32 [2048, 8192], P('dp', 'tensor')
- up_bias_grad: float32 [8192], P('tensor')
- down_weight_grad: float32 [8192, 2048], P('tensor', 'dp')
- down_bias_grad: float32 [2048], replicated
- norm_gain_grad: float32 [2048], replicated
- norm_bias_grad: float32 [2048], replicated
The draws below stay inside these ranges and needn't reach their ends.
All inputs are finite; a program needn't handle non-finite values.
Results may differ from the reference program's by a relative error of at most 0.0089.
Values may be sent and summed in bfloat16 or wider, within the bound.
No kernel may reach another device: no remote copies, remote signals or barrier semaphores. Data moves between devices by JAX's collectives and lax.ppermute only.
A program may use at most 192 MiB of HBM per device.

```python
import jax
import jax.numpy as jnp
from jax import lax

D = 2048
HEADS = 32
HEAD_DIM = 64
ROT = 32
FF = 8192
LEN = 1024
BLOCK = 512
BATCH = 16


def levels(rng, dims, shards, low, largest):
    level = 1.0
    for axis_at, shards_of in shards:
        steps = jax.random.uniform(jax.random.fold_in(jax.random.fold_in(rng, 6), axis_at), (shards_of,), jnp.float32, low / len(shards), largest / len(shards))
        level = level * jnp.repeat(jnp.exp(steps), dims[axis_at] // shards_of).reshape((-1,) + (1,) * (len(dims) - 1 - axis_at))
    return level


def normal_values(key, extent, deviation, reach, split=(), held_as=jnp.bfloat16):
    level = levels(key, extent, split, -0.22, 0.18) if split else 1.0
    values = jax.random.normal(key, extent, jnp.float32) * deviation * level
    return jnp.minimum(jnp.maximum(values, -reach), reach).astype(held_as)


def setup_inputs(seed: int = 0) -> dict:
    seeds = jax.random.split(jax.random.key(seed), 13)
    return {
        "tokens": normal_values(seeds[0], (BATCH, LEN, D), 1.0, 6.0, ((0, 8), (1, 16))),
        "attn_weight": normal_values(seeds[1], (D, 3 * D), D ** -0.5, 0.125, ((0, 8), (1, 16))),
        "attn_bias": normal_values(seeds[2], (3 * D,), 0.5, 3.0, ((0, 16),), jnp.float32),
        "dense_weight": normal_values(seeds[3], (D, D), (D // 32) ** -0.5, 0.75, ((0, 16), (1, 8))),
        "dense_bias": normal_values(seeds[4], (D,), 0.5, 3.0, (), jnp.float32),
        "up_weight": normal_values(seeds[5], (D, FF), D ** -0.5, 0.125, ((0, 8), (1, 16))),
        "up_bias": normal_values(seeds[6], (FF,), 0.5, 3.0, ((0, 16),), jnp.float32),
        "down_weight": normal_values(seeds[7], (FF, D), FF ** -0.5, 0.0625, ((0, 16), (1, 8))),
        "down_bias": normal_values(seeds[8], (D,), 0.5, 3.0, (), jnp.float32),
        "norm_gain": jnp.clip(1.0 + 0.1 * jax.random.normal(seeds[9], (D,), jnp.float32), 0.5, 1.5),
        "norm_bias": normal_values(seeds[10], (D,), 0.3, 2.0, (), jnp.float32),
        "cotangent": normal_values(seeds[11], (BATCH, LEN, D), 1.0, 6.0, ((0, 8), (1, 16))),
    }


highest = lax.Precision.HIGHEST
epsilon = 1e-05

@jax.custom_vjp
def low(v):
    return lax.optimization_barrier(v.astype(jnp.bfloat16)).astype(jnp.float32)

@jax.custom_vjp
def low_back(v):
    return v

def low_keep(v):
    return (low(v), None)

def low_pass(kept, grad):
    return (grad,)

def back_keep(v):
    return (v, None)

def back_low(kept, grad):
    return (low(grad),)
low.defvjp(low_keep, low_pass)
low_back.defvjp(back_keep, back_low)

def normalize(rows_in, norm_gain, norm_bias):
    average = lax.optimization_barrier(jnp.mean(rows_in, axis=-1, keepdims=True))
    centred = rows_in - average
    spread = lax.optimization_barrier(jnp.mean(centred * centred, axis=-1, keepdims=True))
    return centred * lax.rsqrt(spread + epsilon) * norm_gain + norm_bias

def rotary_tables(length):
    half_rot = ROT // 2
    frequency = 10000.0 ** (-(jnp.arange(half_rot, dtype=jnp.float32) * 2.0 / ROT))
    angles = jnp.arange(length, dtype=jnp.float32)[:, None] * frequency[None, :]
    return (jnp.cos(angles), jnp.sin(angles))

def rotate(operand, cosine_table, sine_table):
    half_rot = ROT // 2
    first_half = operand[..., :half_rot]
    second_half = operand[..., half_rot:ROT]
    return jnp.concatenate([first_half * cosine_table - second_half * sine_table, second_half * cosine_table + first_half * sine_table, operand[..., ROT:]], axis=-1)

def attention(queries, keys_all, values_all):
    blocks = LEN // BLOCK
    factor = HEAD_DIM ** (-0.5)
    positions = jnp.arange(LEN, dtype=jnp.int32)

    def one_block(block_index):
        row_start = (block_index * BLOCK).astype(jnp.int32)
        query_rows = lax.dynamic_slice_in_dim(queries, row_start, BLOCK, 1)
        scores = low_back(jnp.einsum('hqd,hkd->hqk', query_rows, keys_all, precision=highest) * factor)
        query_pos = row_start + jnp.arange(BLOCK, dtype=jnp.int32)
        allowed = positions[None, :] <= query_pos[:, None]
        probab = jax.nn.softmax(jnp.where(allowed, scores, -jnp.inf), axis=-1)
        return jnp.einsum('hqk,hkd->hqd', low(probab), values_all, precision=highest)
    gathered = lax.map(jax.checkpoint(one_block), jnp.arange(blocks, dtype=jnp.int32))
    return gathered.transpose(1, 0, 2, 3).reshape(HEADS, LEN, HEAD_DIM)

def layer(rows_in, attn_weight, attn_bias, dense_weight, dense_bias, up_weight, up_bias, down_weight, down_bias, norm_gain, norm_bias):
    normed = normalize(rows_in, norm_gain, norm_bias)
    activations = low(normed)
    projected = low_back(jnp.dot(activations, attn_weight, precision=highest) + attn_bias)
    shaped = projected.reshape(LEN, HEADS, 3, HEAD_DIM).transpose(2, 1, 0, 3)
    cosine_table, sine_table = rotary_tables(LEN)
    queries = low(rotate(shaped[0], cosine_table, sine_table))
    keys_all = low(rotate(shaped[1], cosine_table, sine_table))
    values_all = low(shaped[2])
    attended = attention(queries, keys_all, values_all)
    merged = low(low_back(attended.transpose(1, 0, 2).reshape(LEN, HEADS * HEAD_DIM)))
    hidden = low_back(jnp.dot(activations, up_weight, precision=highest) + up_bias)
    active = low(jax.nn.gelu(hidden, approximate=True))
    branch = jnp.dot(merged, dense_weight, precision=highest) + jnp.dot(active, down_weight, precision=highest)
    return rows_in + branch + dense_bias + down_bias

def reference(tokens, attn_weight, attn_bias, dense_weight, dense_bias, up_weight, up_bias, down_weight, down_bias, norm_gain, norm_bias, cotangent):
    params = tuple((array_in.astype(jnp.float32) for array_in in (attn_weight, attn_bias, dense_weight, dense_bias, up_weight, up_bias, down_weight, down_bias, norm_gain, norm_bias)))

    def forward(inputs, *weights):

        def scan_step(state_in, sequence):
            return (state_in, layer(sequence, *weights))
        unused, result = lax.scan(scan_step, jnp.zeros((), jnp.float32), inputs)
        return result
    result, pullback = jax.vjp(forward, tokens.astype(jnp.float32), *params)
    gradients = pullback(cotangent.astype(jnp.float32))
    return (result.astype(jnp.bfloat16), gradients[0], gradients[1], gradients[2], gradients[3], gradients[4], gradients[5], gradients[6], gradients[7], gradients[8], gradients[9], gradients[10])
```

```python
import functools

import jax
import jax.numpy as jnp
import numpy as np
from jax import lax
from jax.experimental import pallas as pl
from jax.experimental.pallas import tpu as pltpu
from jax.sharding import PartitionSpec as P

HEAD_DIM = 64
ROT = 32
EPS = 1e-05
BF = jnp.bfloat16
F32 = jnp.float32

OFFSETS = (0, -1, 1, 2)


def tensor_index(x, zlo, core):
    return (x % 4) * 4 + (zlo % 2) * 2 + core % 2


def dp_index(zhi, y):
    return (zhi % 2) * 4 + y % 4


def tensor_move(dx, dz, dc):
    return [
        (tensor_index(x, z, c), tensor_index(x + dx, z + dz, c + dc))
        for x in range(4)
        for z in range(2)
        for c in range(2)
    ]


def dp_move(dz, dy):
    return [(dp_index(z, y), dp_index(z + dz, y + dy)) for z in range(2) for y in range(4)]


def x_up(a):
    return lax.ppermute(a, "tensor", tensor_move(1, 0, 0))


def x_down(a):
    return lax.ppermute(a, "tensor", tensor_move(-1, 0, 0))


def z_swap(a):
    return lax.ppermute(a, "tensor", tensor_move(0, 1, 0))


def core_swap(a):
    return lax.ppermute(a, "tensor", tensor_move(0, 0, 1))


def y_up(a):
    return lax.ppermute(a, "dp", dp_move(0, 1))


def y_down(a):
    return lax.ppermute(a, "dp", dp_move(0, -1))


def zz_swap(a):
    return lax.ppermute(a, "dp", dp_move(1, 0))


def gather_blocks(a, up, down, swap):
    z = swap(a)
    left_a, right_a = up(a), down(a)
    left_z, right_z = up(z), down(z)
    far_a, far_z = up(left_a), down(right_z)
    return [a, z, left_a, left_z, right_a, right_z, far_a, far_z]


def reduce_blocks(blocks, up, down, swap):
    own_a, own_z, left_a, left_z, right_a, right_z, far_a, far_z = blocks
    from_left, from_right = up(far_a), down(far_z)
    send_up = (right_a.astype(F32) + from_left.astype(F32)).astype(BF)
    send_down = (left_z.astype(F32) + from_right.astype(F32)).astype(BF)
    up_a, up_z = up(send_up), up(right_z)
    down_a, down_z = down(left_a), down(send_down)
    other = own_z.astype(F32) + up_z.astype(F32) + down_z.astype(F32)
    mine = own_a.astype(F32) + up_a.astype(F32) + down_a.astype(F32)
    return mine + swap(other.astype(BF)).astype(F32)


def vmem(count):
    return [pl.BlockSpec(memory_space=pltpu.VMEM)] * count


def smem():
    return pl.BlockSpec(memory_space=pltpu.SMEM)


def params(**kwargs):
    return pltpu.CompilerParams(vmem_limit_bytes=60 * 1024 * 1024, **kwargs)


def cost(flops, nbytes, trans=0):
    return pl.CostEstimate(flops=flops, bytes_accessed=nbytes, transcendentals=trans)


def pre_body(sc, tok, cot, gain, bias, acts_out, cot_out, cotsum, hold):
    total = jnp.zeros(cotsum.shape, F32)
    for s in range(2):
        seq = sc[8] if s == 0 else 1 - sc[8]
        xin = tok[seq].astype(F32)
        centred = xin - jnp.mean(xin, axis=-1, keepdims=True)
        spread = jnp.mean(centred * centred, axis=-1, keepdims=True)
        hold[...] = (centred * lax.rsqrt(spread + EPS) * gain[...] + bias[...]).astype(BF)
        total = total + jnp.sum(cot[seq].astype(F32), axis=0, keepdims=True)
        for r in range(8):
            cols = pl.ds(pl.multiple_of(sc[r] * 256, 256), 256)
            acts_out[s, :, r * 256 : (r + 1) * 256] = hold[:, cols]
            cot_out[s, :, r * 256 : (r + 1) * 256] = cot[seq, :, cols]
    cotsum[...] = total


def pre(sc, tok, cot, gain, bias):
    width = tok.shape[-1]
    return pl.pallas_call(
        pre_body,
        in_specs=[smem()] + vmem(4),
        out_specs=vmem(3),
        out_shape=[
            jax.ShapeDtypeStruct(tok.shape, BF),
            jax.ShapeDtypeStruct(tok.shape, BF),
            jax.ShapeDtypeStruct((1, width), F32),
        ],
        scratch_shapes=[pltpu.VMEM(tok.shape[1:], BF)],
        compiler_params=params(),
        cost_estimate=cost(4000000, 2000000),
        name="pre",
    )(sc, tok, cot, gain, bias)


def post_out_body(sc, tok, branch, extra, out, hold):
    for s in range(2):
        seq = sc[8] if s == 0 else 1 - sc[8]
        for r in range(8):
            cols = pl.ds(pl.multiple_of(sc[r] * 256, 256), 256)
            hold[:, cols] = branch[s, :, r * 256 : (r + 1) * 256].astype(F32)
        out[seq] = (tok[seq].astype(F32) + hold[...] + extra[...]).astype(BF)


def post_out(sc, tok, branch, extra):
    return pl.pallas_call(
        post_out_body,
        in_specs=[smem()] + vmem(3),
        out_specs=pl.BlockSpec(memory_space=pltpu.VMEM),
        out_shape=jax.ShapeDtypeStruct(tok.shape, BF),
        scratch_shapes=[pltpu.VMEM(tok.shape[1:], F32)],
        compiler_params=params(),
        cost_estimate=cost(1000000, 2000000),
        name="post_out",
    )(sc, tok, branch, extra)


def post_grad_body(sc, tok, cot, gnormed, gain, out, sums, hold):
    gain_sum = jnp.zeros((1, gain.shape[1]), F32)
    bias_sum = jnp.zeros((1, gain.shape[1]), F32)
    for s in range(2):
        seq = sc[8] if s == 0 else 1 - sc[8]
        for r in range(8):
            cols = pl.ds(pl.multiple_of(sc[r] * 256, 256), 256)
            hold[:, cols] = gnormed[s, :, r * 256 : (r + 1) * 256].astype(F32)
        gn = hold[...]
        xin = tok[seq].astype(F32)
        centred = xin - jnp.mean(xin, axis=-1, keepdims=True)
        scale = lax.rsqrt(jnp.mean(centred * centred, axis=-1, keepdims=True) + EPS)
        xhat = centred * scale
        e = gn * gain[...]
        mean_e = jnp.mean(e, axis=-1, keepdims=True)
        mean_x = jnp.mean(e * xhat, axis=-1, keepdims=True)
        out[seq] = cot[seq].astype(F32) + (e - mean_e - xhat * mean_x) * scale
        gain_sum = gain_sum + jnp.sum(xhat * gn, axis=0, keepdims=True)
        bias_sum = bias_sum + jnp.sum(gn, axis=0, keepdims=True)
    sums[0:1, :] = gain_sum
    sums[1:2, :] = bias_sum


def post_grad(sc, tok, cot, gnormed, gain):
    width = tok.shape[-1]
    return pl.pallas_call(
        post_grad_body,
        in_specs=[smem()] + vmem(4),
        out_specs=vmem(2),
        out_shape=[jax.ShapeDtypeStruct(tok.shape, F32), jax.ShapeDtypeStruct((2, width), F32)],
        scratch_shapes=[pltpu.VMEM(tok.shape[1:], F32)],
        compiler_params=params(),
        cost_estimate=cost(4000000, 3000000),
        name="post_grad",
    )(sc, tok, cot, gnormed, gain)


def turn(u, cosine, sine_low, sine_high):
    return (
        u * cosine
        + pltpu.roll(u, u.shape[-1] - ROT // 2, 1) * sine_low
        + pltpu.roll(u, ROT // 2, 1) * sine_high
    )


def turn_back(u, cosine, sine_low, sine_high):
    return (
        u * cosine
        - pltpu.roll(u, u.shape[-1] - ROT // 2, 1) * sine_low
        - pltpu.roll(u, ROT // 2, 1) * sine_high
    )


def dot(a, b):
    return lax.dot_general(a, b, (((1,), (0,)), ((), ())), preferred_element_type=F32)


def dot_nt(a, b):
    return lax.dot_general(a, b, (((1,), (1,)), ((), ())), preferred_element_type=F32)


def dot_tn(a, b):
    return lax.dot_general(a, b, (((0,), (0,)), ((), ())), preferred_element_type=F32)


QB = 256


def diagonal(size):
    keys = lax.broadcasted_iota(jnp.int32, (size, size), 0)
    queries = lax.broadcasted_iota(jnp.int32, (size, size), 1)
    return keys <= queries


def attn_fwd_body(sc, qkv, bias, cos_t, low_t, high_t, merged, q_out, k_out, v_out, lse, hold):
    length = qkv.shape[0]
    for r in range(length // 64):
        here = slice(64 * r, 64 * r + 64)
        there = pl.ds(pl.multiple_of(sc[r] * 64, 64), 64)
        tables = (cos_t[here, :], low_t[here, :], high_t[here, :])
        rows = qkv[here, :] + bias[0]
        q_out[0, there, :] = (turn(rows[:, :128], *tables) * (HEAD_DIM**-0.5)).astype(BF)
        k_out[0, there, :] = turn(rows[:, 128:256], *tables).astype(BF)
        v_out[0, there, :] = rows[:, 256:].astype(BF)
    keys = k_out[0]
    values_t = v_out[0].T
    lane = lax.broadcasted_iota(jnp.int32, (QB, 128), 1)
    allowed = diagonal(QB)
    for b in range(length // QB):
        begin, end = b * QB, (b + 1) * QB
        query = q_out[0, begin:end, :]
        for a in range(2):
            only = jnp.where(lane // HEAD_DIM == a, query, jnp.zeros_like(query))
            scores = dot_nt(keys[:end], only)
            low = jnp.where(allowed, scores[begin:], -jnp.inf)
            top = jnp.max(low, axis=0, keepdims=True)
            if b > 0:
                top = jnp.maximum(top, jnp.max(scores[:begin], axis=0, keepdims=True))
            weights = jnp.exp(low - top)
            total = jnp.sum(weights, axis=0, keepdims=True)
            out = dot(values_t[:, begin:end], weights.astype(BF))
            if b > 0:
                weights = jnp.exp(scores[:begin] - top)
                total = total + jnp.sum(weights, axis=0, keepdims=True)
                out = out + dot(values_t[:, :begin], weights.astype(BF))
            out = out * (1.0 / total)
            hold[a * HEAD_DIM : (a + 1) * HEAD_DIM, begin:end] = out[
                a * HEAD_DIM : (a + 1) * HEAD_DIM, :
            ]
            lse[0, a : a + 1, begin:end] = top + jnp.log(total)
    for r in range(length // 128):
        here = slice(128 * r, 128 * r + 128)
        merged_abs = hold[:, here].T.astype(BF)
        for k in range(2):
            to = pl.ds(pl.multiple_of(sc[16 + 2 * r + k] * 64, 64), 64)
            merged[to, :] = merged_abs[64 * k : 64 * k + 64, :]


def attn_fwd(sc, qkv, bias, cos_t, low_t, high_t):
    length = qkv.shape[0]
    whole = lambda shape: pl.BlockSpec(shape, lambda h: (0,) * len(shape))
    saved = pl.BlockSpec((1, length, 128), lambda h: (h, 0, 0))
    saved_shape = jax.ShapeDtypeStruct((2, length, 128), BF)
    return pl.pallas_call(
        attn_fwd_body,
        grid=(2,),
        in_specs=[
            smem(),
            pl.BlockSpec((length, 384), lambda h: (0, h)),
            pl.BlockSpec((1, 1, 384), lambda h: (h, 0, 0)),
            whole((length, 128)),
            whole((length, 128)),
            whole((length, 128)),
        ],
        out_specs=[
            pl.BlockSpec((length, 128), lambda h: (0, h)),
            saved,
            saved,
            saved,
            pl.BlockSpec((1, 2, length), lambda h: (h, 0, 0)),
        ],
        out_shape=[
            jax.ShapeDtypeStruct((length, 256), BF),
            saved_shape,
            saved_shape,
            saved_shape,
            jax.ShapeDtypeStruct((2, 2, length), F32),
        ],
        scratch_shapes=[pltpu.VMEM((128, length), F32)],
        compiler_params=params(),
        cost_estimate=cost(8000000000, 6000000, 4000000),
        name="attn_fwd",
    )(sc, qkv, bias, cos_t, low_t, high_t)


def attn_bwd_body(
    sc, q_in, k_in, v_in, lse, gm_in, cos_t, low_t, high_t, gqkv, colsum, gm_hold, dq_t, dq, dk, dv
):
    length = gm_in.shape[0]
    for r in range(length // 64):
        there = pl.ds(pl.multiple_of(sc[r] * 64, 64), 64)
        gm_hold[there, :] = gm_in[64 * r : 64 * r + 64, :]
    keys = k_in[0]
    values = v_in[0]
    keys_t = keys.T
    dk[...] = jnp.zeros_like(dk)
    dv[...] = jnp.zeros_like(dv)
    lane = lax.broadcasted_iota(jnp.int32, (QB, 128), 1)
    allowed = diagonal(QB)
    for b in range(length // QB):
        begin, end = b * QB, (b + 1) * QB
        query = q_in[0, begin:end, :]
        grad = gm_hold[begin:end, :]
        for a in range(2):
            mine = lane // HEAD_DIM == a
            only = jnp.where(mine, query, jnp.zeros_like(query))
            grad_only = jnp.where(mine, grad, jnp.zeros_like(grad))
            shift = lse[0, a : a + 1, begin:end]
            scores = dot_nt(keys[:end], only)
            dprobs = dot_nt(values[:end], grad_only)
            low_p = jnp.where(allowed, jnp.exp(scores[begin:] - shift), 0.0)
            delta = jnp.sum(low_p * dprobs[begin:], axis=0, keepdims=True)
            if b > 0:
                high_p = jnp.exp(scores[:begin] - shift)
                delta = delta + jnp.sum(high_p * dprobs[:begin], axis=0, keepdims=True)
            low_g = (low_p * (dprobs[begin:] - delta)).astype(BF)
            dv[begin:end, :] += dot(low_p.astype(BF), grad_only)
            dk[begin:end, :] += dot(low_g, only)
            out = dot(keys_t[:, begin:end], low_g)
            if b > 0:
                high_g = (high_p * (dprobs[:begin] - delta)).astype(BF)
                dv[:begin, :] += dot(high_p.astype(BF), grad_only)
                dk[:begin, :] += dot(high_g, only)
                out = out + dot(keys_t[:, :begin], high_g)
            dq_t[a * HEAD_DIM : (a + 1) * HEAD_DIM, begin:end] = out[
                a * HEAD_DIM : (a + 1) * HEAD_DIM, :
            ]
    for r in range(length // 128):
        here = slice(128 * r, 128 * r + 128)
        dq[here, :] = dq_t[:, here].T
    total = jnp.zeros((1, 384), F32)
    for r in range(length // 64):
        here = slice(64 * r, 64 * r + 64)
        there = pl.ds(pl.multiple_of(sc[r] * 64, 64), 64)
        tables = (cos_t[here, :], low_t[here, :], high_t[here, :])
        gq = turn_back(dq[there, :] * (HEAD_DIM**-0.5), *tables)
        gk = turn_back(dk[there, :], *tables)
        rows = jnp.concatenate([gq, gk, dv[there, :]], axis=1).astype(BF)
        gqkv[here, :] = rows
        total = total + jnp.sum(rows.astype(F32), axis=0, keepdims=True)
    colsum[0] = total


def attn_bwd(sc, q, k, v, lse, gm, cos_t, low_t, high_t):
    length = gm.shape[0]
    whole = lambda shape: pl.BlockSpec(shape, lambda h: (0,) * len(shape))
    saved = pl.BlockSpec((1, length, 128), lambda h: (h, 0, 0))
    return pl.pallas_call(
        attn_bwd_body,
        grid=(2,),
        in_specs=[
            smem(),
            saved,
            saved,
            saved,
            pl.BlockSpec((1, 2, length), lambda h: (h, 0, 0)),
            pl.BlockSpec((length, 128), lambda h: (0, h)),
            whole((length, 128)),
            whole((length, 128)),
            whole((length, 128)),
        ],
        out_specs=[
            pl.BlockSpec((length, 384), lambda h: (0, h)),
            pl.BlockSpec((1, 1, 384), lambda h: (h, 0, 0)),
        ],
        out_shape=[
            jax.ShapeDtypeStruct((length, 768), BF),
            jax.ShapeDtypeStruct((2, 1, 384), F32),
        ],
        scratch_shapes=[
            pltpu.VMEM((length, 128), BF),
            pltpu.VMEM((128, length), F32),
            pltpu.VMEM((length, 128), F32),
            pltpu.VMEM((length, 128), F32),
            pltpu.VMEM((length, 128), F32),
        ],
        compiler_params=params(),
        cost_estimate=cost(16000000000, 6000000, 4000000),
        name="attn_bwd",
    )(sc, q, k, v, lse, gm, cos_t, low_t, high_t)


def rotary_tables(positions):
    frequency = 10000.0 ** (-(jnp.arange(ROT // 2, dtype=F32) * 2.0 / ROT))
    angles = positions.astype(F32)[:, None] * frequency[None, :]
    cosine, sine = jnp.cos(angles), jnp.sin(angles)
    one = jnp.ones((positions.shape[0], HEAD_DIM - ROT), F32)
    zero_half, zero = jnp.zeros_like(sine), jnp.zeros_like(one)
    cos_t = jnp.concatenate([cosine, cosine, one] * 2, axis=1)
    low_t = jnp.concatenate([-sine, zero_half, zero] * 2, axis=1)
    high_t = jnp.concatenate([zero_half, sine, zero] * 2, axis=1)
    return cos_t, low_t, high_t


def by_kind(a):
    lead = a.shape[:-1]
    return jnp.swapaxes(a.reshape(lead + (2, 3, HEAD_DIM)), -3, -2).reshape(lead + (384,))


def by_head(a):
    lead = a.shape[:-1]
    return jnp.swapaxes(a.reshape(lead + (3, 2, HEAD_DIM)), -3, -2).reshape(lead + (384,))


def gelu(h):
    return jax.nn.gelu(h, approximate=True)


def after(value, *others):
    return lax.optimization_barrier((value,) + others)[0]


def shards(
    tokens,
    attn_weight,
    attn_bias,
    dense_weight,
    dense_bias,
    up_weight,
    up_bias,
    down_weight,
    down_bias,
    norm_gain,
    norm_bias,
    cotangent,
):
    t, d = lax.axis_index("tensor"), lax.axis_index("dp")
    x, zlo, core = t // 4, (t // 2) % 2, t % 2
    zhi, y = d // 4, d % 4
    features = [((zhi + j) % 2) * 4 + (y + o) % 4 for o in OFFSETS for j in range(2)]
    sc = jnp.stack(features + [core]).astype(jnp.int32)
    row_blocks = [
        4 * ((x + o) % 4) + 2 * ((zlo + j) % 2) + (core + k) % 2
        for o in OFFSETS
        for j in range(2)
        for k in range(2)
    ]
    row_table = jnp.stack(row_blocks).astype(jnp.int32)
    inverse = jnp.zeros((16,), jnp.int32).at[row_table].set(jnp.arange(16, dtype=jnp.int32))
    rows_sc = jnp.concatenate([row_table, inverse])
    positions = (row_table[:, None] * 64 + jnp.arange(64, dtype=jnp.int32)[None, :]).reshape(-1)
    tables = rotary_tables(positions)
    gain_row, bias_row = norm_gain[None, :], norm_bias[None, :]

    first = jnp.concatenate([by_kind(attn_weight), up_weight], axis=1)
    second = jnp.concatenate([dense_weight, down_weight], axis=0)
    biases = jnp.concatenate([by_kind(attn_bias), up_bias])[None, :]
    other_biases = core_swap(biases)

    acts_own, cot_own, cot_sum = pre(sc, tokens, cotangent, gain_row, bias_row)
    acts_piece = jnp.concatenate([acts_own[0], core_swap(acts_own[1])], axis=0)
    cot_piece = jnp.concatenate([cot_own[0], core_swap(cot_own[1])], axis=0)

    first_blocks = gather_blocks(first, y_up, y_down, zz_swap)
    acts_blocks = gather_blocks(acts_piece, x_up, x_down, z_swap)
    second_blocks = gather_blocks(after(second, first_blocks[2], first_blocks[4]), y_up, y_down, zz_swap)
    cot_blocks = gather_blocks(
        after(cot_piece, acts_blocks[2], acts_blocks[4]), x_up, x_down, z_swap
    )
    out_bias_grad = lax.psum(cot_sum[0], ("dp", "tensor"))

    acts = jnp.concatenate(acts_blocks, axis=0)
    w1_own = jnp.concatenate(first_blocks, axis=0)
    w1_other = core_swap(w1_own)
    w_attn = jnp.concatenate([w1_own[:, :384], w1_other[:, :384]], axis=1)
    w_up = jnp.concatenate([w1_own[:, 384:], w1_other[:, 384:]], axis=1)
    b_attn = jnp.concatenate([biases[:, :384], other_biases[:, :384]], axis=0)[:, None, :]
    b_up = jnp.concatenate([biases[:, 384:], other_biases[:, 384:]], axis=1)

    qkv = dot(acts, w_attn)
    merged, q, k, v, lse = attn_fwd(rows_sc, qkv, b_attn, *tables)
    hidden = dot(acts, w_up) + b_up
    active_full, gelu_back = jax.vjp(gelu, hidden)
    active = active_full.astype(BF)

    w2_own = jnp.concatenate(second_blocks, axis=1)
    w2_other = core_swap(w2_own)
    w2 = jnp.concatenate([w2_own, w2_other], axis=0)
    mixed_own = jnp.concatenate([merged[:, :128], active[:, :512]], axis=1)
    mixed_other = jnp.concatenate([merged[:, 128:], active[:, 512:]], axis=1)
    mixed = jnp.concatenate([mixed_own, mixed_other], axis=1)
    partial = dot(mixed, w2).astype(BF)
    branch = reduce_blocks(
        [partial[128 * r : 128 * r + 128] for r in range(8)], x_up, x_down, z_swap
    )
    branch = branch.astype(BF)
    branch_pair = jnp.stack([branch[:64], core_swap(branch[64:])])
    layer_out = post_out(sc, tokens, branch_pair, (dense_bias + down_bias)[None, :])

    gout = jnp.concatenate(cot_blocks, axis=0)
    gmixed = dot_nt(gout, w2)
    gm = jnp.concatenate([gmixed[:, :128], gmixed[:, 640:768]], axis=1).astype(BF)
    gactive = jnp.concatenate([gmixed[:, 128:640], gmixed[:, 768:]], axis=1)
    ghidden = gelu_back(gactive)[0].astype(BF)
    up_sum = jnp.sum(ghidden.astype(F32), axis=0, keepdims=True)

    g2_other = dot_tn(mixed_other, gout).astype(BF)
    g2 = dot_tn(mixed_own, gout) + core_swap(g2_other).astype(F32)
    g2 = g2.astype(BF)
    second_grad = reduce_blocks(
        [g2[:, 256 * r : 256 * r + 256] for r in range(8)], y_up, y_down, zz_swap
    )

    gqkv, attn_sum = attn_bwd(rows_sc, q, k, v, lse, gm, *tables)
    gnormed_part = (dot_nt(gqkv, w_attn) + dot_nt(ghidden, w_up)).astype(BF)
    gnormed = reduce_blocks(
        [gnormed_part[128 * r : 128 * r + 128] for r in range(8)], x_up, x_down, z_swap
    )
    gnormed = gnormed.astype(BF)
    gnormed_pair = jnp.stack([gnormed[:64], core_swap(gnormed[64:])])

    g1_other = dot_tn(acts, jnp.concatenate([gqkv[:, 384:], ghidden[:, 512:]], axis=1)).astype(BF)
    g1 = dot_tn(acts, jnp.concatenate([gqkv[:, :384], ghidden[:, :512]], axis=1))
    g1 = (g1 + core_swap(g1_other).astype(F32)).astype(BF)
    first_grad = reduce_blocks(
        [g1[256 * r : 256 * r + 256] for r in range(8)], y_up, y_down, zz_swap
    )
    sums_own = jnp.concatenate([attn_sum[0], up_sum[:, :512]], axis=1)
    sums_other = jnp.concatenate([attn_sum[1], up_sum[:, 512:]], axis=1)
    bias_grads = lax.psum(sums_own + core_swap(sums_other), "dp")[0]

    grad_tokens, norm_sums = post_grad(sc, tokens, cotangent, gnormed_pair, gain_row)
    norm_sums = lax.psum(norm_sums, ("dp", "tensor"))
    return (
        layer_out,
        grad_tokens,
        by_head(first_grad[:, :384]),
        by_head(bias_grads[:384]),
        second_grad[:128],
        out_bias_grad,
        first_grad[:, 384:],
        bias_grads[384:],
        second_grad[128:],
        out_bias_grad,
        norm_sums[0],
        norm_sums[1],
    )


def solution(mesh):
    in_specs = (
        P("dp", "tensor", None),
        P("dp", "tensor"),
        P("tensor"),
        P("tensor", "dp"),
        P(),
        P("dp", "tensor"),
        P("tensor"),
        P("tensor", "dp"),
        P(),
        P(),
        P(),
        P("dp", "tensor", None),
    )
    out_specs = (
        P("dp", "tensor", None),
        P("dp", "tensor", None),
        P("dp", "tensor"),
        P("tensor"),
        P("tensor", "dp"),
        P(),
        P("dp", "tensor"),
        P("tensor"),
        P("tensor", "dp"),
        P(),
        P(),
        P(),
    )
    return jax.shard_map(shards, mesh=mesh, in_specs=in_specs, out_specs=out_specs, check_vma=False)
```

```python
import functools

import jax
import jax.numpy as jnp
import numpy as np
from jax import lax
from jax.experimental import pallas as pl
from jax.experimental.pallas import tpu as pltpu
from jax.sharding import PartitionSpec as P

HEAD_DIM = 64
ROT = 32
EPS = 1e-05
BF = jnp.bfloat16
LIMIT = 60
F32 = jnp.float32

OFFSETS = (0, -1, 1, 2)


def tensor_index(x, zlo, core):
    return (x % 4) * 4 + (zlo % 2) * 2 + core % 2


def dp_index(zhi, y):
    return (zhi % 2) * 4 + y % 4


def tensor_move(dx, dz, dc):
    return [
        (tensor_index(x, z, c), tensor_index(x + dx, z + dz, c + dc))
        for x in range(4)
        for z in range(2)
        for c in range(2)
    ]


def dp_move(dz, dy):
    return [(dp_index(z, y), dp_index(z + dz, y + dy)) for z in range(2) for y in range(4)]


def x_up(a):
    return lax.ppermute(a, "tensor", tensor_move(1, 0, 0))


def x_down(a):
    return lax.ppermute(a, "tensor", tensor_move(-1, 0, 0))


def z_swap(a):
    return lax.ppermute(a, "tensor", tensor_move(0, 1, 0))


def core_swap(a):
    return lax.ppermute(a, "tensor", tensor_move(0, 0, 1))


def y_up(a):
    return lax.ppermute(a, "dp", dp_move(0, 1))


def y_down(a):
    return lax.ppermute(a, "dp", dp_move(0, -1))


def zz_swap(a):
    return lax.ppermute(a, "dp", dp_move(1, 0))


def tie_body(*refs):
    pass


def tie(value, *others):
    anywhere = pl.BlockSpec(memory_space=pl.ANY)
    return pl.pallas_call(
        tie_body,
        in_specs=[anywhere] * (1 + len(others)),
        out_specs=anywhere,
        out_shape=jax.ShapeDtypeStruct(value.shape, value.dtype),
        input_output_aliases={0: 0},
        compiler_params=pltpu.CompilerParams(),
        cost_estimate=pl.CostEstimate(flops=0, bytes_accessed=0, transcendentals=0),
        name="tie",
    )(value, *others)


def join_body(a_own, c_own, swapped, a0, a1, c0, c1):
    rows = a_own.shape[0]
    for outs, own, k in (((a0, a1), a_own, 0), ((c0, c1), c_own, 1)):
        for out in outs:
            out[:rows, :], out[rows:, :] = own[...], swapped[k]


def join(acts_own, cot_own, swapped):
    rows, width = acts_own.shape
    return call(
        join_body,
        vmem(3),
        vmem(4),
        [shape((2 * rows, width))] * 4,
        (acts_own, cot_own, swapped),
        "join",
    )


def sum_over(vector, step):
    return vector + step(vector)


def x_pair(a):
    return lax.ppermute(a, "tensor", [(i, tensor_index(i // 4 ^ 1, i // 2 % 2, i % 2)) for i in range(16)])


def x_cross(a):
    return lax.ppermute(a, "tensor", [(i, tensor_index(3 - i // 4, i // 2 % 2, i % 2)) for i in range(16)])


def y_pair(a):
    return lax.ppermute(a, "dp", [(i, dp_index(i // 4, i % 4 ^ 1)) for i in range(8)])


def y_cross(a):
    return lax.ppermute(a, "dp", [(i, dp_index(i // 4, 3 - i % 4)) for i in range(8)])


def vmem(count):
    return [pl.BlockSpec(memory_space=pltpu.VMEM)] * count


def smem():
    return pl.BlockSpec(memory_space=pltpu.SMEM)


def anywhere(count=1):
    return [pl.BlockSpec(memory_space=pl.ANY)] * count


def params(limit=LIMIT):
    return pltpu.CompilerParams(vmem_limit_bytes=limit * 1024 * 1024)


LONG = 40_000_000_000


def call(body, in_specs, out_specs, out_shape, args, name, scratch=(), flops=1, **kwargs):
    return pl.pallas_call(
        body,
        in_specs=in_specs,
        out_specs=out_specs,
        out_shape=out_shape,
        scratch_shapes=list(scratch),
        compiler_params=params(),
        cost_estimate=pl.CostEstimate(flops=flops, bytes_accessed=1, transcendentals=0),
        name=name,
        **kwargs,
    )(*args)


def shape(dims, dtype=BF):
    return jax.ShapeDtypeStruct(dims, dtype)


class Copy:
    def __init__(self, src, dst, sem):
        self.copy, self.waited = pltpu.make_async_copy(src, dst, sem), False
        self.copy.start()

    def wait(self):
        if not self.waited:
            self.copy.wait()
        self.waited = True


def copier(sems):
    used = iter(range(sems.shape[0]))
    return lambda src, dst: Copy(src, dst, sems.at[next(used)])


def wait(copies):
    for copy in copies:
        copy.wait()


def adds_body(groups, count, rows, *refs):
    ins, outs, (sems,) = refs[: sum(groups)], refs[count : count + len(groups)], refs[-1:]
    holds = refs[count + len(groups) : -1]
    start = copier(sems)
    copies = [start(a.at[rows, :], b) for a, b in zip(ins, holds)]
    at = 0
    for size, out in zip(groups, outs):
        wait(copies[at : at + size])
        total = holds[at][...].astype(F32)
        for hold in holds[at + 1 : at + size]:
            total = total + hold[...].astype(F32)
        out[...] = total.astype(out.dtype)
        at += size


def adds(*groups, deps=(), rows=None):
    flat = [a for group in groups for a in group]
    sizes = tuple(len(group) for group in groups)
    rows = rows or slice(0, flat[0].shape[0])
    dims = [(rows.stop - rows.start, group[0].shape[1]) for group in groups]
    return call(
        functools.partial(adds_body, sizes, len(flat) + len(deps), rows),
        anywhere(len(flat) + len(deps)),
        vmem(len(groups)),
        [shape(dim) for dim in dims],
        (*flat, *deps),
        "adds",
        [pltpu.VMEM(dim, BF) for dim, size in zip(dims, sizes) for _ in range(size)] + [pltpu.SemaphoreType.DMA((len(flat),))],
    )


def pre_body(
    sc, tok_in, cot_in, gain, bias, attn_in, up, dense, down, attn_bias, up_bias,
    acts_out, cot_out, pair, cotsum, first, second, biases, tok, cot, attn, hold, sems,
):
    start = copier(sems)
    in_attn = start(attn_in, attn)
    in_tok = start(tok_in, tok)
    in_cot = start(cot_in, cot)
    rest = [start(up, first.at[:, 384:]), start(dense, second.at[:128, :]), start(down, second.at[128:, :])]
    by_kind = lambda a: jnp.concatenate(
        [a[:, (3 * h + k) * 64 : (3 * h + k) * 64 + 64] for k in range(3) for h in range(2)], axis=1
    )
    biases[:, :384] = by_kind(attn_bias[...])
    biases[:, 384:] = up_bias[...]
    in_attn.wait()
    first[:, :384] = by_kind(attn[...])
    in_tok.wait()
    in_cot.wait()
    total = jnp.zeros(cotsum.shape, F32)
    for s in range(2):
        seq = sc[8] if s == 0 else 1 - sc[8]
        xin = tok[seq].astype(F32)
        centred = xin - jnp.mean(xin, axis=-1, keepdims=True)
        spread = jnp.mean(centred * centred, axis=-1, keepdims=True)
        hold[...] = (centred * lax.rsqrt(spread + EPS) * gain[...] + bias[...]).astype(BF)
        total = total + jnp.sum(cot[seq].astype(F32), axis=0, keepdims=True)
        for r in range(8):
            cols = pl.ds(pl.multiple_of(sc[r] * 256, 256), 256)
            to = slice(r * 256, (r + 1) * 256)
            if s == 0:
                acts_out[:, to] = hold[:, cols]
                cot_out[:, to] = cot[seq, :, cols]
            else:
                pair[0, :, to] = hold[:, cols]
                pair[1, :, to] = cot[seq, :, cols]
    cotsum[...] = total
    wait(rest)


def pre(sc, tok, cot, gain, bias, attn, *rest):
    rows, width = tok.shape[1:]
    return call(
        pre_body,
        [smem()] + anywhere(2) + vmem(2) + anywhere(4) + vmem(2),
        vmem(7),
        [
            shape((rows, width)),
            shape((rows, width)),
            shape((2, rows, width)),
            shape((1, width), F32),
            shape((256, 896)),
            shape((640, 256)),
            shape((1, 896), F32),
        ],
        (sc, tok, cot, gain, bias, attn, *rest),
        "pre",
        [pltpu.VMEM(tok.shape, BF), pltpu.VMEM(tok.shape, BF), pltpu.VMEM(attn.shape, BF)]
        + [pltpu.VMEM((rows, width), BF), pltpu.SemaphoreType.DMA((6,))],
    )


def own_rows(sc, parts, received, hold):
    for s in range(2):
        rows = sum(ref[...].astype(F32) for ref in parts) if s == 0 else received[...].astype(F32)
        for r in range(8):
            cols = pl.ds(pl.multiple_of(sc[r] * 256, 256), 256)
            hold[s, :, cols] = rows[:, r * 256 : (r + 1) * 256]


def post_out_body(sc, tok_in, a, b, c, d, received, extra, out, tok, hold, p0, p1, p2, p3, p4, sems):
    start = copier(sems)
    ins = [start(ref.at[:64, :], p) for ref, p in zip((a, b, c, d, received), (p0, p1, p2, p3, p4))]
    wait(ins + [start(tok_in, tok)])
    own_rows(sc, (p0, p1, p2, p3), p4, hold)
    for s in range(2):
        seq = sc[8] if s == 0 else 1 - sc[8]
        out[seq] = (tok[seq].astype(F32) + hold[s] + extra[...]).astype(BF)


def post_out(sc, tok, parts, received, extra):
    rows = tok.shape[1:]
    return call(
        post_out_body,
        [smem()] + anywhere(6) + vmem(1),
        pl.BlockSpec(memory_space=pltpu.VMEM),
        shape(tok.shape),
        (sc, tok, *parts, received, extra),
        "post_out",
        [pltpu.VMEM(tok.shape, BF), pltpu.VMEM(tok.shape, F32)]
        + [pltpu.VMEM(rows, BF)] * 5
        + [pltpu.SemaphoreType.DMA((6,))],
    )


def post_grad_body(sc, tok_in, cot_in, a, b, c, d, received, gain, out, tok, cot, hold, p0, p1, p2, p3, p4, sems):
    start = copier(sems)
    ins = [start(ref.at[:64, :], p) for ref, p in zip((a, b, c, d, received), (p0, p1, p2, p3, p4))]
    wait(ins + [start(tok_in, tok), start(cot_in, cot)])
    own_rows(sc, (p0, p1, p2, p3), p4, hold)
    for s in range(2):
        seq = sc[8] if s == 0 else 1 - sc[8]
        xin = tok[seq].astype(F32)
        centred = xin - jnp.mean(xin, axis=-1, keepdims=True)
        scale = lax.rsqrt(jnp.mean(centred * centred, axis=-1, keepdims=True) + EPS)
        xhat = centred * scale
        e = hold[s] * gain[...]
        mean_e = jnp.mean(e, axis=-1, keepdims=True)
        mean_x = jnp.mean(e * xhat, axis=-1, keepdims=True)
        out[seq] = cot[seq].astype(F32) + (e - mean_e - xhat * mean_x) * scale


def post_grad(sc, tok, cot, parts, received, gain):
    rows = tok.shape[1:]
    return call(
        post_grad_body,
        [smem()] + anywhere(7) + vmem(1),
        pl.BlockSpec(memory_space=pltpu.VMEM),
        shape(tok.shape, F32),
        (sc, tok, cot, *parts, received, gain),
        "post_grad",
        [pltpu.VMEM(tok.shape, BF)] * 2
        + [pltpu.VMEM(tok.shape, F32)]
        + [pltpu.VMEM(rows, BF)] * 5
        + [pltpu.SemaphoreType.DMA((7,))],
    )


def turn(u, cosine, sine_low, sine_high):
    return (
        u * cosine
        + pltpu.roll(u, u.shape[-1] - ROT // 2, 1) * sine_low
        + pltpu.roll(u, ROT // 2, 1) * sine_high
    )


def turn_back(u, cosine, sine_low, sine_high):
    return (
        u * cosine
        - pltpu.roll(u, u.shape[-1] - ROT // 2, 1) * sine_low
        - pltpu.roll(u, ROT // 2, 1) * sine_high
    )


def dot(a, b):
    return lax.dot_general(a, b, (((1,), (0,)), ((), ())), preferred_element_type=F32)


def dot_nt(a, b):
    return lax.dot_general(a, b, (((1,), (1,)), ((), ())), preferred_element_type=F32)


def dot_tn(a, b):
    return lax.dot_general(a, b, (((0,), (0,)), ((), ())), preferred_element_type=F32)


QB = 256


def diagonal(size):
    keys = lax.broadcasted_iota(jnp.int32, (size, size), 0)
    queries = lax.broadcasted_iota(jnp.int32, (size, size), 1)
    return keys <= queries


def attn_fwd_body(sc, *refs):
    dep, merged, lse, out_t, out_abs, q_in, k_in, v_in, sems = refs[6:]
    start = copier(sems)
    wait([start(refs[3 * h + k], held.at[h]) for h in range(2) for k, held in enumerate((q_in, k_in, v_in))])
    for h in range(2):
        attn_fwd_half(h, sc, merged, lse, out_t, out_abs, q_in, k_in, v_in)


def attn_fwd_half(h, sc, merged, lse, out_t, out_abs, q_in, k_in, v_in):
    keys = k_in[h]
    values_t = v_in[h].T
    lane = lax.broadcasted_iota(jnp.int32, (QB, 128), 1)
    allowed = diagonal(QB)
    for b in range(1024 // QB):
        begin, end = b * QB, (b + 1) * QB
        query = q_in[h, begin:end, :]
        for a in range(2):
            heads = slice(a * HEAD_DIM, (a + 1) * HEAD_DIM)
            only = jnp.where(lane // HEAD_DIM == a, query, jnp.zeros_like(query))
            scores = dot_nt(keys[:end], only)
            low = jnp.where(allowed, scores[begin:], -jnp.inf)
            top = jnp.max(low, axis=0, keepdims=True)
            if b > 0:
                top = jnp.maximum(top, jnp.max(scores[:begin], axis=0, keepdims=True))
            weights = jnp.exp(low - top)
            total = jnp.sum(weights, axis=0, keepdims=True)
            out = dot(values_t[:, begin:end], weights.astype(BF))
            if b > 0:
                weights = jnp.exp(scores[:begin] - top)
                total = total + jnp.sum(weights, axis=0, keepdims=True)
                out = out + dot(values_t[:, :begin], weights.astype(BF))
            out_t[heads, begin:end] = (out * (1.0 / total))[heads, :]
            lse[2 * h + a : 2 * h + a + 1, begin:end] = top + jnp.log(total)
    for r in range(1024 // 128):
        here = slice(128 * r, 128 * r + 128)
        out_abs[here, :] = out_t[:, here].T.astype(BF)
    for r in range(1024 // 64):
        there = pl.ds(pl.multiple_of(sc[r] * 64, 64), 64)
        merged[64 * r : 64 * r + 64, 128 * h : 128 * h + 128] = out_abs[there, :]


def attn_fwd(sc, own, other, dep):
    length = own[0].shape[0]
    return call(
        attn_fwd_body,
        [smem()] + anywhere(7),
        vmem(2),
        [shape((length, 256)), shape((4, length), F32)],
        (sc, *own, *other, dep),
        "attn_fwd",
        flops=LONG,
        scratch=[pltpu.VMEM((128, length), F32), pltpu.VMEM((length, 128), BF)]
        + [pltpu.VMEM((2, length, 128), BF)] * 3
        + [pltpu.SemaphoreType.DMA((6,))],
    )


def attn_bwd_body(sc, *refs):
    lse, tables_in, (acts_in, gh_in, dep) = refs[8], refs[9:12], refs[12:15]
    outs, g1_out, colsum = refs[15:17], refs[17], refs[18]
    gqkv, gm_hold, dq_t, dq, dk, dv, q_in, k_in, v_in, gm_in = refs[19:29]
    tables, (acts, rhs, g1, sems) = refs[29:32], refs[32:]
    start = copier(sems)
    held = (gm_in, k_in, q_in, v_in)
    ins = [start(refs[4 * h + k], a.at[h]) for h in (1, 0) for k, a in enumerate(held)]
    ins += [start(a, b) for a, b in zip(tables_in, tables)]
    rest = [start(gh_in, rhs.at[:, 384:]), start(acts_in, acts)]
    wait(ins)
    copies = []
    for h in (1, 0):
        attn_bwd_half(h, sc, lse, *tables, gqkv, colsum, gm_hold, dq_t, dq, dk, dv, q_in, k_in, v_in, gm_in)
        copies.append(start(gqkv.at[h], outs[h]))
    wait(rest)
    rhs[:, :384] = gqkv[1]
    for rows in blocks_of(512, 4):
        g1[rows, :] = dot_tn(acts[:, rows], rhs[...]).astype(BF)
        copies.append(start(g1.at[rows, :], g1_out.at[rows, :]))
    wait(copies)


def attn_bwd_half(
    h, sc, lse, cos_t, low_t, high_t, gqkv, colsum, gm_hold, dq_t, dq, dk, dv, q_in, k_in, v_in, gm_in
):
    for r in range(1024 // 64):
        there = pl.ds(pl.multiple_of(sc[r] * 64, 64), 64)
        gm_hold[there, :] = gm_in[h, 64 * r : 64 * r + 64, :]
    keys = k_in[h]
    values = v_in[h]
    keys_t = keys.T
    lane = lax.broadcasted_iota(jnp.int32, (QB, 128), 1)
    allowed = diagonal(QB)
    for b in reversed(range(1024 // QB)):
        begin, end = b * QB, (b + 1) * QB
        query = q_in[h, begin:end, :]
        grad = gm_hold[begin:end, :]
        add_v, add_k = 0.0, 0.0
        for a in range(2):
            heads = slice(a * HEAD_DIM, (a + 1) * HEAD_DIM)
            mine = lane // HEAD_DIM == a
            only = jnp.where(mine, query, jnp.zeros_like(query))
            grad_only = jnp.where(mine, grad, jnp.zeros_like(grad))
            shift = lse[2 * h + a : 2 * h + a + 1, begin:end]
            scores = dot_nt(keys[:end], only)
            dprobs = dot_nt(values[:end], grad_only)
            low_p = jnp.where(allowed, jnp.exp(scores[begin:] - shift), 0.0)
            probs = low_p if b == 0 else jnp.concatenate([jnp.exp(scores[:begin] - shift), low_p], axis=0)
            delta = jnp.sum(probs * dprobs, axis=0, keepdims=True)
            gscores = (probs * (dprobs - delta)).astype(BF)
            add_v = add_v + dot(probs.astype(BF), grad_only)
            add_k = add_k + dot(gscores, only)
            dq_t[heads, begin:end] = dot(keys_t[:, :end], gscores)[heads, :]
        if end == 1024:
            dv[...], dk[...] = add_v, add_k
        else:
            dv[:end, :] += add_v
            dk[:end, :] += add_k
    for r in range(1024 // 128):
        here = slice(128 * r, 128 * r + 128)
        dq[here, :] = dq_t[:, here].T
    total = jnp.zeros((1, 384), F32)
    for r in range(1024 // 64):
        here = slice(64 * r, 64 * r + 64)
        there = pl.ds(pl.multiple_of(sc[r] * 64, 64), 64)
        tables = (cos_t[there, :], low_t[there, :], high_t[there, :])
        gq = turn_back(dq[there, :] * (HEAD_DIM**-0.5), *tables)
        gk = turn_back(dk[there, :], *tables)
        rows = jnp.concatenate([gq, gk, dv[there, :]], axis=1).astype(BF)
        gqkv[h, here, :] = rows
        total = total + jnp.sum(rows.astype(F32), axis=0, keepdims=True)
    colsum[h] = total


def attn_bwd(sc, own, other, lse, gm_own, gm_other, tables, acts, gh_other, dep):
    length = gm_own.shape[0]
    ins = []
    for (q, k, v), gm in ((own, gm_own), (other, gm_other)):
        ins += [gm, k, q, v]
    return call(
        attn_bwd_body,
        [smem()] + anywhere(8) + vmem(1) + anywhere(6),
        anywhere(3) + vmem(1),
        [shape((length, 384))] * 2 + [shape((2048, 896)), shape((2, 1, 384), F32)],
        (sc, *ins, lse, *tables, acts, gh_other, dep),
        "attn_bwd",
        flops=LONG,
        scratch=[pltpu.VMEM((2, length, 384), BF), pltpu.VMEM((length, 128), BF), pltpu.VMEM((128, length), F32)]
        + [pltpu.VMEM((length, 128), F32)] * 3
        + [pltpu.VMEM((2, length, 128), BF)] * 4
        + [pltpu.VMEM((length, 128), F32)] * 3
        + [pltpu.VMEM((1024, 2048), BF), pltpu.VMEM((1024, 896), BF), pltpu.VMEM((2048, 896), BF)]
        + [pltpu.SemaphoreType.DMA((32,))],
    )


ROWS = 256
HUGE = (pltpu.SemaphoreType.DMA((176,)),)


def blocks_of(size=256, count=8):
    return [slice(size * r, size * r + size) for r in range(count)]


def flat(groups):
    return [copy for group in groups for copy in group]


def project_body(sc, *refs):
    pieces, w_own, w_other = refs[:8], refs[8:16], refs[16:24]
    b_own, b_other, tables_in = refs[24], refs[25], refs[26:29]
    acts_out, qkv_out = refs[29], refs[30:36]
    act_out, slope_out = refs[36:38], refs[38:40]
    acts, w, cos_t, low_t, high_t = refs[40:45]
    qkv, act, slope, sems = refs[45:51], refs[51:53], refs[53:55], refs[55]
    start = copier(sems)

    def tile(j):
        group = []
        for r, rows in enumerate(blocks_of()):
            if j < 6:
                cols = slice(256 * (j % 3), 256 * (j % 3) + 256)
                group.append(((w_own, w_other)[j // 3][r].at[:, cols], w.at[j, rows, :]))
            else:
                group.append((w_own[r].at[:, 768:], w.at[j, rows, :128]))
                group.append((w_other[r].at[:, 768:], w.at[j, rows, 128:]))
        return group

    def rows_in(m):
        return [(pieces[r], acts.at[128 * r : 128 * r + 128, :]) for r in (2 * m, 2 * m + 1)]

    def begin(group):
        return [start(a, b) for a, b in group]

    acts_in = [begin(rows_in(0))]
    w_in = [begin(tile(j)) for j in range(3)]
    rest = begin(zip(tables_in, (cos_t, low_t, high_t)))
    acts_in += [begin(rows_in(m)) for m in range(1, 4)]
    w_in += [begin(tile(j)) for j in range(3, 7)]
    root = (2.0 / np.pi) ** 0.5
    outs = []
    strips = [[(j // 3, 2 * (j % 3) + k) for k in range(2)] for j in range(6)] + [[(0, 6), (1, 6)]]
    steps = [(m, j) for m in range(4) for j in range(3)] + [(m, j) for m in range(4) for j in range(3, 7)]
    for m, j in steps:
        rows = slice(ROWS * m, ROWS * m + ROWS)
        if j == 0 and m == 0:
            wait(acts_in[0] + flat(w_in[:3]) + rest)
        if j == 0 and m == 1:
            wait(flat(acts_in[1:]))
            outs.append(start(acts, acts_out))
        if j == 3 and m == 0:
            wait(flat(w_in[3:]))
        result = dot(acts[rows, :], w[j])
        for k, (core, strip) in enumerate(strips[j]):
            cols = slice(128 * strip, 128 * strip + 128)
            h = result[:, 128 * k : 128 * k + 128] + (b_own, b_other)[core][:, cols]
            if strip < 3:
                for b in range(ROWS // 64):
                    there = pl.ds(pl.multiple_of(sc[4 * m + b] * 64, 64), 64)
                    u = h[64 * b : 64 * b + 64, :]
                    if strip < 2:
                        u = turn(u, cos_t[there, :], low_t[there, :], high_t[there, :])
                    if strip == 0:
                        u = u * (HEAD_DIM**-0.5)
                    qkv[3 * core + strip][there, :] = u.astype(BF)
                continue
            cols = slice(128 * (strip - 3), 128 * (strip - 3) + 128)
            square = h * h
            th = jnp.tanh(root * (h + 0.044715 * (square * h)))
            half = 0.5 + 0.5 * th
            act[core][rows, cols] = (h * half).astype(BF)
            slope[core][rows, cols] = (
                half + (0.5 * h) * (1.0 - th * th) * (root + (3 * 0.044715 * root) * square)
            ).astype(BF)
        if j == 6:
            for a, b in zip((*act, *slope), (*act_out, *slope_out)):
                outs.append(start(a.at[rows, :], b.at[rows, :]))
    for a, b in zip(qkv, qkv_out):
        outs.append(start(a, b))
    wait(outs)


def project(sc, pieces, w_own, w_other, b_own, b_other, tables):
    small, wide, whole = (1024, 128), (1024, 512), (1024, 2048)
    return call(
        project_body,
        [smem()] + anywhere(24) + vmem(2) + anywhere(3),
        anywhere(11),
        [shape(whole)] + [shape(small)] * 6 + [shape(wide)] * 4,
        (sc, *pieces, *w_own, *w_other, b_own, b_other, *tables),
        "project",
        flops=LONG,
        scratch=[pltpu.VMEM(whole, BF), pltpu.VMEM((7, 2048, 256), BF)]
        + [pltpu.VMEM(small, F32)] * 3
        + [pltpu.VMEM(small, BF)] * 6
        + [pltpu.VMEM(wide, BF)] * 4
        + [*HUGE],
    )


def branch_body(merged, act_own, act_other, *refs):
    w_own, w_other, dep, outs = refs[:8], refs[8:16], refs[16], refs[17:25]
    lhs, w, stage, sems = refs[25:]
    start = copier(sems)
    parts = ((merged.at[:, :128], 0, 128), (act_own, 128, 512), (merged.at[:, 128:], 640, 128), (act_other, 768, 512))
    lhs_in = [start(a, lhs.at[:, c : c + n]) for a, c, n in parts]
    w_in = [[start(w_own[r], w.at[r, :640, :]), start(w_other[r], w.at[r, 640:, :])] for r in range(8)]
    copies = []
    for half in (range(3), range(3, 8)):
        wait(lhs_in + flat(w_in[r] for r in half))
        lhs_in = []
        for m in range(4):
            rows = slice(ROWS * m, ROWS * m + ROWS)
            for r in half:
                stage[rows, 256 * r : 256 * r + 256] = dot(lhs[rows, :], w[r]).astype(BF)
            if 7 in half:
                for p in (2 * m, 2 * m + 1):
                    copies.append(start(stage.at[128 * p : 128 * p + 128, :], outs[p]))
    wait(copies)


def branch_part(merged, act_own, act_other, w_own, w_other, dep):
    return call(
        branch_body,
        anywhere(20),
        anywhere(8),
        [shape((128, 2048))] * 8,
        (merged, act_own, act_other, *w_own, *w_other, dep),
        "branch_part",
        flops=LONG,
        scratch=[pltpu.VMEM((1024, 1280), BF), pltpu.VMEM((8, 1280, 256), BF), pltpu.VMEM((1024, 2048), BF), *HUGE],
    )


def grad_in_body(*refs):
    pieces, w_own, w_other = refs[:8], refs[8:16], refs[16:24]
    slope_in, (merged, act, dep) = refs[24:26], refs[26:29]
    gout_out, gm_out, gh_out, g2_out, colsum = refs[29], refs[30:32], refs[32:34], refs[34], refs[35:37]
    gout, w, slope, gm, gh, lhs, stage, sems = refs[37], refs[38], refs[39:41], refs[41:43], refs[43:45], *refs[45:]
    start = copier(sems)

    def tile(j):
        copies = []
        for r, cols in enumerate(blocks_of()):
            for first, source, at in ((0, w_own, 256 * j), (640, w_other, 256 * j - 640)):
                lo, hi = max(at, 0), min(at + 256, 640)
                if lo < hi:
                    copies.append(start(source[r].at[lo:hi, :], w.at[lo + first : hi + first, cols]))
        return copies

    gout_in = [start(pieces[r], gout.at[128 * r : 128 * r + 128, :]) for r in range(8)]
    w_in = [tile(0)]
    slope_copies = [start(a, b) for a, b in zip(slope_in, slope)]
    w_in += [tile(j) for j in range(1, 5)]
    lhs_in = [start(merged.at[:, 128:], lhs.at[:, :128]), start(act, lhs.at[:, 128:])]
    totals = [[jnp.zeros((1, 128), F32)] * 4 for _ in range(2)]
    copies = []
    for j in range(5):
        if j == 0:
            wait(gout_in + w_in[0] + slope_copies)
            copies.append(start(gout, gout_out))
        if j == 1:
            wait(flat(w_in) + lhs_in)
        for m in range(4):
            rows = slice(ROWS * m, ROWS * m + ROWS)
            result = dot_nt(gout[rows, :], w[256 * j : 256 * j + 256, :])
            for k in range(2):
                core, strip = (2 * j + k) // 5, (2 * j + k) % 5
                part = result[:, 128 * k : 128 * k + 128]
                if strip == 0:
                    gm[core][rows, :] = part.astype(BF)
                    continue
                cols = slice(128 * (strip - 1), 128 * strip)
                part = (part * slope[core][rows, cols].astype(F32)).astype(BF)
                gh[core][rows, cols] = part
                totals[core][strip - 1] += jnp.sum(part.astype(F32), axis=0, keepdims=True)
    for core in range(2):
        for strip in range(4):
            colsum[core][:, 128 * strip : 128 * strip + 128] = totals[core][strip]
    for a, b in zip((*gm, *gh), (*gm_out, *gh_out)):
        copies.append(start(a, b))
    for cols in blocks_of(512, 4):
        stage[:, cols] = dot_tn(lhs[...], gout[:, cols]).astype(BF)
        copies.append(start(stage.at[:, cols], g2_out.at[:, cols]))
    wait(copies)


def grad_in(pieces, w_own, w_other, slope_own, slope_other, merged, act_other, dep):
    small, wide, whole = (1024, 128), (1024, 512), (1024, 2048)
    return call(
        grad_in_body,
        anywhere(29),
        anywhere(6) + vmem(2),
        [shape(whole)] + [shape(small)] * 2 + [shape(wide)] * 2 + [shape((640, 2048))] + [shape((1, 512), F32)] * 2,
        (*pieces, *w_own, *w_other, slope_own, slope_other, merged, act_other, dep),
        "grad_in",
        flops=LONG,
        scratch=[pltpu.VMEM(whole, BF), pltpu.VMEM((1280, 2048), BF)]
        + [pltpu.VMEM(wide, BF)] * 2
        + [pltpu.VMEM(small, BF)] * 2
        + [pltpu.VMEM(wide, BF)] * 2
        + [pltpu.VMEM((1024, 640), BF), pltpu.VMEM((640, 2048), BF), *HUGE],
    )


def gnormed_body(sc, q_own, gh_own, q_other, gh_other, acts_in, *refs):
    w_own, w_other, dep, outs, sums = refs[:8], refs[8:16], refs[16], refs[17:25], refs[25]
    lhs, w, acts, stage, sems = refs[26:]
    start = copier(sems)
    parts = ((q_own, 0), (gh_own, 384), (q_other, 896), (gh_other, 1280))

    def rows_in(m):
        rows = slice(ROWS * m, ROWS * m + ROWS)
        copies = [start(a.at[rows, :], lhs.at[rows, c : c + a.shape[1]]) for a, c in parts]
        return copies + [start(acts_in.at[rows, :], acts.at[rows, :])]

    def tile(r):
        rows = slice(256 * r, 256 * r + 256)
        return [start(w_own[r], w.at[rows, :896]), start(w_other[r], w.at[rows, 896:])]

    lhs_in = {3: rows_in(3)}
    w_in = [tile(r) for r in range(8)]
    lhs_in.update({m: rows_in(m) for m in range(3)})
    totals = [[jnp.zeros((1, 256), F32)] * 8 for _ in range(2)]
    copies = []
    for m, first, last in ((3, 0, 3), (3, 3, 8), (0, 0, 8), (1, 0, 8), (2, 0, 8)):
        rows = slice(ROWS * m, ROWS * m + ROWS)
        if m == 3:
            wait(lhs_in[3] + flat(w_in[first:last]))
        if m == 0:
            wait(lhs_in[0] + lhs_in[1] + lhs_in[2])
        for r in range(first, last):
            cols = slice(256 * r, 256 * r + 256)
            result = dot_nt(lhs[rows, :], w[cols, :])
            totals[0][r] += jnp.sum(result, axis=0, keepdims=True)
            totals[1][r] += jnp.sum(result * acts[rows, cols].astype(F32), axis=0, keepdims=True)
            stage[rows, cols] = result.astype(BF)
        if last == 8:
            for p in (2 * m, 2 * m + 1):
                copies.append(start(stage.at[128 * p : 128 * p + 128, :], outs[p]))
    for k in range(2):
        for r in range(8):
            sums[k : k + 1, pl.ds(pl.multiple_of(sc[r] * 256, 256), 256)] = totals[k][r]
    wait(copies)


def gnormed_part(sc, q_own, gh_own, q_other, gh_other, acts, w_own, w_other, dep):
    whole = (1024, 2048)
    return call(
        gnormed_body,
        [smem()] + anywhere(22),
        anywhere(8) + vmem(1),
        [shape((128, 2048))] * 8 + [shape((2, 2048), F32)],
        (sc, q_own, gh_own, q_other, gh_other, acts, *w_own, *w_other, dep),
        "gnormed_part",
        flops=LONG,
        scratch=[pltpu.VMEM((1024, 1792), BF), pltpu.VMEM((2048, 1792), BF), pltpu.VMEM(whole, BF), pltpu.VMEM(whole, BF), *HUGE],
    )


def second_body(merged, act, gout, received, dep, *refs):
    outs, (lhs, rhs, held, stage, sems) = refs[:8], refs[8:]
    start = copier(sems)
    lhs_in = [start(merged.at[:, :128], lhs.at[:, :128]), start(act, lhs.at[:, 128:])]
    ins = []
    for cols in blocks_of(512, 4):
        ins.append([start(gout.at[:, cols], rhs.at[:, cols]), start(received.at[:, cols], held.at[:, cols])])
    copies = []
    for r, cols in enumerate(blocks_of()):
        if r == 0:
            wait(lhs_in + ins[0])
        if r == 2:
            wait(flat(ins))
        result = dot_tn(lhs[...], rhs[:, cols])
        stage[r] = (result + held[:, cols].astype(F32)).astype(BF)
        copies.append(start(stage.at[r], outs[r]))
    wait(copies)


def second_grad(merged, act, gout, received, dep):
    return call(
        second_body,
        anywhere(5),
        anywhere(8),
        [shape((640, 256))] * 8,
        (merged, act, gout, received, dep),
        "second_grad",
        flops=LONG,
        scratch=[pltpu.VMEM((1024, 640), BF), pltpu.VMEM((1024, 2048), BF)]
        + [pltpu.VMEM((640, 2048), BF), pltpu.VMEM((8, 640, 256), BF), *HUGE],
    )


def first_body(gqkv, gh, acts, received, dep, *refs):
    outs, (lhs, rhs, held, stage, sems) = refs[:8], refs[8:]
    start = copier(sems)
    rhs_in = [start(gqkv, rhs.at[:, :384]), start(gh, rhs.at[:, 384:])]
    ins = []
    for rows in blocks_of(512, 4):
        ins.append([start(acts.at[:, rows], lhs.at[:, rows]), start(received.at[rows, :], held.at[rows, :])])
    copies = []
    for r, rows in enumerate(blocks_of()):
        if r == 0:
            wait(rhs_in + ins[0])
        if r == 2:
            wait(flat(ins))
        result = dot_tn(lhs[:, rows], rhs[...])
        stage[r] = (result + held[rows, :].astype(F32)).astype(BF)
        copies.append(start(stage.at[r], outs[r]))
    wait(copies)


def first_grad(gqkv, gh, acts, received, dep):
    return call(
        first_body,
        anywhere(5),
        anywhere(8),
        [shape((256, 896))] * 8,
        (gqkv, gh, acts, received, dep),
        "first_grad",
        flops=LONG,
        scratch=[pltpu.VMEM((1024, 2048), BF), pltpu.VMEM((1024, 896), BF)]
        + [pltpu.VMEM((2048, 896), BF), pltpu.VMEM((8, 256, 896), BF), *HUGE],
    )


def rotary_tables(length):
    frequency = np.float32(10000.0) ** (-(np.arange(ROT // 2, dtype=np.float32) * 2.0 / ROT))
    angles = np.arange(length, dtype=np.float32)[:, None] * frequency.astype(np.float32)[None, :]
    cosine, sine = np.cos(angles), np.sin(angles)
    one = np.ones((length, HEAD_DIM - ROT), np.float32)
    zero_half, zero = np.zeros_like(sine), np.zeros_like(one)
    cos_t = np.concatenate([cosine, cosine, one] * 2, axis=1)
    low_t = np.concatenate([-sine, zero_half, zero] * 2, axis=1)
    high_t = np.concatenate([zero_half, sine, zero] * 2, axis=1)
    return tuple(jnp.asarray(a, F32) for a in (cos_t, low_t, high_t))


def by_head(a):
    lead = a.shape[:-1]
    return jnp.swapaxes(a.reshape(lead + (3, 2, HEAD_DIM)), -3, -2).reshape(lead + (384,))


def shards(
    tokens,
    attn_weight,
    attn_bias,
    dense_weight,
    dense_bias,
    up_weight,
    up_bias,
    down_weight,
    down_bias,
    norm_gain,
    norm_bias,
    cotangent,
):
    t, d = lax.axis_index("tensor"), lax.axis_index("dp")
    x, zlo, core = t // 4, (t // 2) % 2, t % 2
    zhi, y = d // 4, d % 4
    features = [((zhi + j) % 2) * 4 + (y + o) % 4 for o in OFFSETS for j in range(2)]
    sc = jnp.stack(features + [core]).astype(jnp.int32)
    row_blocks = [
        4 * ((x + o) % 4) + 2 * ((zlo + j) % 2) + (core + k) % 2
        for o in OFFSETS
        for j in range(2)
        for k in range(2)
    ]
    rows_sc = jnp.stack(row_blocks).astype(jnp.int32)
    tables = rotary_tables(16 * tokens.shape[1])
    gain_row, bias_row = norm_gain[None, :], norm_bias[None, :]

    acts_own, cot_own, pair, cot_sum, f0, s0, biases = pre(
        sc, tokens, cotangent, gain_row, bias_row, attn_weight, up_weight, dense_weight, down_weight,
        attn_bias[None, :], up_bias[None, :],
    )
    swapped = core_swap(pair)
    f1, f2, f4, f0x = zz_swap(f0), y_up(f0), y_down(f0), core_swap(f0)
    other_biases = core_swap(biases)
    a0, a0z, c0, c0x = join(acts_own, cot_own, swapped)
    a2, a4 = x_up(a0), x_down(a0)
    a1 = z_swap(tie(a0z, f1))
    f1 = tie(f1, f2, f4, a0)
    f3, f5, f1x = y_up(f1), y_down(f1), core_swap(f1)
    f2 = tie(f2, f1)
    f6, f2x, f4x = y_up(f2), core_swap(f2), core_swap(f4)
    a2 = tie(a2, a4, f2)
    a6 = x_up(a2)
    f5 = tie(f5, a2)
    f7, f5x = y_down(f5), core_swap(f5)
    c0 = tie(c0, a1)
    c1 = z_swap(c0)
    a1 = tie(a1, a6, f5)
    a3, a5 = x_up(a1), x_down(a1)
    f3 = tie(f3, a1)
    f3x = core_swap(f3)
    f6 = tie(f6, f7, a1)
    f6x, f7x = core_swap(f6), core_swap(f7)
    s0 = tie(s0, f6)
    s1, s2, s4, s0x = zz_swap(s0), y_up(s0), y_down(s0), core_swap(s0)
    a5 = tie(a5, f6)
    a7 = x_down(a5)
    a3 = tie(a3, a5)
    c0x = tie(c0x, a3)
    c2 = x_up(c0x)
    s1 = tie(s1, s2, s4, c0x)
    s3, s5, s1x = y_up(s1), y_down(s1), core_swap(s1)
    s2 = tie(s2, s1)
    s6, s2x, s4x = y_up(s2), core_swap(s2), core_swap(s4)
    a7 = tie(a7, s1)
    c4 = x_down(tie(c0, a7, c1))
    c1 = tie(c1, c2, a7)
    c3, c5 = x_up(c1), x_down(c1)
    c2 = tie(c2, c1)
    c6 = x_up(c2)
    f_own, f_other = [f0, f1, f2, f3, f4, f5, f6, f7], [f0x, f1x, f2x, f3x, f4x, f5x, f6x, f7x]

    acts, *rest = project(
        rows_sc, [a0, a1, a2, a3, a4, a5, a6, a7], f_own, f_other, biases, other_biases, tables
    )
    qkv_own, qkv_other, (act_own, act_other), (slope_own, slope_other) = rest[:3], rest[3:6], rest[6:8], rest[8:]
    s5 = tie(s5, s3, s6, acts)
    s7, s5x = y_down(s5), core_swap(s5)
    s3, s6 = tie(s3, s5), tie(s6, s5)
    s3x, s6x = core_swap(s3), core_swap(s6)
    merged, lse = attn_fwd(rows_sc, qkv_own, qkv_other, s6)
    s7 = tie(s7, merged)
    s7x = core_swap(s7)
    c5 = tie(c5, c4, c3, s7)
    c7 = x_down(c5)
    s_own, s_other = [s0, s1, s2, s3, s4, s5, s6, s7], [s0x, s1x, s2x, s3x, s4x, s5x, s6x, s7x]
    br = branch_part(merged, act_own, act_other, s_own, s_other, c5)
    c6 = tie(c6, c7, br[0])
    br_6, br_5 = tie(br[6], c6), tie(br[5], c6)
    br_fa, br_fz, br_uz, br_da = x_up(br_6), x_down(br[7]), x_up(br_5), x_down(br[2])

    gout, gm_own, gm_other, gh_own, gh_other, g2_other, up_sum_own, up_sum_other = grad_in(
        [c0, c1, c2, c3, c4, c5, c6, c7], s_own, s_other, slope_own, slope_other, merged, act_other, br_6
    )
    g2_received = core_swap(g2_other)
    gq_own, gq_other, g1_other, attn_sums = attn_bwd(
        rows_sc, qkv_own, qkv_other, lse, gm_own, gm_other, tables, acts, gh_other, gout
    )
    g1_received = core_swap(g1_other)
    br_4, br_3 = adds((br[4], br_fa), (br[3], br_fz), deps=(gq_own, br_uz, br_da))
    br_ua, br_dz = x_up(br_4), x_down(br_3)
    g2 = second_grad(merged, act_own, gout, g2_received, br_4)
    g2_fa, g2_fz, g2_uz, g2_da = y_up(g2[6]), y_down(g2[7]), y_up(g2[5]), y_down(g2[2])
    *gn, sums = gnormed_part(sc, gq_own, gh_own, gq_other, gh_other, acts, f_own, f_other, g2[0])
    gn_fa, gn_fz, gn_uz, gn_da = x_up(gn[6]), x_down(gn[7]), x_up(gn[5]), x_down(gn[2])

    vector = jnp.concatenate([cot_sum, sums.reshape(1, -1)], axis=1)
    own_sums = jnp.concatenate([attn_sums[0], up_sum_own], axis=1)
    other_sums = jnp.concatenate([attn_sums[1], up_sum_other], axis=1)
    received = core_swap(jnp.concatenate([vector, other_sums], axis=1))
    g2_4, g2_3 = adds((g2[4], g2_fa), (g2[3], g2_fz), deps=(gn[0], g2_uz, g2_da, br_ua, br_dz))
    g2_ua, g2_dz = y_up(g2_4), y_down(g2_3)

    g1 = first_grad(gq_own, gh_own, acts, g1_received, g2_4)
    g1_fa, g1_fz, g1_uz, g1_da = y_up(g1[6]), y_down(g1[7]), y_up(g1[5]), y_down(g1[2])
    vector = jnp.concatenate([vector, own_sums], axis=1) + tie(received, g1[0])
    vector = sum_over(vector, y_pair)
    gn_4, gn_3 = adds((gn[4], gn_fa), (gn[3], gn_fz), deps=(vector, gn_uz, gn_da))
    gn_ua, gn_dz = x_up(gn_4), x_down(gn_3)
    (br_1,) = adds((br[1], br_uz, br_dz), deps=(gn_4, g2_ua, g2_dz))
    br_z = z_swap(br_1)
    vector = sum_over(tie(vector, br_1), y_cross)
    g1_4, g1_3 = adds((g1[4], g1_fa), (g1[3], g1_fz), deps=(vector, g1_uz, g1_da))
    g1_ua, g1_dz = y_up(g1_4), y_down(g1_3)
    (g2_1,) = adds((g2[1], g2_uz, g2_dz), deps=(g1_4,))
    g2_z = zz_swap(g2_1)
    br_z = tie(br_z, g2_1)
    br_parts = (br[0], br_ua, br_da, br_z)
    (br_send,) = adds(br_parts, rows=slice(64, 128))
    br_received = core_swap(br_send)
    (gn_1,) = adds((gn[1], gn_uz, gn_dz), deps=(br_send, gn_ua))
    gn_z = z_swap(gn_1)
    layer_out = post_out(sc, tokens, br_parts, tie(br_received, gn_1), (dense_bias + down_bias)[None, :])
    vector = sum_over(tie(vector, layer_out), zz_swap)
    bias_grads = vector[0, 6144:]
    vector = vector[:, :6144]
    (g1_1,) = adds((g1[1], g1_uz, g1_dz), deps=(vector, g1_ua))
    g1_z = zz_swap(g1_1)
    gn_z = tie(gn_z, g1_1)
    gn_parts = (gn[0], gn_ua, gn_da, gn_z)
    (gn_send,) = adds(gn_parts, rows=slice(64, 128))
    gn_received = core_swap(gn_send)
    vector = sum_over(tie(vector, gn_send), z_swap)
    second_out = sum(a.astype(F32) for a in (g2[0], g2_ua, g2_da, tie(g2_z, vector)))
    grad_tokens = post_grad(sc, tokens, cotangent, gn_parts, tie(gn_received, vector), gain_row)
    vector = sum_over(tie(vector, grad_tokens), x_pair)
    first_out = sum(a.astype(F32) for a in (g1[0], g1_ua, g1_da, tie(g1_z, vector)))
    vector = sum_over(vector, x_cross)

    out_bias_grad, norm_bias_grad, weighted = vector[0].reshape(3, -1)
    norm_gain_grad = (weighted - norm_bias * norm_bias_grad) / norm_gain
    return (
        layer_out,
        grad_tokens,
        by_head(first_out[:, :384]),
        by_head(bias_grads[:384]),
        second_out[:128],
        out_bias_grad,
        first_out[:, 384:],
        bias_grads[384:],
        second_out[128:],
        out_bias_grad,
        norm_gain_grad,
        norm_bias_grad,
    )


def solution(mesh):
    in_specs = (
        P("dp", "tensor", None),
        P("dp", "tensor"),
        P("tensor"),
        P("tensor", "dp"),
        P(),
        P("dp", "tensor"),
        P("tensor"),
        P("tensor", "dp"),
        P(),
        P(),
        P(),
        P("dp", "tensor", None),
    )
    out_specs = (
        P("dp", "tensor", None),
        P("dp", "tensor", None),
        P("dp", "tensor"),
        P("tensor"),
        P("tensor", "dp"),
        P(),
        P("dp", "tensor"),
        P("tensor"),
        P("tensor", "dp"),
        P(),
        P(),
        P(),
    )
    return jax.shard_map(shards, mesh=mesh, in_specs=in_specs, out_specs=out_specs, check_vma=False)
```

```python
import functools

import jax
import jax.numpy as jnp
import numpy as np
from jax import lax
from jax.experimental import pallas as pl
from jax.experimental.pallas import tpu as pltpu
from jax.sharding import PartitionSpec as P

HEAD_DIM = 64
ROT = 32
EPS = 1e-05
BF = jnp.bfloat16
LIMIT = 60
F32 = jnp.float32

OFFSETS = (0, -1, 1, 2)


def tensor_index(x, zlo, core):
    return (x % 4) * 4 + (zlo % 2) * 2 + core % 2


def dp_index(zhi, y):
    return (zhi % 2) * 4 + y % 4


def tensor_move(dx, dz, dc):
    return [
        (tensor_index(x, z, c), tensor_index(x + dx, z + dz, c + dc))
        for x in range(4)
        for z in range(2)
        for c in range(2)
    ]


def dp_move(dz, dy):
    return [(dp_index(z, y), dp_index(z + dz, y + dy)) for z in range(2) for y in range(4)]


def x_up(a):
    return lax.ppermute(a, "tensor", tensor_move(1, 0, 0))


def x_down(a):
    return lax.ppermute(a, "tensor", tensor_move(-1, 0, 0))


def z_swap(a):
    return lax.ppermute(a, "tensor", tensor_move(0, 1, 0))


def core_swap(a):
    return lax.ppermute(a, "tensor", tensor_move(0, 0, 1))


def y_up(a):
    return lax.ppermute(a, "dp", dp_move(0, 1))


def y_down(a):
    return lax.ppermute(a, "dp", dp_move(0, -1))


def zz_swap(a):
    return lax.ppermute(a, "dp", dp_move(1, 0))


def tie_body(*refs):
    pass


def tie(value, *others):
    anywhere = pl.BlockSpec(memory_space=pl.ANY)
    return pl.pallas_call(
        tie_body,
        in_specs=[anywhere] * (1 + len(others)),
        out_specs=anywhere,
        out_shape=jax.ShapeDtypeStruct(value.shape, value.dtype),
        input_output_aliases={0: 0},
        compiler_params=pltpu.CompilerParams(),
        cost_estimate=pl.CostEstimate(flops=0, bytes_accessed=0, transcendentals=0),
        name="tie",
    )(value, *others)


def join_body(own, received, *outs):
    rows = own.shape[0]
    for out in outs:
        out[:rows, :], out[rows:, :] = own[...], received[...]


def join(own, received):
    rows, width = own.shape
    return call(join_body, vmem(2), vmem(1), [shape((2 * rows, width))], (own, received), "join")[0]


def x_pair(a):
    return lax.ppermute(a, "tensor", [(i, tensor_index(i // 4 ^ 1, i // 2 % 2, i % 2)) for i in range(16)])


def x_cross(a):
    return lax.ppermute(a, "tensor", [(i, tensor_index(3 - i // 4, i // 2 % 2, i % 2)) for i in range(16)])


def y_pair(a):
    return lax.ppermute(a, "dp", [(i, dp_index(i // 4, i % 4 ^ 1)) for i in range(8)])


def y_cross(a):
    return lax.ppermute(a, "dp", [(i, dp_index(i // 4, 3 - i % 4)) for i in range(8)])


def vmem(count):
    return [pl.BlockSpec(memory_space=pltpu.VMEM)] * count


def feature_blocks():
    d, t = lax.axis_index("dp"), lax.axis_index("tensor")
    zhi, y = d // 4, d % 4
    return [((zhi + j) % 2) * 4 + (y + o) % 4 for o in OFFSETS for j in range(2)] + [t % 2]


def row_blocks():
    t = lax.axis_index("tensor")
    x, zlo, core = t // 4, (t // 2) % 2, t % 2
    return [
        4 * ((x + o) % 4) + 2 * ((zlo + j) % 2) + (core + k) % 2
        for o in OFFSETS
        for j in range(2)
        for k in range(2)
    ]


def anywhere(count=1):
    return [pl.BlockSpec(memory_space=pl.ANY)] * count


def params(limit=LIMIT):
    return pltpu.CompilerParams(vmem_limit_bytes=limit * 1024 * 1024)


TIMES = dict(
    project=17, attn_fwd=10, branch_part=11, grad_in=17, attn_bwd=20, second_grad=60, gnormed_part=15, first_grad=40,
    adds=0, finish=0, post_out=0, post_grad=0, pre=0, join=0,
)
FLOPS = 350_000_000


def call(body, in_specs, out_specs, out_shape, args, name, scratch=(), **kwargs):
    return pl.pallas_call(
        body,
        in_specs=in_specs,
        out_specs=out_specs,
        out_shape=out_shape,
        scratch_shapes=list(scratch),
        compiler_params=params(),
        cost_estimate=pl.CostEstimate(flops=TIMES[name] * FLOPS + 1, bytes_accessed=1, transcendentals=0),
        name=name,
        **kwargs,
    )(*args)


def shape(dims, dtype=BF):
    return jax.ShapeDtypeStruct(dims, dtype)


class Copy:
    def __init__(self, src, dst, sem):
        self.copy, self.waited = pltpu.make_async_copy(src, dst, sem), False
        self.copy.start()

    def wait(self):
        if not self.waited:
            self.copy.wait()
        self.waited = True


def copier(sems):
    used = iter(range(sems.shape[0]))
    return lambda src, dst: Copy(src, dst, sems.at[next(used)])


def wait(copies):
    for copy in copies:
        copy.wait()


def adds_body(groups, count, *refs):
    sizes = [len(group) for group in groups]
    ins, outs, sems = refs[: sum(sizes)], refs[count : count + len(groups)], refs[-1]
    holds = refs[count + len(groups) : -1]
    start = copier(sems)
    rows = [r for group in groups for r in group]
    copies = [start(a if r is None else a.at[r, :], b) for a, r, b in zip(ins, rows, holds)]
    at = 0
    for size, out in zip(sizes, outs):
        wait(copies[at : at + size])
        total = holds[at][...].astype(F32)
        for hold in holds[at + 1 : at + size]:
            total = total + hold[...].astype(F32)
        out[...] = total.astype(out.dtype)
        at += size


def adds(*groups, deps=()):
    groups = [[a if isinstance(a, tuple) else (a, None) for a in group] for group in groups]
    flat_groups = [a for group in groups for a in group]
    dims = [(r.stop - r.start if r else a.shape[0], a.shape[1]) for a, r in flat_groups]
    rows = tuple(tuple(r for _, r in group) for group in groups)
    firsts = [sum(len(group) for group in groups[:k]) for k in range(len(groups))]
    return call(
        functools.partial(adds_body, rows, len(flat_groups) + len(deps)),
        anywhere(len(flat_groups) + len(deps)),
        vmem(len(groups)),
        [shape(dims[k], flat_groups[k][0].dtype) for k in firsts],
        (*(a for a, _ in flat_groups), *deps),
        "adds",
        [pltpu.VMEM(dim, a.dtype) for dim, (a, _) in zip(dims, flat_groups)]
        + [pltpu.SemaphoreType.DMA((len(flat_groups),))],
    )


def finish_first_body(a, b, c, d, attn_out, up_out, p0, p1, p2, p3, sems):
    start = copier(sems)
    wait([start(a, p0), start(b, p1), start(c.at[256:, :], p2), start(d, p3)])
    total = sum(p[...].astype(F32) for p in (p0, p1, p2, p3))
    by_head = [total[:, (2 * k + h) * 64 : (2 * k + h) * 64 + 64] for h in range(2) for k in range(3)]
    attn_out[...] = jnp.concatenate(by_head, axis=1)
    up_out[...] = total[:, 384:]


def finish_first(a, b, c, d, dep):
    return call(
        lambda a, b, c, d, dep, *refs: finish_first_body(a, b, c, d, *refs),
        anywhere(5),
        vmem(2),
        [shape((256, 384), F32), shape((256, 512), F32)],
        (a, b, c, d, dep),
        "finish",
        [pltpu.VMEM((256, 896), BF)] * 4 + [pltpu.SemaphoreType.DMA((4,))],
    )


def finish_second_body(a, b, c, d, dep, dense_out, down_out, p0, p1, p2, p3, sems):
    start = copier(sems)
    wait([start(a, p0), start(b, p1), start(c.at[640:, :], p2), start(d, p3)])
    total = sum(p[...].astype(F32) for p in (p0, p1, p2, p3))
    dense_out[...], down_out[...] = total[:128, :], total[128:, :]


def finish_second(a, b, c, d, dep):
    return call(
        finish_second_body,
        anywhere(5),
        vmem(2),
        [shape((128, 256), F32), shape((512, 256), F32)],
        (a, b, c, d, dep),
        "finish",
        [pltpu.VMEM((640, 256), BF)] * 4 + [pltpu.SemaphoreType.DMA((4,))],
    )


def finish_vector_body(a, b, norm_bias, norm_gain, dep, out_bias, gain_out, bias_out):
    total = a[...] + b[...]
    out_bias[...] = total[0:1, :]
    bias_out[...] = total[1:2, :]
    gain_out[...] = (total[2:3, :] - norm_bias[...] * total[1:2, :]) / norm_gain[...]


def finish_vector(parts, norm_bias, norm_gain, dep):
    return call(
        finish_vector_body,
        vmem(4) + anywhere(),
        vmem(3),
        [shape((1, 2048), F32)] * 3,
        (*parts, norm_bias, norm_gain, dep),
        "finish",
    )


def pre_body(
    tok_in, cot_in, gain, bias, attn_in, up, dense, down,
    acts_out, acts_send, cotsum, first, second, tok, cot, attn, hold, sems,
):
    sc = feature_blocks()
    start = copier(sems)
    in_attn = start(attn_in, attn)
    in_tok = start(tok_in, tok)
    in_cot = start(cot_in, cot)
    rest = [start(up, first.at[:, 384:]), start(dense, second.at[:128, :]), start(down, second.at[128:, :])]
    by_kind = lambda a: jnp.concatenate(
        [a[:, (3 * h + k) * 64 : (3 * h + k) * 64 + 64] for k in range(3) for h in range(2)], axis=1
    )
    in_attn.wait()
    first[:, :384] = by_kind(attn[...])
    in_tok.wait()
    in_cot.wait()
    total = jnp.zeros(cotsum.shape, F32)
    for s in range(2):
        seq = sc[8] if s == 0 else 1 - sc[8]
        xin = tok[seq].astype(F32)
        centred = xin - jnp.mean(xin, axis=-1, keepdims=True)
        spread = jnp.mean(centred * centred, axis=-1, keepdims=True)
        hold[...] = (centred * lax.rsqrt(spread + EPS) * gain[...] + bias[...]).astype(BF)
        total = total + jnp.sum(cot[seq].astype(F32), axis=0, keepdims=True)
        for r in range(8):
            cols = pl.ds(pl.multiple_of(sc[r] * 256, 256), 256)
            to = slice(r * 256, (r + 1) * 256)
            (acts_out, acts_send)[s][:, to] = hold[:, cols]
    cotsum[...] = total
    wait(rest)


def pre(tok, cot, gain, bias, attn, *rest):
    rows, width = tok.shape[1:]
    return call(
        pre_body,
        anywhere(2) + vmem(2) + anywhere(4),
        vmem(5),
        [
            shape((rows, width)),
            shape((rows, width)),
            shape((1, width), F32),
            shape((256, 896)),
            shape((640, 256)),
        ],
        (tok, cot, gain, bias, attn, *rest),
        "pre",
        [pltpu.VMEM(tok.shape, BF), pltpu.VMEM(tok.shape, BF), pltpu.VMEM(attn.shape, BF)]
        + [pltpu.VMEM((rows, width), BF), pltpu.SemaphoreType.DMA((6,))],
    )


def own_rows(sc, parts, received, hold):
    for s in range(2):
        rows = sum(ref[...].astype(F32) for ref in parts) if s == 0 else received[...].astype(F32)
        for r in range(8):
            cols = pl.ds(pl.multiple_of(sc[r] * 256, 256), 256)
            hold[s, :, cols] = rows[:, r * 256 : (r + 1) * 256]


def post_out_body(tok, part, received, extra, out):
    sc = feature_blocks()
    for s in range(2):
        seq = sc[8] if s == 0 else 1 - sc[8]
        rows = (part[:64, :] if s == 0 else received[...]).astype(F32)
        out[seq] = (tok[seq].astype(F32) + rows + extra[...]).astype(BF)


def post_out(tok, part, received, extra):
    return call(
        post_out_body,
        vmem(4),
        pl.BlockSpec(memory_space=pltpu.VMEM),
        shape(tok.shape),
        (tok, part, received, extra),
        "post_out",
    )


def post_grad_body(tok_in, cot_in, a, b, c, d, received, gain, out, tok, cot, hold, p0, p1, p2, p3, p4, sems):
    sc = feature_blocks()
    start = copier(sems)
    ins = [start(ref.at[:64, :], p) for ref, p in zip((a, b, c.at[128:, :], d, received), (p0, p1, p2, p3, p4))]
    wait(ins + [start(tok_in, tok), start(cot_in, cot)])
    own_rows(sc, (p0, p1, p2, p3), p4, hold)
    for s in range(2):
        seq = sc[8] if s == 0 else 1 - sc[8]
        xin = tok[seq].astype(F32)
        centred = xin - jnp.mean(xin, axis=-1, keepdims=True)
        scale = lax.rsqrt(jnp.mean(centred * centred, axis=-1, keepdims=True) + EPS)
        xhat = centred * scale
        e = hold[s] * gain[...]
        mean_e = jnp.mean(e, axis=-1, keepdims=True)
        mean_x = jnp.mean(e * xhat, axis=-1, keepdims=True)
        out[seq] = cot[seq].astype(F32) + (e - mean_e - xhat * mean_x) * scale


def post_grad(tok, cot, parts, received, gain):
    rows = tok.shape[1:]
    return call(
        post_grad_body,
        anywhere(7) + vmem(1),
        pl.BlockSpec(memory_space=pltpu.VMEM),
        shape(tok.shape, F32),
        (tok, cot, *parts, received, gain),
        "post_grad",
        [pltpu.VMEM(tok.shape, BF)] * 2
        + [pltpu.VMEM(tok.shape, F32)]
        + [pltpu.VMEM(rows, BF)] * 5
        + [pltpu.SemaphoreType.DMA((7,))],
    )


def turn(u, cosine, sine_low, sine_high):
    return (
        u * cosine
        + pltpu.roll(u, u.shape[-1] - ROT // 2, 1) * sine_low
        + pltpu.roll(u, ROT // 2, 1) * sine_high
    )


def turn_back(u, cosine, sine_low, sine_high):
    return (
        u * cosine
        - pltpu.roll(u, u.shape[-1] - ROT // 2, 1) * sine_low
        - pltpu.roll(u, ROT // 2, 1) * sine_high
    )


def dot(a, b):
    return lax.dot_general(a, b, (((1,), (0,)), ((), ())), preferred_element_type=F32)


def dot_nt(a, b):
    return lax.dot_general(a, b, (((1,), (1,)), ((), ())), preferred_element_type=F32)


def dot_tn(a, b):
    return lax.dot_general(a, b, (((0,), (0,)), ((), ())), preferred_element_type=F32)


QB = 256


def diagonal(size):
    keys = lax.broadcasted_iota(jnp.int32, (size, size), 0)
    queries = lax.broadcasted_iota(jnp.int32, (size, size), 1)
    return keys <= queries


def attn_fwd_body(*refs):
    sc = row_blocks()
    dep, merged, lse, out_t, out_abs, q_in, k_in, v_in, sems = refs[6:]
    start = copier(sems)
    wait([start(refs[3 * h + k], held.at[h]) for h in range(2) for k, held in enumerate((q_in, k_in, v_in))])
    for h in range(2):
        attn_fwd_half(h, sc, merged, lse, out_t, out_abs, q_in, k_in, v_in)


def attn_fwd_half(h, sc, merged, lse, out_t, out_abs, q_in, k_in, v_in):
    keys = k_in[h]
    values_t = v_in[h].T
    lane = lax.broadcasted_iota(jnp.int32, (QB, 128), 1)
    allowed = diagonal(QB)
    for b in range(1024 // QB):
        begin, end = b * QB, (b + 1) * QB
        query = q_in[h, begin:end, :]
        for a in range(2):
            heads = slice(a * HEAD_DIM, (a + 1) * HEAD_DIM)
            only = jnp.where(lane // HEAD_DIM == a, query, jnp.zeros_like(query))
            scores = dot_nt(keys[:end], only)
            low = jnp.where(allowed, scores[begin:], -jnp.inf)
            top = jnp.max(low, axis=0, keepdims=True)
            if b > 0:
                top = jnp.maximum(top, jnp.max(scores[:begin], axis=0, keepdims=True))
            weights = jnp.exp(low - top)
            total = jnp.sum(weights, axis=0, keepdims=True)
            out = dot(values_t[:, begin:end], weights.astype(BF))
            if b > 0:
                weights = jnp.exp(scores[:begin] - top)
                total = total + jnp.sum(weights, axis=0, keepdims=True)
                out = out + dot(values_t[:, :begin], weights.astype(BF))
            out_t[heads, begin:end] = (out * (1.0 / total))[heads, :]
            lse[2 * h + a : 2 * h + a + 1, begin:end] = top + jnp.log(total)
    for r in range(1024 // 128):
        here = slice(128 * r, 128 * r + 128)
        out_abs[here, :] = out_t[:, here].T.astype(BF)
    for r in range(1024 // 64):
        there = pl.ds(pl.multiple_of(sc[r] * 64, 64), 64)
        merged[64 * r : 64 * r + 64, 128 * h : 128 * h + 128] = out_abs[there, :]


def attn_fwd(own, other, dep):
    length = own[0].shape[0]
    return call(
        attn_fwd_body,
        anywhere(7),
        vmem(2),
        [shape((length, 256)), shape((4, length), F32)],
        (*own, *other, dep),
        "attn_fwd",
        [pltpu.VMEM((128, length), F32), pltpu.VMEM((length, 128), BF)]
        + [pltpu.VMEM((2, length, 128), BF)] * 3
        + [pltpu.SemaphoreType.DMA((6,))],
    )


def attn_bwd_body(*refs):
    sc = row_blocks()
    lse, tables_in, (acts_in, gh_in, dep) = refs[8], refs[9:12], refs[12:15]
    outs, g1_out, colsum = refs[15:17], refs[17], refs[18]
    gqkv, gm_hold, dq_t, dq, dk, dv, q_in, k_in, v_in, gm_in = refs[19:29]
    tables, (acts, rhs, g1, sems) = refs[29:32], refs[32:]
    start = copier(sems)
    held = (gm_in, k_in, q_in, v_in)
    ins = [start(refs[4 * h + k], a.at[h]) for h in (1, 0) for k, a in enumerate(held)]
    ins += [start(a, b) for a, b in zip(tables_in, tables)]
    rest = [start(gh_in, rhs.at[:, 384:]), start(acts_in, acts)]
    wait(ins)
    copies = []
    for h in (1, 0):
        attn_bwd_half(h, sc, lse, *tables, gqkv, colsum, gm_hold, dq_t, dq, dk, dv, q_in, k_in, v_in, gm_in)
        copies.append(start(gqkv.at[h], outs[h]))
    wait(rest)
    rhs[:, :384] = gqkv[1]
    for rows in blocks_of(512, 4):
        g1[rows, :] = dot_tn(acts[:, rows], rhs[...]).astype(BF)
        copies.append(start(g1.at[rows, :], g1_out.at[rows, :]))
    wait(copies)


def attn_bwd_half(
    h, sc, lse, cos_t, low_t, high_t, gqkv, colsum, gm_hold, dq_t, dq, dk, dv, q_in, k_in, v_in, gm_in
):
    for r in range(1024 // 64):
        there = pl.ds(pl.multiple_of(sc[r] * 64, 64), 64)
        gm_hold[there, :] = gm_in[h, 64 * r : 64 * r + 64, :]
    keys = k_in[h]
    values = v_in[h]
    keys_t = keys.T
    lane = lax.broadcasted_iota(jnp.int32, (QB, 128), 1)
    allowed = diagonal(QB)
    for b in reversed(range(1024 // QB)):
        begin, end = b * QB, (b + 1) * QB
        query = q_in[h, begin:end, :]
        grad = gm_hold[begin:end, :]
        add_v, add_k = 0.0, 0.0
        for a in range(2):
            heads = slice(a * HEAD_DIM, (a + 1) * HEAD_DIM)
            mine = lane // HEAD_DIM == a
            only = jnp.where(mine, query, jnp.zeros_like(query))
            grad_only = jnp.where(mine, grad, jnp.zeros_like(grad))
            shift = lse[2 * h + a : 2 * h + a + 1, begin:end]
            scores = dot_nt(keys[:end], only)
            dprobs = dot_nt(values[:end], grad_only)
            low_p = jnp.where(allowed, jnp.exp(scores[begin:] - shift), 0.0)
            probs = low_p if b == 0 else jnp.concatenate([jnp.exp(scores[:begin] - shift), low_p], axis=0)
            delta = jnp.sum(probs * dprobs, axis=0, keepdims=True)
            gscores = (probs * (dprobs - delta)).astype(BF)
            add_v = add_v + dot(probs.astype(BF), grad_only)
            add_k = add_k + dot(gscores, only)
            dq_t[heads, begin:end] = dot(keys_t[:, :end], gscores)[heads, :]
        if end == 1024:
            dv[...], dk[...] = add_v, add_k
        else:
            dv[:end, :] += add_v
            dk[:end, :] += add_k
    for r in range(1024 // 128):
        here = slice(128 * r, 128 * r + 128)
        dq[here, :] = dq_t[:, here].T
    total = jnp.zeros((1, 384), F32)
    for r in range(1024 // 64):
        here = slice(64 * r, 64 * r + 64)
        there = pl.ds(pl.multiple_of(sc[r] * 64, 64), 64)
        tables = (cos_t[there, :], low_t[there, :], high_t[there, :])
        gq = turn_back(dq[there, :] * (HEAD_DIM**-0.5), *tables)
        gk = turn_back(dk[there, :], *tables)
        rows = jnp.concatenate([gq, gk, dv[there, :]], axis=1).astype(BF)
        gqkv[h, here, :] = rows
        total = total + jnp.sum(rows.astype(F32), axis=0, keepdims=True)
    colsum[h] = total


def attn_bwd(own, other, lse, gm_own, gm_other, tables, acts, gh_other, dep):
    length = gm_own.shape[0]
    ins = []
    for (q, k, v), gm in ((own, gm_own), (other, gm_other)):
        ins += [gm, k, q, v]
    return call(
        attn_bwd_body,
        anywhere(8) + vmem(1) + anywhere(6),
        anywhere(3) + vmem(1),
        [shape((length, 384))] * 2 + [shape((2048, 896)), shape((2, 1, 384), F32)],
        (*ins, lse, *tables, acts, gh_other, dep),
        "attn_bwd",
        [pltpu.VMEM((2, length, 384), BF), pltpu.VMEM((length, 128), BF), pltpu.VMEM((128, length), F32)]
        + [pltpu.VMEM((length, 128), F32)] * 3
        + [pltpu.VMEM((2, length, 128), BF)] * 4
        + [pltpu.VMEM((length, 128), F32)] * 3
        + [pltpu.VMEM((1024, 2048), BF), pltpu.VMEM((1024, 896), BF), pltpu.VMEM((2048, 896), BF)]
        + [pltpu.SemaphoreType.DMA((32,))],
    )


ROWS = 256
HUGE = (pltpu.SemaphoreType.DMA((176,)),)


def blocks_of(size=256, count=8):
    return [slice(size * r, size * r + size) for r in range(count)]


def message_places(outs, rows):
    up, down, own_a, own_z, left_z, right_a = outs
    one, two = slice(0, rows), slice(rows, 2 * rows)
    return [own_a, own_z, down.at[two, :], left_z, right_a, up.at[two, :], up.at[one, :], down.at[one, :]]


def flat(groups):
    return [copy for group in groups for copy in group]


def project_body(*refs):
    sc = row_blocks()
    pieces, w_own, w_other = refs[:8], refs[8:16], refs[16:24]
    b_own, b_other, tables_in = refs[24], refs[25], refs[26:29]
    acts_out, qkv_out = refs[29], refs[30:36]
    act_out, slope_out = refs[36:38], refs[38:40]
    acts, w, cos_t, low_t, high_t = refs[40:45]
    qkv, act, slope, sems = refs[45:51], refs[51:53], refs[53:55], refs[55]
    start = copier(sems)

    def tile(j):
        group = []
        for r, rows in enumerate(blocks_of()):
            if j < 6:
                cols = slice(256 * (j % 3), 256 * (j % 3) + 256)
                group.append(((w_own, w_other)[j // 3][r].at[:, cols], w.at[j, rows, :]))
            else:
                group.append((w_own[r].at[:, 768:], w.at[j, rows, :128]))
                group.append((w_other[r].at[:, 768:], w.at[j, rows, 128:]))
        return group

    def rows_in(m):
        return [(pieces[r], acts.at[128 * r : 128 * r + 128, :]) for r in (2 * m, 2 * m + 1)]

    def begin(group):
        return [start(a, b) for a, b in group]

    acts_in = [begin(rows_in(0))]
    w_in = [begin(tile(j)) for j in range(3)]
    rest = begin(zip(tables_in, (cos_t, low_t, high_t)))
    acts_in += [begin(rows_in(m)) for m in range(1, 4)]
    w_in += [begin(tile(j)) for j in range(3, 7)]
    root = (2.0 / np.pi) ** 0.5
    outs = []
    strips = [[(j // 3, 2 * (j % 3) + k) for k in range(2)] for j in range(6)] + [[(0, 6), (1, 6)]]
    steps = [(m, j) for m in range(4) for j in range(3)] + [(m, j) for m in range(4) for j in range(3, 7)]
    for m, j in steps:
        rows = slice(ROWS * m, ROWS * m + ROWS)
        if j == 0 and m == 0:
            wait(acts_in[0] + flat(w_in[:3]) + rest)
        if j == 0 and m == 1:
            wait(flat(acts_in[1:]))
            outs.append(start(acts, acts_out))
        if j == 3 and m == 0:
            wait(flat(w_in[3:]))
        result = dot(acts[rows, :], w[j])
        for k, (core, strip) in enumerate(strips[j]):
            cols = slice(128 * strip, 128 * strip + 128)
            h = result[:, 128 * k : 128 * k + 128] + (b_own, b_other)[core][:, cols]
            if strip < 3:
                for b in range(ROWS // 64):
                    there = pl.ds(pl.multiple_of(sc[4 * m + b] * 64, 64), 64)
                    u = h[64 * b : 64 * b + 64, :]
                    if strip < 2:
                        u = turn(u, cos_t[there, :], low_t[there, :], high_t[there, :])
                    if strip == 0:
                        u = u * (HEAD_DIM**-0.5)
                    qkv[3 * core + strip][there, :] = u.astype(BF)
                continue
            cols = slice(128 * (strip - 3), 128 * (strip - 3) + 128)
            square = h * h
            th = jnp.tanh(root * (h + 0.044715 * (square * h)))
            half = 0.5 + 0.5 * th
            act[core][rows, cols] = (h * half).astype(BF)
            slope[core][rows, cols] = (
                half + (0.5 * h) * (1.0 - th * th) * (root + (3 * 0.044715 * root) * square)
            ).astype(BF)
        if j == 6:
            for a, b in zip((*act, *slope), (*act_out, *slope_out)):
                outs.append(start(a.at[rows, :], b.at[rows, :]))
    for a, b in zip(qkv, qkv_out):
        outs.append(start(a, b))
    wait(outs)


def project(pieces, w_own, w_other, b_own, b_other, tables):
    small, wide, whole = (1024, 128), (1024, 512), (1024, 2048)
    return call(
        project_body,
        anywhere(24) + vmem(2) + anywhere(3),
        anywhere(11),
        [shape(whole)] + [shape(small)] * 6 + [shape(wide)] * 4,
        (*pieces, *w_own, *w_other, b_own, b_other, *tables),
        "project",
        [pltpu.VMEM(whole, BF), pltpu.VMEM((7, 2048, 256), BF)]
        + [pltpu.VMEM(small, F32)] * 3
        + [pltpu.VMEM(small, BF)] * 6
        + [pltpu.VMEM(wide, BF)] * 4
        + [*HUGE],
    )


def branch_body(merged, act_own, act_other, w_own, w_other, dep, out, lhs, w, stage, sems):
    sc = row_blocks()
    start = copier(sems)
    parts = ((merged.at[:, :128], 0, 128), (act_own, 128, 512), (merged.at[:, 128:], 640, 128), (act_other, 768, 512))
    lhs_in = [start(a, lhs.at[:, c : c + n]) for a, c, n in parts]
    w_in = [[start(w_own.at[r], w.at[r, :640, :]), start(w_other.at[r], w.at[r, 640:, :])] for r in range(8)]
    copies = []
    for half in (range(3), range(3, 8)):
        wait(lhs_in + flat(w_in[r] for r in half))
        for m in range(4):
            rows = slice(ROWS * m, ROWS * m + ROWS)
            for r in half:
                stage[rows, 256 * r : 256 * r + 256] = dot(lhs[rows, :], w[r]).astype(BF)
            if 7 in half:
                for p in (2 * m, 2 * m + 1):
                    to = pl.ds(pl.multiple_of(sc[2 * p] // 2 * 128, 128), 128)
                    copies.append(start(stage.at[128 * p : 128 * p + 128, :], out.at[to, :]))
    wait(copies)


def branch_part(merged, act_own, act_other, w_own, w_other, dep):
    return call(
        branch_body,
        anywhere(6),
        pl.BlockSpec(memory_space=pl.ANY),
        shape((1024, 2048)),
        (merged, act_own, act_other, w_own, w_other, dep),
        "branch_part",
        [pltpu.VMEM((1024, 1280), BF), pltpu.VMEM((8, 1280, 256), BF), pltpu.VMEM((1024, 2048), BF), *HUGE],
    )


def grad_in_body(cot, w_own, w_other, *refs):
    core, rows_sc = feature_blocks()[8], row_blocks()
    slope_in, (merged, act, dep) = refs[:2], refs[2:5]
    gout_out, gm_out, gh_out, g2_out, colsum = refs[5], refs[6:8], refs[8:10], refs[10], refs[11:13]
    gout, w, slope, gm, gh, lhs, stage, sems = refs[13], refs[14], refs[15:17], refs[17:19], refs[19:21], *refs[21:]
    start = copier(sems)

    def tile(j):
        copies = []
        for r, cols in enumerate(blocks_of()):
            for first, source, at in ((0, w_own, 256 * j), (640, w_other, 256 * j - 640)):
                lo, hi = max(at, 0), min(at + 256, 640)
                if lo < hi:
                    copies.append(start(source.at[r, lo:hi, :], w.at[lo + first : hi + first, cols]))
        return copies

    gout_in = [start(cot.at[rows_sc[r], core], gout.at[64 * r : 64 * r + 64, :]) for r in range(16)]
    w_in = [tile(0)]
    slope_copies = [start(a, b) for a, b in zip(slope_in, slope)]
    w_in += [tile(j) for j in range(1, 5)]
    lhs_in = [start(merged.at[:, 128:], lhs.at[:, :128]), start(act, lhs.at[:, 128:])]
    totals = [[jnp.zeros((1, 128), F32)] * 4 for _ in range(2)]
    copies = []
    for j in range(5):
        if j == 0:
            wait(gout_in + w_in[0] + slope_copies)
            copies.append(start(gout, gout_out))
        if j == 1:
            wait(flat(w_in) + lhs_in)
        for m in range(4):
            rows = slice(ROWS * m, ROWS * m + ROWS)
            result = dot_nt(gout[rows, :], w[256 * j : 256 * j + 256, :])
            for k in range(2):
                half, strip = (2 * j + k) // 5, (2 * j + k) % 5
                part = result[:, 128 * k : 128 * k + 128]
                if strip == 0:
                    gm[half][rows, :] = part.astype(BF)
                    continue
                cols = slice(128 * (strip - 1), 128 * strip)
                part = (part * slope[half][rows, cols].astype(F32)).astype(BF)
                gh[half][rows, cols] = part
                totals[half][strip - 1] += jnp.sum(part.astype(F32), axis=0, keepdims=True)
    for core in range(2):
        for strip in range(4):
            colsum[core][:, 128 * strip : 128 * strip + 128] = totals[core][strip]
    for a, b in zip((*gm, *gh), (*gm_out, *gh_out)):
        copies.append(start(a, b))
    for cols in blocks_of(512, 4):
        stage[:, cols] = dot_tn(lhs[...], gout[:, cols]).astype(BF)
        copies.append(start(stage.at[:, cols], g2_out.at[:, cols]))
    wait(copies)


def grad_in(cot, w_own, w_other, slope_own, slope_other, merged, act_other, dep):
    small, wide, whole = (1024, 128), (1024, 512), (1024, 2048)
    return call(
        grad_in_body,
        anywhere(8),
        anywhere(6) + vmem(2),
        [shape(whole)] + [shape(small)] * 2 + [shape(wide)] * 2 + [shape((640, 2048))] + [shape((1, 512), F32)] * 2,
        (cot, w_own, w_other, slope_own, slope_other, merged, act_other, dep),
        "grad_in",
        [pltpu.VMEM(whole, BF), pltpu.VMEM((1280, 2048), BF)]
        + [pltpu.VMEM(wide, BF)] * 2
        + [pltpu.VMEM(small, BF)] * 2
        + [pltpu.VMEM(wide, BF)] * 2
        + [pltpu.VMEM((1024, 640), BF), pltpu.VMEM((640, 2048), BF), *HUGE],
    )


def gnormed_body(q_own, gh_own, q_other, gh_other, acts_in, *refs):
    sc = feature_blocks()
    w_own, w_other, dep, cot_sum, attn_sums, up_own, up_other = refs[:8], refs[8:16], *refs[16:21]
    outs, vec_own, vec_send, (lhs, w, acts, stage, sems) = refs[21:27], refs[27], refs[28], refs[29:]
    places = message_places(outs, 128)
    start = copier(sems)
    parts = ((q_own, 0), (gh_own, 384), (q_other, 896), (gh_other, 1280))

    def rows_in(m):
        rows = slice(ROWS * m, ROWS * m + ROWS)
        copies = [start(a.at[rows, :], lhs.at[rows, c : c + a.shape[1]]) for a, c in parts]
        return copies + [start(acts_in.at[rows, :], acts.at[rows, :])]

    def tile(r):
        rows = slice(256 * r, 256 * r + 256)
        return [start(w_own[r], w.at[rows, :896]), start(w_other[r], w.at[rows, 896:])]

    lhs_in = {3: rows_in(3)}
    w_in = [tile(r) for r in range(8)]
    lhs_in.update({m: rows_in(m) for m in range(3)})
    totals = [[jnp.zeros((1, 256), F32)] * 8 for _ in range(2)]
    copies = []
    for m, first, last in ((3, 0, 3), (3, 3, 8), (0, 0, 8), (1, 0, 8), (2, 0, 8)):
        rows = slice(ROWS * m, ROWS * m + ROWS)
        if m == 3:
            wait(lhs_in[3] + flat(w_in[first:last]))
        if m == 0:
            wait(lhs_in[0] + lhs_in[1] + lhs_in[2])
        for r in range(first, last):
            cols = slice(256 * r, 256 * r + 256)
            result = dot_nt(lhs[rows, :], w[cols, :])
            totals[0][r] += jnp.sum(result, axis=0, keepdims=True)
            totals[1][r] += jnp.sum(result * acts[rows, cols].astype(F32), axis=0, keepdims=True)
            stage[rows, cols] = result.astype(BF)
        if last == 8:
            for p in (2 * m, 2 * m + 1):
                copies.append(start(stage.at[128 * p : 128 * p + 128, :], places[p]))
    for vec, half, up in ((vec_own, 0, up_own), (vec_send, 1, up_other)):
        vec[0:1, :] = cot_sum[...]
        for k in range(2):
            for r in range(8):
                vec[k + 1 : k + 2, pl.ds(pl.multiple_of(sc[r] * 256, 256), 256)] = totals[k][r]
        vec[3:4, :384], vec[3:4, 384:896] = attn_sums[half], up[...]
        vec[3:4, 896:] = jnp.zeros((1, 2048 - 896), F32)
    wait(copies)


def gnormed_part(q_own, gh_own, q_other, gh_other, acts, w_own, w_other, dep, *vectors):
    whole, piece = (1024, 2048), shape((128, 2048))
    *outs, vec_own, vec_send = call(
        gnormed_body,
        anywhere(22) + vmem(4),
        anywhere(6) + vmem(2),
        [shape((256, 2048))] * 2 + [piece] * 4 + [shape((4, 2048), F32)] * 2,
        (q_own, gh_own, q_other, gh_other, acts, *w_own, *w_other, dep, *vectors),
        "gnormed_part",
        [pltpu.VMEM((1024, 1792), BF), pltpu.VMEM((2048, 1792), BF), pltpu.VMEM(whole, BF), pltpu.VMEM(whole, BF), *HUGE],
    )
    return outs, vec_own, vec_send


def second_body(merged, act, gout, received, dep, *refs):
    sc = feature_blocks()
    places, (lhs, rhs, held, stage, sems) = message_places(refs[:6], 640), refs[6:]
    start = copier(sems)
    lhs_in = [start(merged.at[:, :128], lhs.at[:, :128]), start(act, lhs.at[:, 128:])]
    ins = []
    for r in range(8):
        cols = pl.ds(pl.multiple_of(sc[r] * 256, 256), 256)
        ins.append([start(gout.at[:, cols], rhs.at[r]), start(received.at[:, cols], held.at[r])])
    copies = []
    for r in range(8):
        if r == 0:
            wait(lhs_in + flat(ins[:3]))
        if r == 3:
            wait(flat(ins))
        result = dot_tn(lhs[...], rhs[r])
        stage[r] = (result + held[r].astype(F32)).astype(BF)
        copies.append(start(stage.at[r], places[r]))
    wait(copies)


def second_grad(merged, act, gout, received, dep):
    return call(
        second_body,
        anywhere(5),
        anywhere(6),
        [shape((1280, 256))] * 2 + [shape((640, 256))] * 4,
        (merged, act, gout, received, dep),
        "second_grad",
        [pltpu.VMEM((1024, 640), BF), pltpu.VMEM((8, 1024, 256), BF)]
        + [pltpu.VMEM((8, 640, 256), BF)] * 2
        + [*HUGE],
    )


def first_body(blocks, count, gqkv, gh, acts, received, *refs):
    outs, (lhs, rhs, held, stage, sems) = refs[count - 4 : -5], refs[-5:]
    places = [out.at[256 * k : 256 * k + 256, :] for out in outs for k in range(out.shape[0] // 256)]
    start = copier(sems)
    rhs_in = [start(gqkv, rhs.at[:, :384]), start(gh, rhs.at[:, 384:])]
    ins = []
    for k, r in enumerate(blocks):
        rows = slice(256 * r, 256 * r + 256)
        ins.append([start(acts.at[:, rows], lhs.at[k]), start(received.at[rows, :], held.at[k])])
    copies = []
    for k in range(4):
        if k == 0:
            wait(rhs_in + ins[0])
        if k == 1:
            wait(flat(ins))
        result = dot_tn(lhs[k], rhs[...])
        stage[k] = (result + held[k].astype(F32)).astype(BF)
        copies.append(start(stage.at[k], places[k]))
    wait(copies)


def first_grad(blocks, rows, *args):
    return call(
        functools.partial(first_body, blocks, len(args)),
        anywhere(len(args)),
        anywhere(1024 // rows),
        [shape((rows, 896))] * (1024 // rows),
        args,
        "first_grad",
        [pltpu.VMEM((4, 1024, 256), BF), pltpu.VMEM((1024, 896), BF)]
        + [pltpu.VMEM((4, 256, 896), BF)] * 2
        + [*HUGE],
    )


def rotary_tables(length):
    frequency = np.float32(10000.0) ** (-(np.arange(ROT // 2, dtype=np.float32) * 2.0 / ROT))
    angles = np.arange(length, dtype=np.float32)[:, None] * frequency.astype(np.float32)[None, :]
    cosine, sine = np.cos(angles), np.sin(angles)
    one = np.ones((length, HEAD_DIM - ROT), np.float32)
    zero_half, zero = np.zeros_like(sine), np.zeros_like(one)
    cos_t = np.concatenate([cosine, cosine, one] * 2, axis=1)
    low_t = np.concatenate([-sine, zero_half, zero] * 2, axis=1)
    high_t = np.concatenate([zero_half, sine, zero] * 2, axis=1)
    return tuple(jnp.asarray(a, F32) for a in (cos_t, low_t, high_t))


def by_kind(a):
    return jnp.swapaxes(a.reshape(2, 3, HEAD_DIM), 0, 1).reshape(384)


def by_head(a):
    lead = a.shape[:-1]
    return jnp.swapaxes(a.reshape(lead + (3, 2, HEAD_DIM)), -3, -2).reshape(lead + (384,))


def shards(
    tokens,
    attn_weight,
    attn_bias,
    dense_weight,
    dense_bias,
    up_weight,
    up_bias,
    down_weight,
    down_bias,
    norm_gain,
    norm_bias,
    cotangent,
):
    tables = rotary_tables(16 * tokens.shape[1])
    gain_row, bias_row = norm_gain[None, :], norm_bias[None, :]

    cot = lax.all_gather(cotangent, "tensor", axis=0)
    acts_own, acts_send, cot_sum, f0, s0 = pre(
        tokens, cotangent, gain_row, bias_row, attn_weight, up_weight, dense_weight, down_weight
    )
    swapped = core_swap(acts_send)
    f1, f2, f4, f0x = zz_swap(f0), y_up(f0), y_down(f0), core_swap(f0)
    s_own = lax.all_gather(s0, "dp", axis=0)
    a0 = join(acts_own, swapped)
    a2, a4, a1 = x_up(a0), x_down(a0), z_swap(a0)
    f1 = tie(f1, f2, f4, a0)
    f3, f5, f1x = y_up(f1), y_down(f1), core_swap(f1)
    f2 = tie(f2, f1)
    f6, f2x, f4x = y_up(f2), core_swap(f2), core_swap(f4)
    a2 = tie(a2, a4, f2)
    a6 = x_up(a2)
    a1 = tie(a1, a2, f3, f5)
    a3, a5 = x_up(a1), x_down(a1)
    f5 = tie(f5, a1)
    f7, f5x = y_down(f5), core_swap(f5)
    a5 = tie(a5, f6)
    a7 = x_down(a5)
    f3 = tie(f3, a5, a6)
    f3x = core_swap(f3)
    f6 = tie(f6, f7, a3, f3)
    f6x, f7x = core_swap(f6), core_swap(f7)
    biases = tie(jnp.concatenate([by_kind(attn_bias), up_bias])[None, :], f1)
    other_biases = core_swap(biases)
    f_own, f_other = [f0, f1, f2, f3, f4, f5, f6, f7], [f0x, f1x, f2x, f3x, f4x, f5x, f6x, f7x]

    acts, *rest = project([a0, a1, a2, a3, a4, a5, a6, a7], f_own, f_other, biases, other_biases, tables)
    qkv_own, qkv_other, (act_own, act_other), (slope_own, slope_other) = rest[:3], rest[3:6], rest[6:8], rest[8:]
    merged, lse = attn_fwd(qkv_own, qkv_other, acts)
    s_own = tie(s_own, acts)
    s_other = core_swap(s_own)
    br = branch_part(merged, act_own, act_other, s_own, s_other, acts)
    group = [[2 * p + c for p in range(8)] for c in range(2)]
    br_sum = lax.psum_scatter(br, "tensor", scatter_dimension=0, axis_index_groups=group, tiled=True)

    gout, gm_own, gm_other, gh_own, gh_other, g2_other, up_sum_own, up_sum_other = grad_in(
        cot, s_own, s_other, slope_own, slope_other, merged, act_other, br
    )
    g2_received = core_swap(g2_other)
    gq_own, gq_other, g1_other, attn_sums = attn_bwd(
        qkv_own, qkv_other, lse, gm_own, gm_other, tables, acts, gh_other, gout
    )
    g1_received = core_swap(g1_other)
    g2_up, g2_down, g2_0, g2_1, g2_3, g2_4 = second_grad(merged, act_own, gout, g2_received, gq_own)
    g2_u, g2_d = y_up(g2_up), y_down(g2_down)
    (gn_up, gn_down, gn_0, gn_1, gn_3, gn_4), vec, vec_send = gnormed_part(
        gq_own, gh_own, gq_other, gh_other, acts, f_own, f_other, g2_0, cot_sum, attn_sums, up_sum_own, up_sum_other
    )
    gn_u, gn_d = x_up(gn_up), x_down(gn_down)
    step = core_swap(vec_send)

    n_one, n_two, m_one, m_two = slice(0, 128), slice(128, 256), slice(0, 256), slice(256, 512)
    one, two, last = slice(0, 640), slice(640, 1280), slice(64, 128)
    vec, g2_4, g2_3 = adds((vec, step), (g2_4, (g2_u, one)), (g2_3, (g2_d, one)), deps=(gn_0,))
    step = y_pair(vec)
    g2_ua, g2_dz = y_up(g2_4), y_down(g2_3)
    g1_up, g1_down = first_grad((6, 5, 7, 2), 512, gq_own, gh_own, acts, g1_received, g2_4)
    g1_u, g1_d = y_up(g1_up), y_down(g1_down)
    g1_0, g1_1, g1_3, g1_4 = first_grad(
        (0, 1, 3, 4), 256, gq_own, gh_own, acts, g1_received, g1_up, g2_ua, g2_dz
    )
    (vec,) = adds((vec, step), deps=(g1_0,))
    step = y_cross(vec)
    vec, g2_1 = adds((vec, step), (g2_1, (g2_u, two), g2_dz), deps=(g2_ua,))
    step, g2_z = zz_swap(vec), zz_swap(g2_1)
    gn_4, gn_3 = adds((gn_4, (gn_u, n_one)), (gn_3, (gn_d, n_one)), deps=(g2_1,))
    gn_ua, gn_dz = x_up(gn_4), x_down(gn_3)
    br_sum = tie(br_sum, gn_4)
    br_received = core_swap(br_sum[64:])
    layer_out = post_out(tokens, br_sum, br_received, (dense_bias + down_bias)[None, :])
    vec, g1_4, g1_3 = adds((vec, step), (g1_4, (g1_u, m_one)), (g1_3, (g1_d, m_one)), deps=(layer_out,))
    bias_grads = vec
    step = z_swap(vec)
    g1_ua, g1_dz = y_up(g1_4), y_down(g1_3)
    dense_grad, down_grad = finish_second(g2_0, g2_ua, g2_d, g2_z, g1_4)
    gn_1, vec = adds((gn_1, (gn_u, n_two), gn_dz), (vec, step), deps=(dense_grad, gn_ua))
    gn_z = z_swap(gn_1)
    step = x_pair(vec)
    g1_1, vec = adds((g1_1, (g1_u, m_two), g1_dz), (vec, step), deps=(gn_1, g1_ua))
    g1_z = zz_swap(g1_1)
    step = x_cross(vec)
    out_bias_grad, norm_gain_grad, norm_bias_grad = finish_vector(
        (vec, step), norm_bias[None, :], norm_gain[None, :], g1_1
    )
    (gn_send,) = adds(((gn_0, last), (gn_ua, last), (gn_d, slice(192, 256)), (gn_z, last)), deps=(out_bias_grad,))
    gn_received = core_swap(gn_send)
    grad_tokens = post_grad(tokens, cotangent, (gn_0, gn_ua, gn_d, gn_z), gn_received, gain_row)
    attn_grad, up_grad = finish_first(g1_0, g1_ua, g1_d, g1_z, grad_tokens)
    bias_grads, out_bias_grad = bias_grads[3, :896], out_bias_grad[0]
    return (
        layer_out,
        grad_tokens,
        attn_grad,
        by_head(bias_grads[:384]),
        dense_grad,
        out_bias_grad,
        up_grad,
        bias_grads[384:],
        down_grad,
        out_bias_grad,
        norm_gain_grad[0],
        norm_bias_grad[0],
    )


def solution(mesh):
    in_specs = (
        P("dp", "tensor", None),
        P("dp", "tensor"),
        P("tensor"),
        P("tensor", "dp"),
        P(),
        P("dp", "tensor"),
        P("tensor"),
        P("tensor", "dp"),
        P(),
        P(),
        P(),
        P("dp", "tensor", None),
    )
    out_specs = (
        P("dp", "tensor", None),
        P("dp", "tensor", None),
        P("dp", "tensor"),
        P("tensor"),
        P("tensor", "dp"),
        P(),
        P("dp", "tensor"),
        P("tensor"),
        P("tensor", "dp"),
        P(),
        P(),
        P(),
    )
    return jax.shard_map(shards, mesh=mesh, in_specs=in_specs, out_specs=out_specs, check_vma=False)
```

```python
import functools

import jax
import jax.numpy as jnp
import numpy as np
from jax import lax
from jax.experimental import pallas as pl
from jax.experimental.pallas import tpu as pltpu
from jax.sharding import PartitionSpec as P

HEAD_DIM = 64
ROT = 32
EPS = 1e-05
BF = jnp.bfloat16
LIMIT = 60
F32 = jnp.float32

OFFSETS = (0, -1, 1, 2)


def tensor_index(x, zlo, core):
    return (x % 4) * 4 + (zlo % 2) * 2 + core % 2


def dp_index(zhi, y):
    return (zhi % 2) * 4 + y % 4


def tensor_move(dx, dz, dc):
    return [
        (tensor_index(x, z, c), tensor_index(x + dx, z + dz, c + dc))
        for x in range(4)
        for z in range(2)
        for c in range(2)
    ]


def dp_move(dz, dy):
    return [(dp_index(z, y), dp_index(z + dz, y + dy)) for z in range(2) for y in range(4)]


def x_up(a):
    return lax.ppermute(a, "tensor", tensor_move(1, 0, 0))


def x_down(a):
    return lax.ppermute(a, "tensor", tensor_move(-1, 0, 0))


def z_swap(a):
    return lax.ppermute(a, "tensor", tensor_move(0, 1, 0))


def core_swap(a):
    return lax.ppermute(a, "tensor", tensor_move(0, 0, 1))


def y_up(a):
    return lax.ppermute(a, "dp", dp_move(0, 1))


def y_down(a):
    return lax.ppermute(a, "dp", dp_move(0, -1))


def zz_swap(a):
    return lax.ppermute(a, "dp", dp_move(1, 0))


def tie_body(*refs):
    pass


def tie(value, *others):
    anywhere = pl.BlockSpec(memory_space=pl.ANY)
    return pl.pallas_call(
        tie_body,
        in_specs=[anywhere] * (1 + len(others)),
        out_specs=anywhere,
        out_shape=jax.ShapeDtypeStruct(value.shape, value.dtype),
        input_output_aliases={0: 0},
        compiler_params=pltpu.CompilerParams(),
        cost_estimate=pl.CostEstimate(flops=0, bytes_accessed=0, transcendentals=0),
        name="tie",
    )(value, *others)


def join_body(own, received, *outs):
    rows = own.shape[0]
    for out in outs:
        out[:rows, :], out[rows:, :] = own[...], received[...]


def join(own, received):
    rows, width = own.shape
    return call(join_body, vmem(2), vmem(1), [shape((2 * rows, width))], (own, received), "join")[0]


def x_pair(a):
    return lax.ppermute(a, "tensor", [(i, tensor_index(i // 4 ^ 1, i // 2 % 2, i % 2)) for i in range(16)])


def x_cross(a):
    return lax.ppermute(a, "tensor", [(i, tensor_index(3 - i // 4, i // 2 % 2, i % 2)) for i in range(16)])


def y_pair(a):
    return lax.ppermute(a, "dp", [(i, dp_index(i // 4, i % 4 ^ 1)) for i in range(8)])


def y_cross(a):
    return lax.ppermute(a, "dp", [(i, dp_index(i // 4, 3 - i % 4)) for i in range(8)])


def vmem(count):
    return [pl.BlockSpec(memory_space=pltpu.VMEM)] * count


def feature_blocks():
    d, t = lax.axis_index("dp"), lax.axis_index("tensor")
    zhi, y = d // 4, d % 4
    return [((zhi + j) % 2) * 4 + (y + o) % 4 for o in OFFSETS for j in range(2)] + [t % 2]


def row_blocks():
    t = lax.axis_index("tensor")
    x, zlo, core = t // 4, (t // 2) % 2, t % 2
    return [
        4 * ((x + o) % 4) + 2 * ((zlo + j) % 2) + (core + k) % 2
        for o in OFFSETS
        for j in range(2)
        for k in range(2)
    ]


def anywhere(count=1):
    return [pl.BlockSpec(memory_space=pl.ANY)] * count


def params(limit=LIMIT):
    return pltpu.CompilerParams(vmem_limit_bytes=limit * 1024 * 1024)


TIMES = dict(
    project=17, attn_fwd=10, branch_part=11, grad_in=17, attn_bwd=20, second_grad=60, gnormed_part=15, first_grad=40,
    adds=0, early_adds=0, finish=0, post_out=0, post_grad=0, pre=0, join=0,
)
FLOPS = 350_000_000
LARGE = ("pre", "early_adds", "project", "attn_fwd", "branch_part", "grad_in", "attn_bwd", "second_grad", "gnormed_part", "first_grad")


def call(body, in_specs, out_specs, out_shape, args, name, scratch=(), **kwargs):
    return pl.pallas_call(
        body,
        in_specs=in_specs,
        out_specs=out_specs,
        out_shape=out_shape,
        scratch_shapes=list(scratch),
        compiler_params=params(LIMIT if name in LARGE else 16),
        cost_estimate=pl.CostEstimate(flops=TIMES[name] * FLOPS + 1, bytes_accessed=1, transcendentals=0),
        name=name,
        **kwargs,
    )(*args)


def shape(dims, dtype=BF):
    return jax.ShapeDtypeStruct(dims, dtype)


class Copy:
    def __init__(self, src, dst, sem):
        self.copy, self.waited = pltpu.make_async_copy(src, dst, sem), False
        self.copy.start()

    def wait(self):
        if not self.waited:
            self.copy.wait()
        self.waited = True


def copier(sems):
    used = iter(range(sems.shape[0]))
    return lambda src, dst: Copy(src, dst, sems.at[next(used)])


def wait(copies):
    for copy in copies:
        copy.wait()


def adds_body(groups, count, *refs):
    sizes = [len(group) for group in groups]
    ins, outs, sems = refs[: sum(sizes)], refs[count : count + len(groups)], refs[-1]
    holds = refs[count + len(groups) : -1]
    start = copier(sems)
    rows = [r for group in groups for r in group]
    copies = [start(a.at[r, :] if isinstance(r, slice) else a, b) for a, r, b in zip(ins, rows, holds)]
    at = 0
    for size, out in zip(sizes, outs):
        wait(copies[at : at + size])
        total = holds[at][...].astype(F32)
        for k in range(at + 1, at + size):
            term = holds[k][...].astype(F32)
            if rows[k] == "top":
                term = jnp.where(lax.broadcasted_iota(jnp.int32, term.shape, 0) < 3, term, 0.0)
            total = total + term
        out[...] = total.astype(out.dtype)
        at += size


def adds(*groups, deps=(), name="adds"):
    groups = [[a if isinstance(a, tuple) else (a, None) for a in group] for group in groups]
    flat_groups = [a for group in groups for a in group]
    dims = [(r.stop - r.start if isinstance(r, slice) else a.shape[0], a.shape[1]) for a, r in flat_groups]
    rows = tuple(tuple(r for _, r in group) for group in groups)
    firsts = [sum(len(group) for group in groups[:k]) for k in range(len(groups))]
    return call(
        functools.partial(adds_body, rows, len(flat_groups) + len(deps)),
        anywhere(len(flat_groups) + len(deps)),
        vmem(len(groups)),
        [shape(dims[k], flat_groups[k][0].dtype) for k in firsts],
        (*(a for a, _ in flat_groups), *deps),
        name,
        [pltpu.VMEM(dim, a.dtype) for dim, (a, _) in zip(dims, flat_groups)]
        + [pltpu.SemaphoreType.DMA((len(flat_groups),))],
    )


def finish_first_body(a, b, c, d, attn_out, up_out, p0, p1, p2, p3, sems):
    start = copier(sems)
    wait([start(a, p0), start(b, p1), start(c.at[256:, :], p2), start(d, p3)])
    total = sum(p[...].astype(F32) for p in (p0, p1, p2, p3))
    by_head = [total[:, (2 * k + h) * 64 : (2 * k + h) * 64 + 64] for h in range(2) for k in range(3)]
    attn_out[...] = jnp.concatenate(by_head, axis=1)
    up_out[...] = total[:, 384:]


def finish_first(a, b, c, d, dep):
    return call(
        lambda a, b, c, d, dep, *refs: finish_first_body(a, b, c, d, *refs),
        anywhere(5),
        vmem(2),
        [shape((256, 384), F32), shape((256, 512), F32)],
        (a, b, c, d, dep),
        "finish",
        [pltpu.VMEM((256, 896), BF)] * 4 + [pltpu.SemaphoreType.DMA((4,))],
    )


def finish_second_body(a, b, c, d, vec, dep, dense_out, down_out, attn_bias, up_bias, p0, p1, p2, p3, sems):
    start = copier(sems)
    copies = [start(a, p0), start(b, p1), start(c.at[640:, :], p2), start(d, p3)]
    row = vec[3:4, :]
    by_head = [row[:, (2 * k + h) * 64 : (2 * k + h) * 64 + 64] for h in range(2) for k in range(3)]
    attn_bias[...] = jnp.concatenate(by_head, axis=1)
    up_bias[...] = row[:, 384:896]
    wait(copies)
    total = sum(p[...].astype(F32) for p in (p0, p1, p2, p3))
    dense_out[...], down_out[...] = total[:128, :], total[128:, :]


def finish_second(a, b, c, d, vec, dep):
    return call(
        finish_second_body,
        anywhere(4) + vmem(1) + anywhere(),
        vmem(4),
        [shape((128, 256), F32), shape((512, 256), F32), shape((1, 384), F32), shape((1, 512), F32)],
        (a, b, c, d, vec, dep),
        "finish",
        [pltpu.VMEM((640, 256), BF)] * 4 + [pltpu.SemaphoreType.DMA((4,))],
    )


def finish_vector_body(a, b, norm_bias, norm_gain, dep, out_bias, gain_out, bias_out):
    total = a[...] + b[...]
    out_bias[...] = total[0:1, :]
    bias_out[...] = total[1:2, :]
    gain_out[...] = (total[2:3, :] - norm_bias[...] * total[1:2, :]) / norm_gain[...]


def finish_vector(parts, norm_bias, norm_gain, dep):
    return call(
        finish_vector_body,
        vmem(4) + anywhere(),
        vmem(3),
        [shape((1, 2048), F32)] * 3,
        (*parts, norm_bias, norm_gain, dep),
        "finish",
    )


def pre_body(
    tok_in, cot_in, gain, bias, attn_in, up, dense, down,
    acts_out, acts_send, cotsum, first, second, tok, cot, attn, hold, sems,
):
    sc = feature_blocks()
    start = copier(sems)
    in_attn = start(attn_in, attn)
    in_tok = start(tok_in, tok)
    in_cot = start(cot_in, cot)
    rest = [start(up, first.at[:, 384:]), start(dense, second.at[:128, :]), start(down, second.at[128:, :])]
    by_kind = lambda a: jnp.concatenate(
        [a[:, (3 * h + k) * 64 : (3 * h + k) * 64 + 64] for k in range(3) for h in range(2)], axis=1
    )
    in_attn.wait()
    first[:, :384] = by_kind(attn[...])
    in_tok.wait()
    in_cot.wait()
    total = jnp.zeros(cotsum.shape, F32)
    for s in range(2):
        seq = sc[8] if s == 0 else 1 - sc[8]
        xin = tok[seq].astype(F32)
        centred = xin - jnp.mean(xin, axis=-1, keepdims=True)
        spread = jnp.mean(centred * centred, axis=-1, keepdims=True)
        hold[...] = (centred * lax.rsqrt(spread + EPS) * gain[...] + bias[...]).astype(BF)
        total = total + jnp.sum(cot[seq].astype(F32), axis=0, keepdims=True)
        for r in range(8):
            cols = pl.ds(pl.multiple_of(sc[r] * 256, 256), 256)
            to = slice(r * 256, (r + 1) * 256)
            (acts_out, acts_send)[s][:, to] = hold[:, cols]
    cotsum[...] = total
    wait(rest)


def pre(tok, cot, gain, bias, attn, *rest):
    rows, width = tok.shape[1:]
    return call(
        pre_body,
        anywhere(2) + vmem(2) + anywhere(4),
        vmem(5),
        [
            shape((rows, width)),
            shape((rows, width)),
            shape((1, width), F32),
            shape((256, 896)),
            shape((640, 256)),
        ],
        (tok, cot, gain, bias, attn, *rest),
        "pre",
        [pltpu.VMEM(tok.shape, BF), pltpu.VMEM(tok.shape, BF), pltpu.VMEM(attn.shape, BF)]
        + [pltpu.VMEM((rows, width), BF), pltpu.SemaphoreType.DMA((6,))],
    )


def own_rows(sc, parts, received, hold):
    for s in range(2):
        rows = sum(ref[...].astype(F32) for ref in parts) if s == 0 else received[...].astype(F32)
        for r in range(8):
            cols = pl.ds(pl.multiple_of(sc[r] * 256, 256), 256)
            hold[s, :, cols] = rows[:, r * 256 : (r + 1) * 256]


def post_out_body(tok, part, received, extra, out):
    sc = feature_blocks()
    for s in range(2):
        seq = sc[8] if s == 0 else 1 - sc[8]
        rows = (part[:64, :] if s == 0 else received[...]).astype(F32)
        out[seq] = (tok[seq].astype(F32) + rows + extra[...]).astype(BF)


def post_out(tok, part, received, extra):
    return call(
        post_out_body,
        vmem(4),
        pl.BlockSpec(memory_space=pltpu.VMEM),
        shape(tok.shape),
        (tok, part, received, extra),
        "post_out",
    )


def post_grad_body(tok_in, cot_in, a, b, c, d, received, gain, out, tok, cot, hold, p0, p1, p2, p3, p4, sems):
    sc = feature_blocks()
    start = copier(sems)
    ins = [start(ref.at[:64, :], p) for ref, p in zip((a, b, c.at[128:, :], d, received), (p0, p1, p2, p3, p4))]
    wait(ins + [start(tok_in, tok), start(cot_in, cot)])
    own_rows(sc, (p0, p1, p2, p3), p4, hold)
    for s in range(2):
        seq = sc[8] if s == 0 else 1 - sc[8]
        xin = tok[seq].astype(F32)
        centred = xin - jnp.mean(xin, axis=-1, keepdims=True)
        scale = lax.rsqrt(jnp.mean(centred * centred, axis=-1, keepdims=True) + EPS)
        xhat = centred * scale
        e = hold[s] * gain[...]
        mean_e = jnp.mean(e, axis=-1, keepdims=True)
        mean_x = jnp.mean(e * xhat, axis=-1, keepdims=True)
        out[seq] = cot[seq].astype(F32) + (e - mean_e - xhat * mean_x) * scale


def post_grad(tok, cot, parts, received, gain):
    rows = tok.shape[1:]
    return call(
        post_grad_body,
        anywhere(7) + vmem(1),
        pl.BlockSpec(memory_space=pltpu.VMEM),
        shape(tok.shape, F32),
        (tok, cot, *parts, received, gain),
        "post_grad",
        [pltpu.VMEM(tok.shape, BF)] * 2
        + [pltpu.VMEM(tok.shape, F32)]
        + [pltpu.VMEM(rows, BF)] * 5
        + [pltpu.SemaphoreType.DMA((7,))],
    )


def turn(u, cosine, sine_low, sine_high):
    return (
        u * cosine
        + pltpu.roll(u, u.shape[-1] - ROT // 2, 1) * sine_low
        + pltpu.roll(u, ROT // 2, 1) * sine_high
    )


def turn_back(u, cosine, sine_low, sine_high):
    return (
        u * cosine
        - pltpu.roll(u, u.shape[-1] - ROT // 2, 1) * sine_low
        - pltpu.roll(u, ROT // 2, 1) * sine_high
    )


def dot(a, b):
    return lax.dot_general(a, b, (((1,), (0,)), ((), ())), preferred_element_type=F32)


def dot_nt(a, b):
    return lax.dot_general(a, b, (((1,), (1,)), ((), ())), preferred_element_type=F32)


def dot_tn(a, b):
    return lax.dot_general(a, b, (((0,), (0,)), ((), ())), preferred_element_type=F32)


QB = 256


def diagonal(size):
    keys = lax.broadcasted_iota(jnp.int32, (size, size), 0)
    queries = lax.broadcasted_iota(jnp.int32, (size, size), 1)
    return keys <= queries


def attn_fwd_body(*refs):
    sc = row_blocks()
    dep, merged, lse, out_t, out_abs, q_in, k_in, v_in, sems = refs[6:]
    start = copier(sems)
    wait([start(refs[3 * h + k], held.at[h]) for h in range(2) for k, held in enumerate((q_in, k_in, v_in))])
    for h in range(2):
        attn_fwd_half(h, sc, merged, lse, out_t, out_abs, q_in, k_in, v_in)


def attn_fwd_half(h, sc, merged, lse, out_t, out_abs, q_in, k_in, v_in):
    keys = k_in[h]
    values_t = v_in[h].T
    lane = lax.broadcasted_iota(jnp.int32, (QB, 128), 1)
    allowed = diagonal(QB)
    for b in range(1024 // QB):
        begin, end = b * QB, (b + 1) * QB
        query = q_in[h, begin:end, :]
        for a in range(2):
            heads = slice(a * HEAD_DIM, (a + 1) * HEAD_DIM)
            only = jnp.where(lane // HEAD_DIM == a, query, jnp.zeros_like(query))
            scores = dot_nt(keys[:end], only)
            low = jnp.where(allowed, scores[begin:], -jnp.inf)
            top = jnp.max(low, axis=0, keepdims=True)
            if b > 0:
                top = jnp.maximum(top, jnp.max(scores[:begin], axis=0, keepdims=True))
            weights = jnp.exp(low - top)
            total = jnp.sum(weights, axis=0, keepdims=True)
            out = dot(values_t[:, begin:end], weights.astype(BF))
            if b > 0:
                weights = jnp.exp(scores[:begin] - top)
                total = total + jnp.sum(weights, axis=0, keepdims=True)
                out = out + dot(values_t[:, :begin], weights.astype(BF))
            out_t[heads, begin:end] = (out * (1.0 / total))[heads, :]
            lse[2 * h + a : 2 * h + a + 1, begin:end] = top + jnp.log(total)
    for r in range(1024 // 128):
        here = slice(128 * r, 128 * r + 128)
        out_abs[here, :] = out_t[:, here].T.astype(BF)
    for r in range(1024 // 64):
        there = pl.ds(pl.multiple_of(sc[r] * 64, 64), 64)
        merged[64 * r : 64 * r + 64, 128 * h : 128 * h + 128] = out_abs[there, :]


def attn_fwd(own, other, dep):
    length = own[0].shape[0]
    return call(
        attn_fwd_body,
        anywhere(7),
        vmem(2),
        [shape((length, 256)), shape((4, length), F32)],
        (*own, *other, dep),
        "attn_fwd",
        [pltpu.VMEM((128, length), F32), pltpu.VMEM((length, 128), BF)]
        + [pltpu.VMEM((2, length, 128), BF)] * 3
        + [pltpu.SemaphoreType.DMA((6,))],
    )


def attn_bwd_body(*refs):
    sc = row_blocks()
    lse, tables_in, (acts_in, gh_in, dep) = refs[8], refs[9:12], refs[12:15]
    outs, g1_out, colsum = refs[15:17], refs[17], refs[18]
    gqkv, gm_hold, dq_t, dq, dk, dv, q_in, k_in, v_in, gm_in = refs[19:29]
    tables, (acts, rhs, g1, sems) = refs[29:32], refs[32:]
    start = copier(sems)
    held = (gm_in, k_in, q_in, v_in)
    ins = [start(refs[4 * h + k], a.at[h]) for h in (1, 0) for k, a in enumerate(held)]
    ins += [start(a, b) for a, b in zip(tables_in, tables)]
    rest = [start(gh_in, rhs.at[:, 384:]), start(acts_in, acts)]
    wait(ins)
    copies = []
    for h in (1, 0):
        attn_bwd_half(h, sc, lse, *tables, gqkv, colsum, gm_hold, dq_t, dq, dk, dv, q_in, k_in, v_in, gm_in)
        copies.append(start(gqkv.at[h], outs[h]))
    wait(rest)
    rhs[:, :384] = gqkv[1]
    for rows in blocks_of(512, 4):
        g1[rows, :] = dot_tn(acts[:, rows], rhs[...]).astype(BF)
        copies.append(start(g1.at[rows, :], g1_out.at[rows, :]))
    wait(copies)


def attn_bwd_half(
    h, sc, lse, cos_t, low_t, high_t, gqkv, colsum, gm_hold, dq_t, dq, dk, dv, q_in, k_in, v_in, gm_in
):
    for r in range(1024 // 64):
        there = pl.ds(pl.multiple_of(sc[r] * 64, 64), 64)
        gm_hold[there, :] = gm_in[h, 64 * r : 64 * r + 64, :]
    keys = k_in[h]
    values = v_in[h]
    keys_t = keys.T
    lane = lax.broadcasted_iota(jnp.int32, (QB, 128), 1)
    allowed = diagonal(QB)
    for b in reversed(range(1024 // QB)):
        begin, end = b * QB, (b + 1) * QB
        query = q_in[h, begin:end, :]
        grad = gm_hold[begin:end, :]
        add_v, add_k = 0.0, 0.0
        for a in range(2):
            heads = slice(a * HEAD_DIM, (a + 1) * HEAD_DIM)
            mine = lane // HEAD_DIM == a
            only = jnp.where(mine, query, jnp.zeros_like(query))
            grad_only = jnp.where(mine, grad, jnp.zeros_like(grad))
            shift = lse[2 * h + a : 2 * h + a + 1, begin:end]
            scores = dot_nt(keys[:end], only)
            dprobs = dot_nt(values[:end], grad_only)
            low_p = jnp.where(allowed, jnp.exp(scores[begin:] - shift), 0.0)
            probs = low_p if b == 0 else jnp.concatenate([jnp.exp(scores[:begin] - shift), low_p], axis=0)
            delta = jnp.sum(probs * dprobs, axis=0, keepdims=True)
            gscores = (probs * (dprobs - delta)).astype(BF)
            add_v = add_v + dot(probs.astype(BF), grad_only)
            add_k = add_k + dot(gscores, only)
            dq_t[heads, begin:end] = dot(keys_t[:, :end], gscores)[heads, :]
        if end == 1024:
            dv[...], dk[...] = add_v, add_k
        else:
            dv[:end, :] += add_v
            dk[:end, :] += add_k
    for r in range(1024 // 128):
        here = slice(128 * r, 128 * r + 128)
        dq[here, :] = dq_t[:, here].T
    total = jnp.zeros((1, 384), F32)
    for r in range(1024 // 64):
        here = slice(64 * r, 64 * r + 64)
        there = pl.ds(pl.multiple_of(sc[r] * 64, 64), 64)
        tables = (cos_t[there, :], low_t[there, :], high_t[there, :])
        gq = turn_back(dq[there, :] * (HEAD_DIM**-0.5), *tables)
        gk = turn_back(dk[there, :], *tables)
        rows = jnp.concatenate([gq, gk, dv[there, :]], axis=1).astype(BF)
        gqkv[h, here, :] = rows
        total = total + jnp.sum(rows.astype(F32), axis=0, keepdims=True)
    colsum[h] = total


def attn_bwd(own, other, lse, gm_own, gm_other, tables, acts, gh_other, dep):
    length = gm_own.shape[0]
    ins = []
    for (q, k, v), gm in ((own, gm_own), (other, gm_other)):
        ins += [gm, k, q, v]
    return call(
        attn_bwd_body,
        anywhere(8) + vmem(1) + anywhere(6),
        anywhere(3) + vmem(1),
        [shape((length, 384))] * 2 + [shape((2048, 896)), shape((2, 1, 384), F32)],
        (*ins, lse, *tables, acts, gh_other, dep),
        "attn_bwd",
        [pltpu.VMEM((2, length, 384), BF), pltpu.VMEM((length, 128), BF), pltpu.VMEM((128, length), F32)]
        + [pltpu.VMEM((length, 128), F32)] * 3
        + [pltpu.VMEM((2, length, 128), BF)] * 4
        + [pltpu.VMEM((length, 128), F32)] * 3
        + [pltpu.VMEM((1024, 2048), BF), pltpu.VMEM((1024, 896), BF), pltpu.VMEM((2048, 896), BF)]
        + [pltpu.SemaphoreType.DMA((32,))],
    )


ROWS = 256
HUGE = (pltpu.SemaphoreType.DMA((176,)),)


def blocks_of(size=256, count=8):
    return [slice(size * r, size * r + size) for r in range(count)]


def message_places(outs, rows):
    up, down, own_a, own_z, left_z, right_a = outs
    one, two = slice(0, rows), slice(rows, 2 * rows)
    return [own_a, own_z, down.at[two, :], left_z, right_a, up.at[two, :], up.at[one, :], down.at[one, :]]


def flat(groups):
    return [copy for group in groups for copy in group]


def project_body(*refs):
    sc = row_blocks()
    pieces, w_own, w_other = refs[:8], refs[8:16], refs[16:24]
    b_own, b_other, tables_in = refs[24], refs[25], refs[26:29]
    acts_out, qkv_out = refs[29], refs[30:36]
    act_out, slope_out = refs[36:38], refs[38:40]
    acts, w, cos_t, low_t, high_t = refs[40:45]
    qkv, act, slope, sems = refs[45:51], refs[51:53], refs[53:55], refs[55]
    start = copier(sems)

    def tile(j):
        group = []
        for r, rows in enumerate(blocks_of()):
            if j < 6:
                cols = slice(256 * (j % 3), 256 * (j % 3) + 256)
                group.append(((w_own, w_other)[j // 3][r].at[:, cols], w.at[j, rows, :]))
            else:
                group.append((w_own[r].at[:, 768:], w.at[j, rows, :128]))
                group.append((w_other[r].at[:, 768:], w.at[j, rows, 128:]))
        return group

    def rows_in(m):
        return [(pieces[r], acts.at[128 * r : 128 * r + 128, :]) for r in (2 * m, 2 * m + 1)]

    def begin(group):
        return [start(a, b) for a, b in group]

    acts_in = [begin(rows_in(0))]
    w_in = [begin(tile(j)) for j in range(3)]
    rest = begin(zip(tables_in, (cos_t, low_t, high_t)))
    acts_in += [begin(rows_in(m)) for m in range(1, 4)]
    w_in += [begin(tile(j)) for j in range(3, 7)]
    root = (2.0 / np.pi) ** 0.5
    outs = []
    strips = [[(j // 3, 2 * (j % 3) + k) for k in range(2)] for j in range(6)] + [[(0, 6), (1, 6)]]
    steps = [(m, j) for m in range(4) for j in range(3)] + [(m, j) for m in range(4) for j in range(3, 7)]
    for m, j in steps:
        rows = slice(ROWS * m, ROWS * m + ROWS)
        if j == 0 and m == 0:
            wait(acts_in[0] + flat(w_in[:3]) + rest)
        if j == 0 and m == 1:
            wait(flat(acts_in[1:]))
            outs.append(start(acts, acts_out))
        if j == 3 and m == 0:
            wait(flat(w_in[3:]))
        result = dot(acts[rows, :], w[j])
        for k, (core, strip) in enumerate(strips[j]):
            cols = slice(128 * strip, 128 * strip + 128)
            h = result[:, 128 * k : 128 * k + 128] + (b_own, b_other)[core][:, cols]
            if strip < 3:
                for b in range(ROWS // 64):
                    there = pl.ds(pl.multiple_of(sc[4 * m + b] * 64, 64), 64)
                    u = h[64 * b : 64 * b + 64, :]
                    if strip < 2:
                        u = turn(u, cos_t[there, :], low_t[there, :], high_t[there, :])
                    if strip == 0:
                        u = u * (HEAD_DIM**-0.5)
                    qkv[3 * core + strip][there, :] = u.astype(BF)
                continue
            cols = slice(128 * (strip - 3), 128 * (strip - 3) + 128)
            square = h * h
            th = jnp.tanh(root * (h + 0.044715 * (square * h)))
            half = 0.5 + 0.5 * th
            act[core][rows, cols] = (h * half).astype(BF)
            slope[core][rows, cols] = (
                half + (0.5 * h) * (1.0 - th * th) * (root + (3 * 0.044715 * root) * square)
            ).astype(BF)
        if j == 6:
            for a, b in zip((*act, *slope), (*act_out, *slope_out)):
                outs.append(start(a.at[rows, :], b.at[rows, :]))
    for a, b in zip(qkv, qkv_out):
        outs.append(start(a, b))
    wait(outs)


def project(pieces, w_own, w_other, b_own, b_other, tables):
    small, wide, whole = (1024, 128), (1024, 512), (1024, 2048)
    return call(
        project_body,
        anywhere(24) + vmem(2) + anywhere(3),
        anywhere(11),
        [shape(whole)] + [shape(small)] * 6 + [shape(wide)] * 4,
        (*pieces, *w_own, *w_other, b_own, b_other, *tables),
        "project",
        [pltpu.VMEM(whole, BF), pltpu.VMEM((7, 2048, 256), BF)]
        + [pltpu.VMEM(small, F32)] * 3
        + [pltpu.VMEM(small, BF)] * 6
        + [pltpu.VMEM(wide, BF)] * 4
        + [*HUGE],
    )


def branch_body(merged, act_own, act_other, w_own, w_other, dep, out, lhs, w, stage, sems):
    sc = row_blocks()
    start = copier(sems)
    parts = ((merged.at[:, :128], 0, 128), (act_own, 128, 512), (merged.at[:, 128:], 640, 128), (act_other, 768, 512))
    lhs_in = [start(a, lhs.at[:, c : c + n]) for a, c, n in parts]
    w_in = [[start(w_own.at[r], w.at[r, :640, :]), start(w_other.at[r], w.at[r, 640:, :])] for r in range(8)]
    copies = []
    for half in (range(3), range(3, 8)):
        wait(lhs_in + flat(w_in[r] for r in half))
        for m in range(4):
            rows = slice(ROWS * m, ROWS * m + ROWS)
            for r in half:
                stage[rows, 256 * r : 256 * r + 256] = dot(lhs[rows, :], w[r]).astype(BF)
            if 7 in half:
                for p in (2 * m, 2 * m + 1):
                    to = pl.ds(pl.multiple_of(sc[2 * p] // 2 * 128, 128), 128)
                    copies.append(start(stage.at[128 * p : 128 * p + 128, :], out.at[to, :]))
    wait(copies)


def branch_part(merged, act_own, act_other, w_own, w_other, dep):
    return call(
        branch_body,
        anywhere(6),
        pl.BlockSpec(memory_space=pl.ANY),
        shape((1024, 2048)),
        (merged, act_own, act_other, w_own, w_other, dep),
        "branch_part",
        [pltpu.VMEM((1024, 1280), BF), pltpu.VMEM((8, 1280, 256), BF), pltpu.VMEM((1024, 2048), BF), *HUGE],
    )


def grad_in_body(cot, w_own, w_other, *refs):
    core, rows_sc = feature_blocks()[8], row_blocks()
    slope_in, (merged, act, dep) = refs[:2], refs[2:5]
    gout_out, gm_out, gh_out, g2_out, colsum = refs[5], refs[6:8], refs[8:10], refs[10], refs[11:13]
    gout, w, slope, gm, gh, lhs, stage, sems = refs[13], refs[14], refs[15:17], refs[17:19], refs[19:21], *refs[21:]
    start = copier(sems)

    def tile(j):
        copies = []
        for r, cols in enumerate(blocks_of()):
            for first, source, at in ((0, w_own, 256 * j), (640, w_other, 256 * j - 640)):
                lo, hi = max(at, 0), min(at + 256, 640)
                if lo < hi:
                    copies.append(start(source.at[r, lo:hi, :], w.at[lo + first : hi + first, cols]))
        return copies

    gout_in = [start(cot.at[rows_sc[r], core], gout.at[64 * r : 64 * r + 64, :]) for r in range(16)]
    w_in = [tile(0)]
    slope_copies = [start(a, b) for a, b in zip(slope_in, slope)]
    w_in += [tile(j) for j in range(1, 5)]
    lhs_in = [start(merged.at[:, 128:], lhs.at[:, :128]), start(act, lhs.at[:, 128:])]
    totals = [[jnp.zeros((1, 128), F32)] * 4 for _ in range(2)]
    copies = []
    for j in range(5):
        if j == 0:
            wait(gout_in + w_in[0] + slope_copies)
            copies.append(start(gout, gout_out))
        if j == 1:
            wait(flat(w_in) + lhs_in)
        for m in range(4):
            rows = slice(ROWS * m, ROWS * m + ROWS)
            result = dot_nt(gout[rows, :], w[256 * j : 256 * j + 256, :])
            for k in range(2):
                half, strip = (2 * j + k) // 5, (2 * j + k) % 5
                part = result[:, 128 * k : 128 * k + 128]
                if strip == 0:
                    gm[half][rows, :] = part.astype(BF)
                    continue
                cols = slice(128 * (strip - 1), 128 * strip)
                part = (part * slope[half][rows, cols].astype(F32)).astype(BF)
                gh[half][rows, cols] = part
                totals[half][strip - 1] += jnp.sum(part.astype(F32), axis=0, keepdims=True)
    for core in range(2):
        for strip in range(4):
            colsum[core][:, 128 * strip : 128 * strip + 128] = totals[core][strip]
    for a, b in zip((*gm, *gh), (*gm_out, *gh_out)):
        copies.append(start(a, b))
    for cols in blocks_of(512, 4):
        stage[:, cols] = dot_tn(lhs[...], gout[:, cols]).astype(BF)
        copies.append(start(stage.at[:, cols], g2_out.at[:, cols]))
    wait(copies)


def grad_in(cot, w_own, w_other, slope_own, slope_other, merged, act_other, dep):
    small, wide, whole = (1024, 128), (1024, 512), (1024, 2048)
    return call(
        grad_in_body,
        anywhere(8),
        anywhere(6) + vmem(2),
        [shape(whole)] + [shape(small)] * 2 + [shape(wide)] * 2 + [shape((640, 2048))] + [shape((1, 512), F32)] * 2,
        (cot, w_own, w_other, slope_own, slope_other, merged, act_other, dep),
        "grad_in",
        [pltpu.VMEM(whole, BF), pltpu.VMEM((1280, 2048), BF)]
        + [pltpu.VMEM(wide, BF)] * 2
        + [pltpu.VMEM(small, BF)] * 2
        + [pltpu.VMEM(wide, BF)] * 2
        + [pltpu.VMEM((1024, 640), BF), pltpu.VMEM((640, 2048), BF), *HUGE],
    )


def gnormed_body(q_own, gh_own, q_other, gh_other, acts_in, *refs):
    sc = feature_blocks()
    w_own, w_other, dep, cot_sum, attn_sums, up_own, up_other = refs[:8], refs[8:16], *refs[16:21]
    outs, vec_own, vec_send, (lhs, w, acts, stage, sems) = refs[21:27], refs[27], refs[28], refs[29:]
    places = message_places(outs, 128)
    start = copier(sems)
    parts = ((q_own, 0), (gh_own, 384), (q_other, 896), (gh_other, 1280))

    def rows_in(m):
        rows = slice(ROWS * m, ROWS * m + ROWS)
        copies = [start(a.at[rows, :], lhs.at[rows, c : c + a.shape[1]]) for a, c in parts]
        return copies + [start(acts_in.at[rows, :], acts.at[rows, :])]

    def tile(r):
        rows = slice(256 * r, 256 * r + 256)
        return [start(w_own[r], w.at[rows, :896]), start(w_other[r], w.at[rows, 896:])]

    lhs_in = {3: rows_in(3)}
    w_in = [tile(r) for r in range(8)]
    lhs_in.update({m: rows_in(m) for m in range(3)})
    totals = [[jnp.zeros((1, 256), F32)] * 8 for _ in range(2)]
    copies = []
    for m, first, last in ((3, 0, 3), (3, 3, 8), (0, 0, 8), (1, 0, 8), (2, 0, 8)):
        rows = slice(ROWS * m, ROWS * m + ROWS)
        if m == 3:
            wait(lhs_in[3] + flat(w_in[first:last]))
        if m == 0:
            wait(lhs_in[0] + lhs_in[1] + lhs_in[2])
        for r in range(first, last):
            cols = slice(256 * r, 256 * r + 256)
            result = dot_nt(lhs[rows, :], w[cols, :])
            totals[0][r] += jnp.sum(result, axis=0, keepdims=True)
            totals[1][r] += jnp.sum(result * acts[rows, cols].astype(F32), axis=0, keepdims=True)
            stage[rows, cols] = result.astype(BF)
        if last == 8:
            for p in (2 * m, 2 * m + 1):
                copies.append(start(stage.at[128 * p : 128 * p + 128, :], places[p]))
    for vec, half, up in ((vec_own, 0, up_own), (vec_send, 1, up_other)):
        vec[0:1, :] = cot_sum[...]
        for k in range(2):
            for r in range(8):
                vec[k + 1 : k + 2, pl.ds(pl.multiple_of(sc[r] * 256, 256), 256)] = totals[k][r]
        vec[3:4, :384], vec[3:4, 384:896] = attn_sums[half], up[...]
        vec[3:4, 896:] = jnp.zeros((1, 2048 - 896), F32)
    wait(copies)


def gnormed_part(q_own, gh_own, q_other, gh_other, acts, w_own, w_other, dep, *vectors):
    whole, piece = (1024, 2048), shape((128, 2048))
    *outs, vec_own, vec_send = call(
        gnormed_body,
        anywhere(22) + vmem(4),
        anywhere(6) + vmem(2),
        [shape((256, 2048))] * 2 + [piece] * 4 + [shape((4, 2048), F32)] * 2,
        (q_own, gh_own, q_other, gh_other, acts, *w_own, *w_other, dep, *vectors),
        "gnormed_part",
        [pltpu.VMEM((1024, 1792), BF), pltpu.VMEM((2048, 1792), BF), pltpu.VMEM(whole, BF), pltpu.VMEM(whole, BF), *HUGE],
    )
    return outs, vec_own, vec_send


def second_body(merged, act, gout, received, dep, *refs):
    sc = feature_blocks()
    places, (lhs, rhs, held, stage, sems) = message_places(refs[:6], 640), refs[6:]
    start = copier(sems)
    lhs_in = [start(merged.at[:, :128], lhs.at[:, :128]), start(act, lhs.at[:, 128:])]
    ins = []
    for r in range(8):
        cols = pl.ds(pl.multiple_of(sc[r] * 256, 256), 256)
        ins.append([start(gout.at[:, cols], rhs.at[r]), start(received.at[:, cols], held.at[r])])
    copies = []
    for r in range(8):
        if r == 0:
            wait(lhs_in + flat(ins[:3]))
        if r == 3:
            wait(flat(ins))
        result = dot_tn(lhs[...], rhs[r])
        stage[r] = (result + held[r].astype(F32)).astype(BF)
        copies.append(start(stage.at[r], places[r]))
    wait(copies)


def second_grad(merged, act, gout, received, dep):
    return call(
        second_body,
        anywhere(5),
        anywhere(6),
        [shape((1280, 256))] * 2 + [shape((640, 256))] * 4,
        (merged, act, gout, received, dep),
        "second_grad",
        [pltpu.VMEM((1024, 640), BF), pltpu.VMEM((8, 1024, 256), BF)]
        + [pltpu.VMEM((8, 640, 256), BF)] * 2
        + [*HUGE],
    )


def first_body(blocks, count, gqkv, gh, acts, received, *refs):
    outs, (lhs, rhs, held, stage, sems) = refs[count - 4 : -5], refs[-5:]
    places = [out.at[256 * k : 256 * k + 256, :] for out in outs for k in range(out.shape[0] // 256)]
    start = copier(sems)
    rhs_in = [start(gqkv, rhs.at[:, :384]), start(gh, rhs.at[:, 384:])]
    ins = []
    for k, r in enumerate(blocks):
        rows = slice(256 * r, 256 * r + 256)
        ins.append([start(acts.at[:, rows], lhs.at[k]), start(received.at[rows, :], held.at[k])])
    copies = []
    for k in range(4):
        if k == 0:
            wait(rhs_in + ins[0])
        if k == 1:
            wait(flat(ins))
        result = dot_tn(lhs[k], rhs[...])
        stage[k] = (result + held[k].astype(F32)).astype(BF)
        copies.append(start(stage.at[k], places[k]))
    wait(copies)


def first_grad(blocks, rows, *args):
    return call(
        functools.partial(first_body, blocks, len(args)),
        anywhere(len(args)),
        anywhere(1024 // rows),
        [shape((rows, 896))] * (1024 // rows),
        args,
        "first_grad",
        [pltpu.VMEM((4, 1024, 256), BF), pltpu.VMEM((1024, 896), BF)]
        + [pltpu.VMEM((4, 256, 896), BF)] * 2
        + [*HUGE],
    )


def rotary_tables(length):
    frequency = np.float32(10000.0) ** (-(np.arange(ROT // 2, dtype=np.float32) * 2.0 / ROT))
    angles = np.arange(length, dtype=np.float32)[:, None] * frequency.astype(np.float32)[None, :]
    cosine, sine = np.cos(angles), np.sin(angles)
    one = np.ones((length, HEAD_DIM - ROT), np.float32)
    zero_half, zero = np.zeros_like(sine), np.zeros_like(one)
    cos_t = np.concatenate([cosine, cosine, one] * 2, axis=1)
    low_t = np.concatenate([-sine, zero_half, zero] * 2, axis=1)
    high_t = np.concatenate([zero_half, sine, zero] * 2, axis=1)
    return tuple(jnp.asarray(a, F32) for a in (cos_t, low_t, high_t))


def by_kind(a):
    return jnp.swapaxes(a.reshape(2, 3, HEAD_DIM), 0, 1).reshape(384)


def shards(
    tokens,
    attn_weight,
    attn_bias,
    dense_weight,
    dense_bias,
    up_weight,
    up_bias,
    down_weight,
    down_bias,
    norm_gain,
    norm_bias,
    cotangent,
):
    tables = rotary_tables(16 * tokens.shape[1])
    gain_row, bias_row = norm_gain[None, :], norm_bias[None, :]

    cot = lax.all_gather(cotangent, "tensor", axis=0)
    acts_own, acts_send, cot_sum, f0, s0 = pre(
        tokens, cotangent, gain_row, bias_row, attn_weight, up_weight, dense_weight, down_weight
    )
    swapped = core_swap(acts_send)
    f1, f2, f4, f0x = zz_swap(f0), y_up(f0), y_down(f0), core_swap(f0)
    s_own = lax.all_gather(s0, "dp", axis=0)
    a0 = join(acts_own, swapped)
    a2, a4, a1 = x_up(a0), x_down(a0), z_swap(a0)
    f1 = tie(f1, f2, f4, a0)
    f3, f5, f1x = y_up(f1), y_down(f1), core_swap(f1)
    f2 = tie(f2, f1)
    f6, f2x, f4x = y_up(f2), core_swap(f2), core_swap(f4)
    a2 = tie(a2, a4, f2)
    a6 = x_up(a2)
    a1 = tie(a1, a2, f3, f5)
    a3, a5 = x_up(a1), x_down(a1)
    f5 = tie(f5, a1)
    f7, f5x = y_down(f5), core_swap(f5)
    a5 = tie(a5, f6)
    a7 = x_down(a5)
    f3 = tie(f3, a5, a6)
    f3x = core_swap(f3)
    f6 = tie(f6, f7, a3, f3)
    f6x, f7x = core_swap(f6), core_swap(f7)
    biases = tie(jnp.concatenate([by_kind(attn_bias), up_bias])[None, :], f1)
    other_biases = core_swap(biases)
    f_own, f_other = [f0, f1, f2, f3, f4, f5, f6, f7], [f0x, f1x, f2x, f3x, f4x, f5x, f6x, f7x]

    acts, *rest = project([a0, a1, a2, a3, a4, a5, a6, a7], f_own, f_other, biases, other_biases, tables)
    qkv_own, qkv_other, (act_own, act_other), (slope_own, slope_other) = rest[:3], rest[3:6], rest[6:8], rest[8:]
    merged, lse = attn_fwd(qkv_own, qkv_other, acts)
    s_own = tie(s_own, acts)
    s_other = core_swap(s_own)
    br = branch_part(merged, act_own, act_other, s_own, s_other, acts)
    group = [[2 * p + c for p in range(8)] for c in range(2)]
    br_sum = lax.psum_scatter(br, "tensor", scatter_dimension=0, axis_index_groups=group, tiled=True)

    gout, gm_own, gm_other, gh_own, gh_other, g2_other, up_sum_own, up_sum_other = grad_in(
        cot, s_own, s_other, slope_own, slope_other, merged, act_other, br
    )
    g2_received = core_swap(g2_other)
    gq_own, gq_other, g1_other, attn_sums = attn_bwd(
        qkv_own, qkv_other, lse, gm_own, gm_other, tables, acts, gh_other, gout
    )
    g1_received = core_swap(g1_other)
    g2_up, g2_down, g2_0, g2_1, g2_3, g2_4 = second_grad(merged, act_own, gout, g2_received, gq_own)
    g2_u, g2_d = y_up(g2_up), y_down(g2_down)
    (gn_up, gn_down, gn_0, gn_1, gn_3, gn_4), vec, vec_send = gnormed_part(
        gq_own, gh_own, gq_other, gh_other, acts, f_own, f_other, g2_0, cot_sum, attn_sums, up_sum_own, up_sum_other
    )
    gn_u, gn_d = x_up(gn_up), x_down(gn_down)
    step = core_swap(vec_send)

    n_one, n_two, m_one, m_two = slice(0, 128), slice(128, 256), slice(0, 256), slice(256, 512)
    one, two, last = slice(0, 640), slice(640, 1280), slice(64, 128)
    vec, g2_4, g2_3 = adds((vec, step), (g2_4, (g2_u, one)), (g2_3, (g2_d, one)), deps=(gn_0,), name="early_adds")
    step = zz_swap(vec)
    g2_ua, g2_dz = y_up(g2_4), y_down(g2_3)
    g1_up, g1_down = first_grad((6, 5, 7, 2), 512, gq_own, gh_own, acts, g1_received, g2_4)
    g1_u, g1_d = y_up(g1_up), y_down(g1_down)
    (vec,) = adds((vec, step), deps=(g1_up, g2_ua, g2_dz))
    step = z_swap(vec)
    g1_0, g1_1, g1_3, g1_4 = first_grad((0, 1, 3, 4), 256, gq_own, gh_own, acts, g1_received, vec)
    br_sum = tie(br_sum, g1_0)
    br_received = core_swap(br_sum[64:])
    layer_out = post_out(tokens, br_sum, br_received, (dense_bias + down_bias)[None, :])
    gn_4, gn_3, vec, g2_1 = adds(
        (gn_4, (gn_u, n_one)),
        (gn_3, (gn_d, n_one)),
        (vec, (step, "top")),
        (g2_1, (g2_u, two), g2_dz),
        deps=(layer_out,),
        name="early_adds",
    )
    gn_ua, gn_dz = x_up(gn_4), x_down(gn_3)
    step, g2_z = y_pair(vec), zz_swap(g2_1)
    g1_4, g1_3, vec = adds((g1_4, (g1_u, m_one)), (g1_3, (g1_d, m_one)), (vec, step), deps=(gn_4,))
    g1_ua, g1_dz = y_up(g1_4), y_down(g1_3)
    step = y_cross(vec)
    (gn_1,) = adds((gn_1, (gn_u, n_two), gn_dz), deps=(g1_4, gn_ua, g2_z))
    gn_z = z_swap(gn_1)
    g1_1, vec = adds((g1_1, (g1_u, m_two), g1_dz), (vec, step), deps=(gn_1, g1_ua))
    g1_z = zz_swap(g1_1)
    step = x_pair(vec)
    dense_grad, down_grad, attn_bias_grad, up_bias_grad = finish_second(g2_0, g2_ua, g2_d, g2_z, vec, vec)
    gn_send, vec = adds(
        ((gn_0, last), (gn_ua, last), (gn_d, slice(192, 256)), (gn_z, last)), (vec, (step, "top")), deps=(dense_grad,)
    )
    gn_received, step = core_swap(gn_send), x_cross(vec)
    grad_tokens = post_grad(tokens, cotangent, (gn_0, gn_ua, gn_d, gn_z), gn_received, gain_row)
    out_bias_grad, norm_gain_grad, norm_bias_grad = finish_vector(
        (vec, step), norm_bias[None, :], norm_gain[None, :], grad_tokens
    )
    attn_grad, up_grad = finish_first(g1_0, g1_ua, g1_d, g1_z, out_bias_grad)
    out_bias_grad = out_bias_grad[0]
    return (
        layer_out,
        grad_tokens,
        attn_grad,
        attn_bias_grad[0],
        dense_grad,
        out_bias_grad,
        up_grad,
        up_bias_grad[0],
        down_grad,
        out_bias_grad,
        norm_gain_grad[0],
        norm_bias_grad[0],
    )


def solution(mesh):
    in_specs = (
        P("dp", "tensor", None),
        P("dp", "tensor"),
        P("tensor"),
        P("tensor", "dp"),
        P(),
        P("dp", "tensor"),
        P("tensor"),
        P("tensor", "dp"),
        P(),
        P(),
        P(),
        P("dp", "tensor", None),
    )
    out_specs = (
        P("dp", "tensor", None),
        P("dp", "tensor", None),
        P("dp", "tensor"),
        P("tensor"),
        P("tensor", "dp"),
        P(),
        P("dp", "tensor"),
        P("tensor"),
        P("tensor", "dp"),
        P(),
        P(),
        P(),
    )
    return jax.shard_map(shards, mesh=mesh, in_specs=in_specs, out_specs=out_specs, check_vma=False)
```

```python
import functools

import jax
import jax.numpy as jnp
import numpy as np
from jax import lax
from jax.experimental import pallas as pl
from jax.experimental.pallas import tpu as pltpu
from jax.sharding import PartitionSpec as P

HEAD_DIM = 64
ROT = 32
EPS = 1e-05
BF = jnp.bfloat16
LIMIT = 60
F32 = jnp.float32

OFFSETS = (0, -1, 1, 2)


def tensor_index(x, zlo, core):
    return (x % 4) * 4 + (zlo % 2) * 2 + core % 2


def dp_index(zhi, y):
    return (zhi % 2) * 4 + y % 4


def tensor_move(dx, dz, dc):
    return [
        (tensor_index(x, z, c), tensor_index(x + dx, z + dz, c + dc))
        for x in range(4)
        for z in range(2)
        for c in range(2)
    ]


def dp_move(dz, dy):
    return [(dp_index(z, y), dp_index(z + dz, y + dy)) for z in range(2) for y in range(4)]


def x_up(a):
    return lax.ppermute(a, "tensor", tensor_move(1, 0, 0))


def x_down(a):
    return lax.ppermute(a, "tensor", tensor_move(-1, 0, 0))


def z_swap(a):
    return lax.ppermute(a, "tensor", tensor_move(0, 1, 0))


def core_swap(a):
    return lax.ppermute(a, "tensor", tensor_move(0, 0, 1))


def y_up(a):
    return lax.ppermute(a, "dp", dp_move(0, 1))


def y_down(a):
    return lax.ppermute(a, "dp", dp_move(0, -1))


def zz_swap(a):
    return lax.ppermute(a, "dp", dp_move(1, 0))


def tie_body(*refs):
    pass


def tie(value, *others):
    anywhere = pl.BlockSpec(memory_space=pl.ANY)
    return pl.pallas_call(
        tie_body,
        in_specs=[anywhere] * (1 + len(others)),
        out_specs=anywhere,
        out_shape=jax.ShapeDtypeStruct(value.shape, value.dtype),
        input_output_aliases={0: 0},
        compiler_params=pltpu.CompilerParams(),
        cost_estimate=pl.CostEstimate(flops=0, bytes_accessed=0, transcendentals=0),
        name="tie",
    )(value, *others)


def join_body(own, received, *outs):
    rows = own.shape[0]
    for out in outs:
        out[:rows, :], out[rows:, :] = own[...], received[...]


def join(own, received):
    rows, width = own.shape
    return call(join_body, vmem(2), vmem(1), [shape((2 * rows, width))], (own, received), "join")[0]


def x_pair(a):
    return lax.ppermute(a, "tensor", [(i, tensor_index(i // 4 ^ 1, i // 2 % 2, i % 2)) for i in range(16)])


def x_cross(a):
    return lax.ppermute(a, "tensor", [(i, tensor_index(3 - i // 4, i // 2 % 2, i % 2)) for i in range(16)])


def y_pair(a):
    return lax.ppermute(a, "dp", [(i, dp_index(i // 4, i % 4 ^ 1)) for i in range(8)])


def y_cross(a):
    return lax.ppermute(a, "dp", [(i, dp_index(i // 4, 3 - i % 4)) for i in range(8)])


def vmem(count):
    return [pl.BlockSpec(memory_space=pltpu.VMEM)] * count


def feature_blocks():
    d, t = lax.axis_index("dp"), lax.axis_index("tensor")
    zhi, y = d // 4, d % 4
    return [((zhi + j) % 2) * 4 + (y + o) % 4 for o in OFFSETS for j in range(2)] + [t % 2]


def row_blocks():
    t = lax.axis_index("tensor")
    x, zlo, core = t // 4, (t // 2) % 2, t % 2
    return [
        4 * ((x + o) % 4) + 2 * ((zlo + j) % 2) + (core + k) % 2
        for o in OFFSETS
        for j in range(2)
        for k in range(2)
    ]


def anywhere(count=1):
    return [pl.BlockSpec(memory_space=pl.ANY)] * count


def params(limit=LIMIT):
    return pltpu.CompilerParams(vmem_limit_bytes=limit * 1024 * 1024)


TIMES = dict(
    project=17, attn_fwd=10, branch_part=11, grad_in=17, attn_bwd=20, second_grad=60, gnormed_part=15, first_grad=40,
    adds=0, early_adds=0, finish=0, post_out=0, post_grad=0, pre=0, join=0,
)
FLOPS = 200_000_000
LARGE = ("pre", "early_adds", "project", "attn_fwd", "branch_part", "grad_in", "attn_bwd", "second_grad", "gnormed_part", "first_grad")


def call(body, in_specs, out_specs, out_shape, args, name, scratch=(), **kwargs):
    return pl.pallas_call(
        body,
        in_specs=in_specs,
        out_specs=out_specs,
        out_shape=out_shape,
        scratch_shapes=list(scratch),
        compiler_params=params(LIMIT if name in LARGE else 16),
        cost_estimate=pl.CostEstimate(flops=TIMES[name] * FLOPS + 1, bytes_accessed=1, transcendentals=0),
        name=name,
        **kwargs,
    )(*args)


def shape(dims, dtype=BF):
    return jax.ShapeDtypeStruct(dims, dtype)


class Copy:
    def __init__(self, src, dst, sem):
        self.copy, self.waited = pltpu.make_async_copy(src, dst, sem), False
        self.copy.start()

    def wait(self):
        if not self.waited:
            self.copy.wait()
        self.waited = True


def copier(sems):
    used = iter(range(sems.shape[0]))
    return lambda src, dst: Copy(src, dst, sems.at[next(used)])


def wait(copies):
    for copy in copies:
        copy.wait()


def adds_body(groups, count, *refs):
    sizes = [len(group) for group in groups]
    ins, outs, sems = refs[: sum(sizes)], refs[count : count + len(groups)], refs[-1]
    holds = refs[count + len(groups) : -1]
    start = copier(sems)
    rows = [r for group in groups for r in group]
    copies = [start(a.at[r, :] if isinstance(r, slice) else a, b) for a, r, b in zip(ins, rows, holds)]
    at = 0
    for size, out in zip(sizes, outs):
        wait(copies[at : at + size])
        total = holds[at][...].astype(F32)
        for k in range(at + 1, at + size):
            term = holds[k][...].astype(F32)
            if rows[k] == "top":
                term = jnp.where(lax.broadcasted_iota(jnp.int32, term.shape, 0) < 3, term, 0.0)
            total = total + term
        out[...] = total.astype(out.dtype)
        at += size


def adds(*groups, deps=(), name="adds"):
    groups = [[a if isinstance(a, tuple) else (a, None) for a in group] for group in groups]
    flat_groups = [a for group in groups for a in group]
    dims = [(r.stop - r.start if isinstance(r, slice) else a.shape[0], a.shape[1]) for a, r in flat_groups]
    rows = tuple(tuple(r for _, r in group) for group in groups)
    firsts = [sum(len(group) for group in groups[:k]) for k in range(len(groups))]
    return call(
        functools.partial(adds_body, rows, len(flat_groups) + len(deps)),
        anywhere(len(flat_groups) + len(deps)),
        vmem(len(groups)),
        [shape(dims[k], flat_groups[k][0].dtype) for k in firsts],
        (*(a for a, _ in flat_groups), *deps),
        name,
        [pltpu.VMEM(dim, a.dtype) for dim, (a, _) in zip(dims, flat_groups)]
        + [pltpu.SemaphoreType.DMA((len(flat_groups),))],
    )


def finish_first_body(a, b, c, d, attn_out, up_out, p0, p1, p2, p3, sems):
    start = copier(sems)
    wait([start(a, p0), start(b, p1), start(c.at[256:, :], p2), start(d, p3)])
    total = sum(p[...].astype(F32) for p in (p0, p1, p2, p3))
    by_head = [total[:, (2 * k + h) * 64 : (2 * k + h) * 64 + 64] for h in range(2) for k in range(3)]
    attn_out[...] = jnp.concatenate(by_head, axis=1)
    up_out[...] = total[:, 384:]


def finish_first(a, b, c, d, dep):
    return call(
        lambda a, b, c, d, dep, *refs: finish_first_body(a, b, c, d, *refs),
        anywhere(5),
        vmem(2),
        [shape((256, 384), F32), shape((256, 512), F32)],
        (a, b, c, d, dep),
        "finish",
        [pltpu.VMEM((256, 896), BF)] * 4 + [pltpu.SemaphoreType.DMA((4,))],
    )


def finish_second_body(a, b, c, d, vec, dep, dense_out, down_out, attn_bias, up_bias, p0, p1, p2, p3, sems):
    start = copier(sems)
    copies = [start(a, p0), start(b, p1), start(c.at[640:, :], p2), start(d, p3)]
    row = vec[3:4, :]
    by_head = [row[:, (2 * k + h) * 64 : (2 * k + h) * 64 + 64] for h in range(2) for k in range(3)]
    attn_bias[...] = jnp.concatenate(by_head, axis=1)
    up_bias[...] = row[:, 384:896]
    wait(copies)
    total = sum(p[...].astype(F32) for p in (p0, p1, p2, p3))
    dense_out[...], down_out[...] = total[:128, :], total[128:, :]


def finish_second(a, b, c, d, vec, dep):
    return call(
        finish_second_body,
        anywhere(4) + vmem(1) + anywhere(),
        vmem(4),
        [shape((128, 256), F32), shape((512, 256), F32), shape((1, 384), F32), shape((1, 512), F32)],
        (a, b, c, d, vec, dep),
        "finish",
        [pltpu.VMEM((640, 256), BF)] * 4 + [pltpu.SemaphoreType.DMA((4,))],
    )


def finish_vector_body(a, b, norm_bias, norm_gain, dep, out_bias, gain_out, bias_out):
    total = a[...] + b[...]
    out_bias[...] = total[0:1, :]
    bias_out[...] = total[1:2, :]
    gain_out[...] = (total[2:3, :] - norm_bias[...] * total[1:2, :]) / norm_gain[...]


def finish_vector(parts, norm_bias, norm_gain, dep):
    return call(
        finish_vector_body,
        vmem(4) + anywhere(),
        vmem(3),
        [shape((1, 2048), F32)] * 3,
        (*parts, norm_bias, norm_gain, dep),
        "finish",
    )


def pre_body(
    tok_in, cot_in, gain, bias, attn_in, up, dense, down,
    acts_out, acts_send, cotsum, first, second, tok, cot, attn, hold, sems,
):
    sc = feature_blocks()
    start = copier(sems)
    in_attn = start(attn_in, attn)
    in_tok = start(tok_in, tok)
    in_cot = start(cot_in, cot)
    rest = [start(up, first.at[:, 384:]), start(dense, second.at[:128, :]), start(down, second.at[128:, :])]
    by_kind = lambda a: jnp.concatenate(
        [a[:, (3 * h + k) * 64 : (3 * h + k) * 64 + 64] for k in range(3) for h in range(2)], axis=1
    )
    in_attn.wait()
    first[:, :384] = by_kind(attn[...])
    in_tok.wait()
    in_cot.wait()
    total = jnp.zeros(cotsum.shape, F32)
    for s in range(2):
        seq = sc[8] if s == 0 else 1 - sc[8]
        xin = tok[seq].astype(F32)
        centred = xin - jnp.mean(xin, axis=-1, keepdims=True)
        spread = jnp.mean(centred * centred, axis=-1, keepdims=True)
        hold[...] = (centred * lax.rsqrt(spread + EPS) * gain[...] + bias[...]).astype(BF)
        total = total + jnp.sum(cot[seq].astype(F32), axis=0, keepdims=True)
        for r in range(8):
            cols = pl.ds(pl.multiple_of(sc[r] * 256, 256), 256)
            to = slice(r * 256, (r + 1) * 256)
            (acts_out, acts_send)[s][:, to] = hold[:, cols]
    cotsum[...] = total
    wait(rest)


def pre(tok, cot, gain, bias, attn, *rest):
    rows, width = tok.shape[1:]
    return call(
        pre_body,
        anywhere(2) + vmem(2) + anywhere(4),
        vmem(5),
        [
            shape((rows, width)),
            shape((rows, width)),
            shape((1, width), F32),
            shape((256, 896)),
            shape((640, 256)),
        ],
        (tok, cot, gain, bias, attn, *rest),
        "pre",
        [pltpu.VMEM(tok.shape, BF), pltpu.VMEM(tok.shape, BF), pltpu.VMEM(attn.shape, BF)]
        + [pltpu.VMEM((rows, width), BF), pltpu.SemaphoreType.DMA((6,))],
    )


def own_rows(sc, parts, received, hold):
    for s in range(2):
        rows = sum(ref[...].astype(F32) for ref in parts) if s == 0 else received[...].astype(F32)
        for r in range(8):
            cols = pl.ds(pl.multiple_of(sc[r] * 256, 256), 256)
            hold[s, :, cols] = rows[:, r * 256 : (r + 1) * 256]


def post_out_body(tok, part, received, extra, out):
    sc = feature_blocks()
    for s in range(2):
        seq = sc[8] if s == 0 else 1 - sc[8]
        rows = (part[:64, :] if s == 0 else received[...]).astype(F32)
        out[seq] = (tok[seq].astype(F32) + rows + extra[...]).astype(BF)


def post_out(tok, part, received, extra):
    return call(
        post_out_body,
        vmem(4),
        pl.BlockSpec(memory_space=pltpu.VMEM),
        shape(tok.shape),
        (tok, part, received, extra),
        "post_out",
    )


def post_grad_body(tok_in, cot_in, a, b, c, d, received, gain, out, tok, cot, hold, p0, p1, p2, p3, p4, sems):
    sc = feature_blocks()
    start = copier(sems)
    ins = [start(ref.at[:64, :], p) for ref, p in zip((a, b, c.at[128:, :], d, received), (p0, p1, p2, p3, p4))]
    wait(ins + [start(tok_in, tok), start(cot_in, cot)])
    own_rows(sc, (p0, p1, p2, p3), p4, hold)
    for s in range(2):
        seq = sc[8] if s == 0 else 1 - sc[8]
        xin = tok[seq].astype(F32)
        centred = xin - jnp.mean(xin, axis=-1, keepdims=True)
        scale = lax.rsqrt(jnp.mean(centred * centred, axis=-1, keepdims=True) + EPS)
        xhat = centred * scale
        e = hold[s] * gain[...]
        mean_e = jnp.mean(e, axis=-1, keepdims=True)
        mean_x = jnp.mean(e * xhat, axis=-1, keepdims=True)
        out[seq] = cot[seq].astype(F32) + (e - mean_e - xhat * mean_x) * scale


def post_grad(tok, cot, parts, received, gain):
    rows = tok.shape[1:]
    return call(
        post_grad_body,
        anywhere(7) + vmem(1),
        pl.BlockSpec(memory_space=pltpu.VMEM),
        shape(tok.shape, F32),
        (tok, cot, *parts, received, gain),
        "post_grad",
        [pltpu.VMEM(tok.shape, BF)] * 2
        + [pltpu.VMEM(tok.shape, F32)]
        + [pltpu.VMEM(rows, BF)] * 5
        + [pltpu.SemaphoreType.DMA((7,))],
    )


def turn(u, cosine, sine_low, sine_high):
    return (
        u * cosine
        + pltpu.roll(u, u.shape[-1] - ROT // 2, 1) * sine_low
        + pltpu.roll(u, ROT // 2, 1) * sine_high
    )


def turn_back(u, cosine, sine_low, sine_high):
    return (
        u * cosine
        - pltpu.roll(u, u.shape[-1] - ROT // 2, 1) * sine_low
        - pltpu.roll(u, ROT // 2, 1) * sine_high
    )


def dot(a, b):
    return lax.dot_general(a, b, (((1,), (0,)), ((), ())), preferred_element_type=F32)


def dot_nt(a, b):
    return lax.dot_general(a, b, (((1,), (1,)), ((), ())), preferred_element_type=F32)


def dot_tn(a, b):
    return lax.dot_general(a, b, (((0,), (0,)), ((), ())), preferred_element_type=F32)


QB = 256


def diagonal(size):
    keys = lax.broadcasted_iota(jnp.int32, (size, size), 0)
    queries = lax.broadcasted_iota(jnp.int32, (size, size), 1)
    return keys <= queries


def attn_fwd_body(*refs):
    sc = row_blocks()
    dep, merged, lse, out_t, out_abs, q_in, k_in, v_in, sems = refs[6:]
    start = copier(sems)
    wait([start(refs[3 * h + k], held.at[h]) for h in range(2) for k, held in enumerate((q_in, k_in, v_in))])
    for h in range(2):
        attn_fwd_half(h, sc, merged, lse, out_t, out_abs, q_in, k_in, v_in)


def attn_fwd_half(h, sc, merged, lse, out_t, out_abs, q_in, k_in, v_in):
    keys = k_in[h]
    values_t = v_in[h].T
    lane = lax.broadcasted_iota(jnp.int32, (QB, 128), 1)
    allowed = diagonal(QB)
    for b in range(1024 // QB):
        begin, end = b * QB, (b + 1) * QB
        query = q_in[h, begin:end, :]
        for a in range(2):
            heads = slice(a * HEAD_DIM, (a + 1) * HEAD_DIM)
            only = jnp.where(lane // HEAD_DIM == a, query, jnp.zeros_like(query))
            scores = dot_nt(keys[:end], only)
            low = jnp.where(allowed, scores[begin:], -jnp.inf)
            top = jnp.max(low, axis=0, keepdims=True)
            if b > 0:
                top = jnp.maximum(top, jnp.max(scores[:begin], axis=0, keepdims=True))
            weights = jnp.exp(low - top)
            total = jnp.sum(weights, axis=0, keepdims=True)
            out = dot(values_t[:, begin:end], weights.astype(BF))
            if b > 0:
                weights = jnp.exp(scores[:begin] - top)
                total = total + jnp.sum(weights, axis=0, keepdims=True)
                out = out + dot(values_t[:, :begin], weights.astype(BF))
            out_t[heads, begin:end] = (out * (1.0 / total))[heads, :]
            lse[2 * h + a : 2 * h + a + 1, begin:end] = top + jnp.log(total)
    for r in range(1024 // 128):
        here = slice(128 * r, 128 * r + 128)
        out_abs[here, :] = out_t[:, here].T.astype(BF)
    for r in range(1024 // 64):
        there = pl.ds(pl.multiple_of(sc[r] * 64, 64), 64)
        merged[64 * r : 64 * r + 64, 128 * h : 128 * h + 128] = out_abs[there, :]


def attn_fwd(own, other, dep):
    length = own[0].shape[0]
    return call(
        attn_fwd_body,
        anywhere(7),
        vmem(2),
        [shape((length, 256)), shape((4, length), F32)],
        (*own, *other, dep),
        "attn_fwd",
        [pltpu.VMEM((128, length), F32), pltpu.VMEM((length, 128), BF)]
        + [pltpu.VMEM((2, length, 128), BF)] * 3
        + [pltpu.SemaphoreType.DMA((6,))],
    )


def attn_bwd_body(*refs):
    sc = row_blocks()
    lse, tables_in, (acts_in, gh_in, dep) = refs[8], refs[9:12], refs[12:15]
    outs, g1_out, colsum = refs[15:17], refs[17], refs[18]
    gqkv, gm_hold, dq_t, dq, dk, dv, q_in, k_in, v_in, gm_in = refs[19:29]
    tables, (acts, rhs, g1, sems) = refs[29:32], refs[32:]
    start = copier(sems)
    held = (gm_in, k_in, q_in, v_in)
    ins = [start(refs[4 * h + k], a.at[h]) for h in (1, 0) for k, a in enumerate(held)]
    ins += [start(a, b) for a, b in zip(tables_in, tables)]
    rest = [start(gh_in, rhs.at[:, 384:]), start(acts_in, acts)]
    wait(ins)
    copies = []
    for h in (1, 0):
        attn_bwd_half(h, sc, lse, *tables, gqkv, colsum, gm_hold, dq_t, dq, dk, dv, q_in, k_in, v_in, gm_in)
        copies.append(start(gqkv.at[h], outs[h]))
    wait(rest)
    rhs[:, :384] = gqkv[1]
    for rows in blocks_of(512, 4):
        g1[rows, :] = dot_tn(acts[:, rows], rhs[...]).astype(BF)
        copies.append(start(g1.at[rows, :], g1_out.at[rows, :]))
    wait(copies)


def attn_bwd_half(
    h, sc, lse, cos_t, low_t, high_t, gqkv, colsum, gm_hold, dq_t, dq, dk, dv, q_in, k_in, v_in, gm_in
):
    for r in range(1024 // 64):
        there = pl.ds(pl.multiple_of(sc[r] * 64, 64), 64)
        gm_hold[there, :] = gm_in[h, 64 * r : 64 * r + 64, :]
    keys = k_in[h]
    values = v_in[h]
    keys_t = keys.T
    lane = lax.broadcasted_iota(jnp.int32, (QB, 128), 1)
    allowed = diagonal(QB)
    for b in reversed(range(1024 // QB)):
        begin, end = b * QB, (b + 1) * QB
        query = q_in[h, begin:end, :]
        grad = gm_hold[begin:end, :]
        add_v, add_k = 0.0, 0.0
        for a in range(2):
            heads = slice(a * HEAD_DIM, (a + 1) * HEAD_DIM)
            mine = lane // HEAD_DIM == a
            only = jnp.where(mine, query, jnp.zeros_like(query))
            grad_only = jnp.where(mine, grad, jnp.zeros_like(grad))
            shift = lse[2 * h + a : 2 * h + a + 1, begin:end]
            scores = dot_nt(keys[:end], only)
            dprobs = dot_nt(values[:end], grad_only)
            low_p = jnp.where(allowed, jnp.exp(scores[begin:] - shift), 0.0)
            probs = low_p if b == 0 else jnp.concatenate([jnp.exp(scores[:begin] - shift), low_p], axis=0)
            delta = jnp.sum(probs * dprobs, axis=0, keepdims=True)
            gscores = (probs * (dprobs - delta)).astype(BF)
            add_v = add_v + dot(probs.astype(BF), grad_only)
            add_k = add_k + dot(gscores, only)
            dq_t[heads, begin:end] = dot(keys_t[:, :end], gscores)[heads, :]
        if end == 1024:
            dv[...], dk[...] = add_v, add_k
        else:
            dv[:end, :] += add_v
            dk[:end, :] += add_k
    for r in range(1024 // 128):
        here = slice(128 * r, 128 * r + 128)
        dq[here, :] = dq_t[:, here].T
    total = jnp.zeros((1, 384), F32)
    for r in range(1024 // 64):
        here = slice(64 * r, 64 * r + 64)
        there = pl.ds(pl.multiple_of(sc[r] * 64, 64), 64)
        tables = (cos_t[there, :], low_t[there, :], high_t[there, :])
        gq = turn_back(dq[there, :] * (HEAD_DIM**-0.5), *tables)
        gk = turn_back(dk[there, :], *tables)
        rows = jnp.concatenate([gq, gk, dv[there, :]], axis=1).astype(BF)
        gqkv[h, here, :] = rows
        total = total + jnp.sum(rows.astype(F32), axis=0, keepdims=True)
    colsum[h] = total


def attn_bwd(own, other, lse, gm_own, gm_other, tables, acts, gh_other, dep):
    length = gm_own.shape[0]
    ins = []
    for (q, k, v), gm in ((own, gm_own), (other, gm_other)):
        ins += [gm, k, q, v]
    return call(
        attn_bwd_body,
        anywhere(8) + vmem(1) + anywhere(6),
        anywhere(3) + vmem(1),
        [shape((length, 384))] * 2 + [shape((2048, 896)), shape((2, 1, 384), F32)],
        (*ins, lse, *tables, acts, gh_other, dep),
        "attn_bwd",
        [pltpu.VMEM((2, length, 384), BF), pltpu.VMEM((length, 128), BF), pltpu.VMEM((128, length), F32)]
        + [pltpu.VMEM((length, 128), F32)] * 3
        + [pltpu.VMEM((2, length, 128), BF)] * 4
        + [pltpu.VMEM((length, 128), F32)] * 3
        + [pltpu.VMEM((1024, 2048), BF), pltpu.VMEM((1024, 896), BF), pltpu.VMEM((2048, 896), BF)]
        + [pltpu.SemaphoreType.DMA((32,))],
    )


ROWS = 256
HUGE = (pltpu.SemaphoreType.DMA((176,)),)


def blocks_of(size=256, count=8):
    return [slice(size * r, size * r + size) for r in range(count)]


def message_places(outs, rows):
    up, down, own_a, own_z, left_z, right_a = outs
    one, two = slice(0, rows), slice(rows, 2 * rows)
    return [own_a, own_z, down.at[two, :], left_z, right_a, up.at[two, :], up.at[one, :], down.at[one, :]]


def flat(groups):
    return [copy for group in groups for copy in group]


def project_body(*refs):
    sc = row_blocks()
    pieces, w_own, w_other = refs[:8], refs[8:16], refs[16:24]
    b_own, b_other, tables_in = refs[24], refs[25], refs[26:29]
    acts_out, qkv_out = refs[29], refs[30:36]
    act_out, slope_out = refs[36:38], refs[38:40]
    acts, w, cos_t, low_t, high_t = refs[40:45]
    qkv, act, slope, sems = refs[45:51], refs[51:53], refs[53:55], refs[55]
    start = copier(sems)

    def tile(j):
        group = []
        for r, rows in enumerate(blocks_of()):
            if j < 6:
                cols = slice(256 * (j % 3), 256 * (j % 3) + 256)
                group.append(((w_own, w_other)[j // 3][r].at[:, cols], w.at[j, rows, :]))
            else:
                group.append((w_own[r].at[:, 768:], w.at[j, rows, :128]))
                group.append((w_other[r].at[:, 768:], w.at[j, rows, 128:]))
        return group

    def rows_in(m):
        return [(pieces[r], acts.at[128 * r : 128 * r + 128, :]) for r in (2 * m, 2 * m + 1)]

    def begin(group):
        return [start(a, b) for a, b in group]

    acts_in = [begin(rows_in(0))]
    w_in = [begin(tile(j)) for j in range(3)]
    rest = begin(zip(tables_in, (cos_t, low_t, high_t)))
    acts_in += [begin(rows_in(m)) for m in range(1, 4)]
    w_in += [begin(tile(j)) for j in range(3, 7)]
    root = (2.0 / np.pi) ** 0.5
    outs = []
    strips = [[(j // 3, 2 * (j % 3) + k) for k in range(2)] for j in range(6)] + [[(0, 6), (1, 6)]]
    steps = [(m, j) for m in range(4) for j in range(3)] + [(m, j) for m in range(4) for j in range(3, 7)]
    for m, j in steps:
        rows = slice(ROWS * m, ROWS * m + ROWS)
        if j == 0 and m == 0:
            wait(acts_in[0] + flat(w_in[:3]) + rest)
        if j == 0 and m == 1:
            wait(flat(acts_in[1:]))
            outs.append(start(acts, acts_out))
        if j == 3 and m == 0:
            wait(flat(w_in[3:]))
        result = dot(acts[rows, :], w[j])
        for k, (core, strip) in enumerate(strips[j]):
            cols = slice(128 * strip, 128 * strip + 128)
            h = result[:, 128 * k : 128 * k + 128] + (b_own, b_other)[core][:, cols]
            if strip < 3:
                for b in range(ROWS // 64):
                    there = pl.ds(pl.multiple_of(sc[4 * m + b] * 64, 64), 64)
                    u = h[64 * b : 64 * b + 64, :]
                    if strip < 2:
                        u = turn(u, cos_t[there, :], low_t[there, :], high_t[there, :])
                    if strip == 0:
                        u = u * (HEAD_DIM**-0.5)
                    qkv[3 * core + strip][there, :] = u.astype(BF)
                continue
            cols = slice(128 * (strip - 3), 128 * (strip - 3) + 128)
            square = h * h
            th = jnp.tanh(root * (h + 0.044715 * (square * h)))
            half = 0.5 + 0.5 * th
            act[core][rows, cols] = (h * half).astype(BF)
            slope[core][rows, cols] = (
                half + (0.5 * h) * (1.0 - th * th) * (root + (3 * 0.044715 * root) * square)
            ).astype(BF)
        if j == 6:
            for a, b in zip((*act, *slope), (*act_out, *slope_out)):
                outs.append(start(a.at[rows, :], b.at[rows, :]))
    for a, b in zip(qkv, qkv_out):
        outs.append(start(a, b))
    wait(outs)


def project(pieces, w_own, w_other, b_own, b_other, tables):
    small, wide, whole = (1024, 128), (1024, 512), (1024, 2048)
    return call(
        project_body,
        anywhere(24) + vmem(2) + anywhere(3),
        anywhere(11),
        [shape(whole)] + [shape(small)] * 6 + [shape(wide)] * 4,
        (*pieces, *w_own, *w_other, b_own, b_other, *tables),
        "project",
        [pltpu.VMEM(whole, BF), pltpu.VMEM((7, 2048, 256), BF)]
        + [pltpu.VMEM(small, F32)] * 3
        + [pltpu.VMEM(small, BF)] * 6
        + [pltpu.VMEM(wide, BF)] * 4
        + [*HUGE],
    )


def branch_body(merged, act_own, act_other, w_own, w_other, dep, out, lhs, w, stage, sems):
    sc = row_blocks()
    start = copier(sems)
    parts = ((merged.at[:, :128], 0, 128), (act_own, 128, 512), (merged.at[:, 128:], 640, 128), (act_other, 768, 512))
    lhs_in = [start(a, lhs.at[:, c : c + n]) for a, c, n in parts]
    w_in = [[start(w_own.at[r], w.at[r, :640, :]), start(w_other.at[r], w.at[r, 640:, :])] for r in range(8)]
    copies = []
    for half in (range(3), range(3, 8)):
        wait(lhs_in + flat(w_in[r] for r in half))
        for m in range(4):
            rows = slice(ROWS * m, ROWS * m + ROWS)
            for r in half:
                stage[rows, 256 * r : 256 * r + 256] = dot(lhs[rows, :], w[r]).astype(BF)
            if 7 in half:
                for p in (2 * m, 2 * m + 1):
                    to = pl.ds(pl.multiple_of(sc[2 * p] // 2 * 128, 128), 128)
                    copies.append(start(stage.at[128 * p : 128 * p + 128, :], out.at[to, :]))
    wait(copies)


def branch_part(merged, act_own, act_other, w_own, w_other, dep):
    return call(
        branch_body,
        anywhere(6),
        pl.BlockSpec(memory_space=pl.ANY),
        shape((1024, 2048)),
        (merged, act_own, act_other, w_own, w_other, dep),
        "branch_part",
        [pltpu.VMEM((1024, 1280), BF), pltpu.VMEM((8, 1280, 256), BF), pltpu.VMEM((1024, 2048), BF), *HUGE],
    )


def grad_in_body(cot, w_own, w_other, *refs):
    core, rows_sc = feature_blocks()[8], row_blocks()
    slope_in, (merged, act, dep) = refs[:2], refs[2:5]
    gout_out, gm_out, gh_out, g2_out, colsum = refs[5], refs[6:8], refs[8:10], refs[10], refs[11:13]
    gout, w, slope, gm, gh, lhs, stage, sems = refs[13], refs[14], refs[15:17], refs[17:19], refs[19:21], *refs[21:]
    start = copier(sems)

    def tile(j):
        copies = []
        for r, cols in enumerate(blocks_of()):
            for first, source, at in ((0, w_own, 256 * j), (640, w_other, 256 * j - 640)):
                lo, hi = max(at, 0), min(at + 256, 640)
                if lo < hi:
                    copies.append(start(source.at[r, lo:hi, :], w.at[lo + first : hi + first, cols]))
        return copies

    gout_in = [start(cot.at[rows_sc[r], core], gout.at[64 * r : 64 * r + 64, :]) for r in range(16)]
    w_in = [tile(0)]
    slope_copies = [start(a, b) for a, b in zip(slope_in, slope)]
    w_in += [tile(j) for j in range(1, 5)]
    lhs_in = [start(merged.at[:, 128:], lhs.at[:, :128]), start(act, lhs.at[:, 128:])]
    totals = [[jnp.zeros((1, 128), F32)] * 4 for _ in range(2)]
    copies = []
    for j in range(5):
        if j == 0:
            wait(gout_in + w_in[0] + slope_copies)
            copies.append(start(gout, gout_out))
        if j == 1:
            wait(flat(w_in) + lhs_in)
        for m in range(4):
            rows = slice(ROWS * m, ROWS * m + ROWS)
            result = dot_nt(gout[rows, :], w[256 * j : 256 * j + 256, :])
            for k in range(2):
                half, strip = (2 * j + k) // 5, (2 * j + k) % 5
                part = result[:, 128 * k : 128 * k + 128]
                if strip == 0:
                    gm[half][rows, :] = part.astype(BF)
                    continue
                cols = slice(128 * (strip - 1), 128 * strip)
                part = (part * slope[half][rows, cols].astype(F32)).astype(BF)
                gh[half][rows, cols] = part
                totals[half][strip - 1] += jnp.sum(part.astype(F32), axis=0, keepdims=True)
    for core in range(2):
        for strip in range(4):
            colsum[core][:, 128 * strip : 128 * strip + 128] = totals[core][strip]
    for a, b in zip((*gm, *gh), (*gm_out, *gh_out)):
        copies.append(start(a, b))
    for cols in blocks_of(512, 4):
        stage[:, cols] = dot_tn(lhs[...], gout[:, cols]).astype(BF)
        copies.append(start(stage.at[:, cols], g2_out.at[:, cols]))
    wait(copies)


def grad_in(cot, w_own, w_other, slope_own, slope_other, merged, act_other, dep):
    small, wide, whole = (1024, 128), (1024, 512), (1024, 2048)
    return call(
        grad_in_body,
        anywhere(8),
        anywhere(6) + vmem(2),
        [shape(whole)] + [shape(small)] * 2 + [shape(wide)] * 2 + [shape((640, 2048))] + [shape((1, 512), F32)] * 2,
        (cot, w_own, w_other, slope_own, slope_other, merged, act_other, dep),
        "grad_in",
        [pltpu.VMEM(whole, BF), pltpu.VMEM((1280, 2048), BF)]
        + [pltpu.VMEM(wide, BF)] * 2
        + [pltpu.VMEM(small, BF)] * 2
        + [pltpu.VMEM(wide, BF)] * 2
        + [pltpu.VMEM((1024, 640), BF), pltpu.VMEM((640, 2048), BF), *HUGE],
    )


def gnormed_body(q_own, gh_own, q_other, gh_other, acts_in, *refs):
    sc = feature_blocks()
    w_own, w_other, dep, cot_sum, attn_sums, up_own, up_other = refs[:8], refs[8:16], *refs[16:21]
    outs, vec_own, vec_send, (lhs, w, acts, stage, sems) = refs[21:27], refs[27], refs[28], refs[29:]
    places = message_places(outs, 128)
    start = copier(sems)
    parts = ((q_own, 0), (gh_own, 384), (q_other, 896), (gh_other, 1280))

    def rows_in(m):
        rows = slice(ROWS * m, ROWS * m + ROWS)
        copies = [start(a.at[rows, :], lhs.at[rows, c : c + a.shape[1]]) for a, c in parts]
        return copies + [start(acts_in.at[rows, :], acts.at[rows, :])]

    def tile(r):
        rows = slice(256 * r, 256 * r + 256)
        return [start(w_own[r], w.at[rows, :896]), start(w_other[r], w.at[rows, 896:])]

    lhs_in = {3: rows_in(3)}
    w_in = [tile(r) for r in range(8)]
    lhs_in.update({m: rows_in(m) for m in range(3)})
    totals = [[jnp.zeros((1, 256), F32)] * 8 for _ in range(2)]
    copies = []
    for m, first, last in ((3, 0, 3), (3, 3, 8), (0, 0, 8), (1, 0, 8), (2, 0, 8)):
        rows = slice(ROWS * m, ROWS * m + ROWS)
        if m == 3:
            wait(lhs_in[3] + flat(w_in[first:last]))
        if m == 0:
            wait(lhs_in[0] + lhs_in[1] + lhs_in[2])
        for r in range(first, last):
            cols = slice(256 * r, 256 * r + 256)
            result = dot_nt(lhs[rows, :], w[cols, :])
            totals[0][r] += jnp.sum(result, axis=0, keepdims=True)
            totals[1][r] += jnp.sum(result * acts[rows, cols].astype(F32), axis=0, keepdims=True)
            stage[rows, cols] = result.astype(BF)
        if last == 8:
            for p in (2 * m, 2 * m + 1):
                copies.append(start(stage.at[128 * p : 128 * p + 128, :], places[p]))
    for vec, half, up in ((vec_own, 0, up_own), (vec_send, 1, up_other)):
        vec[0:1, :] = cot_sum[...]
        for k in range(2):
            for r in range(8):
                vec[k + 1 : k + 2, pl.ds(pl.multiple_of(sc[r] * 256, 256), 256)] = totals[k][r]
        vec[3:4, :384], vec[3:4, 384:896] = attn_sums[half], up[...]
        vec[3:4, 896:] = jnp.zeros((1, 2048 - 896), F32)
    wait(copies)


def gnormed_part(q_own, gh_own, q_other, gh_other, acts, w_own, w_other, dep, *vectors):
    whole, piece = (1024, 2048), shape((128, 2048))
    *outs, vec_own, vec_send = call(
        gnormed_body,
        anywhere(22) + vmem(4),
        anywhere(6) + vmem(2),
        [shape((256, 2048))] * 2 + [piece] * 4 + [shape((4, 2048), F32)] * 2,
        (q_own, gh_own, q_other, gh_other, acts, *w_own, *w_other, dep, *vectors),
        "gnormed_part",
        [pltpu.VMEM((1024, 1792), BF), pltpu.VMEM((2048, 1792), BF), pltpu.VMEM(whole, BF), pltpu.VMEM(whole, BF), *HUGE],
    )
    return outs, vec_own, vec_send


def second_body(merged, act, gout, received, dep, *refs):
    sc = feature_blocks()
    places, (lhs, rhs, held, stage, sems) = message_places(refs[:6], 640), refs[6:]
    start = copier(sems)
    lhs_in = [start(merged.at[:, :128], lhs.at[:, :128]), start(act, lhs.at[:, 128:])]
    ins = []
    for r in range(8):
        cols = pl.ds(pl.multiple_of(sc[r] * 256, 256), 256)
        ins.append([start(gout.at[:, cols], rhs.at[r]), start(received.at[:, cols], held.at[r])])
    copies = []
    for r in range(8):
        if r == 0:
            wait(lhs_in + flat(ins[:3]))
        if r == 3:
            wait(flat(ins))
        result = dot_tn(lhs[...], rhs[r])
        stage[r] = (result + held[r].astype(F32)).astype(BF)
        copies.append(start(stage.at[r], places[r]))
    wait(copies)


def second_grad(merged, act, gout, received, dep):
    return call(
        second_body,
        anywhere(5),
        anywhere(6),
        [shape((1280, 256))] * 2 + [shape((640, 256))] * 4,
        (merged, act, gout, received, dep),
        "second_grad",
        [pltpu.VMEM((1024, 640), BF), pltpu.VMEM((8, 1024, 256), BF)]
        + [pltpu.VMEM((8, 640, 256), BF)] * 2
        + [*HUGE],
    )


def first_body(blocks, count, gqkv, gh, acts, received, *refs):
    outs, (lhs, rhs, held, stage, sems) = refs[count - 4 : -5], refs[-5:]
    places = [out.at[256 * k : 256 * k + 256, :] for out in outs for k in range(out.shape[0] // 256)]
    start = copier(sems)
    rhs_in = [start(gqkv, rhs.at[:, :384]), start(gh, rhs.at[:, 384:])]
    ins = []
    for k, r in enumerate(blocks):
        rows = slice(256 * r, 256 * r + 256)
        ins.append([start(acts.at[:, rows], lhs.at[k]), start(received.at[rows, :], held.at[k])])
    copies = []
    for k in range(4):
        if k == 0:
            wait(rhs_in + ins[0])
        if k == 1:
            wait(flat(ins))
        result = dot_tn(lhs[k], rhs[...])
        stage[k] = (result + held[k].astype(F32)).astype(BF)
        copies.append(start(stage.at[k], places[k]))
    wait(copies)


def first_grad(blocks, rows, *args):
    return call(
        functools.partial(first_body, blocks, len(args)),
        anywhere(len(args)),
        anywhere(1024 // rows),
        [shape((rows, 896))] * (1024 // rows),
        args,
        "first_grad",
        [pltpu.VMEM((4, 1024, 256), BF), pltpu.VMEM((1024, 896), BF)]
        + [pltpu.VMEM((4, 256, 896), BF)] * 2
        + [*HUGE],
    )


def rotary_tables(length):
    frequency = np.float32(10000.0) ** (-(np.arange(ROT // 2, dtype=np.float32) * 2.0 / ROT))
    angles = np.arange(length, dtype=np.float32)[:, None] * frequency.astype(np.float32)[None, :]
    cosine, sine = np.cos(angles), np.sin(angles)
    one = np.ones((length, HEAD_DIM - ROT), np.float32)
    zero_half, zero = np.zeros_like(sine), np.zeros_like(one)
    cos_t = np.concatenate([cosine, cosine, one] * 2, axis=1)
    low_t = np.concatenate([-sine, zero_half, zero] * 2, axis=1)
    high_t = np.concatenate([zero_half, sine, zero] * 2, axis=1)
    return tuple(jnp.asarray(a, F32) for a in (cos_t, low_t, high_t))


def by_kind(a):
    return jnp.swapaxes(a.reshape(2, 3, HEAD_DIM), 0, 1).reshape(384)


def shards(
    tokens,
    attn_weight,
    attn_bias,
    dense_weight,
    dense_bias,
    up_weight,
    up_bias,
    down_weight,
    down_bias,
    norm_gain,
    norm_bias,
    cotangent,
):
    tables = rotary_tables(16 * tokens.shape[1])
    gain_row, bias_row = norm_gain[None, :], norm_bias[None, :]

    cot = lax.all_gather(cotangent, "tensor", axis=0)
    acts_own, acts_send, cot_sum, f0, s0 = pre(
        tokens, cotangent, gain_row, bias_row, attn_weight, up_weight, dense_weight, down_weight
    )
    swapped = core_swap(acts_send)
    f1, f2, f4, f0x = zz_swap(f0), y_up(f0), y_down(f0), core_swap(f0)
    s_own = lax.all_gather(s0, "dp", axis=0)
    a0 = join(acts_own, swapped)
    a2, a4, a1 = x_up(a0), x_down(a0), z_swap(a0)
    f1 = tie(f1, f2, f4, a0)
    f3, f5, f1x = y_up(f1), y_down(f1), core_swap(f1)
    f2 = tie(f2, f1)
    f6, f2x, f4x = y_up(f2), core_swap(f2), core_swap(f4)
    a2 = tie(a2, a4, f2)
    a6 = x_up(a2)
    a1 = tie(a1, a2, f3, f5)
    a3, a5 = x_up(a1), x_down(a1)
    f5 = tie(f5, a1)
    f7, f5x = y_down(f5), core_swap(f5)
    a5 = tie(a5, f6)
    a7 = x_down(a5)
    f3 = tie(f3, a5, a6)
    f3x = core_swap(f3)
    f6 = tie(f6, f7, a3, f3)
    f6x, f7x = core_swap(f6), core_swap(f7)
    biases = tie(jnp.concatenate([by_kind(attn_bias), up_bias])[None, :], f1)
    other_biases = core_swap(biases)
    f_own, f_other = [f0, f1, f2, f3, f4, f5, f6, f7], [f0x, f1x, f2x, f3x, f4x, f5x, f6x, f7x]

    acts, *rest = project([a0, a1, a2, a3, a4, a5, a6, a7], f_own, f_other, biases, other_biases, tables)
    qkv_own, qkv_other, (act_own, act_other), (slope_own, slope_other) = rest[:3], rest[3:6], rest[6:8], rest[8:]
    merged, lse = attn_fwd(qkv_own, qkv_other, acts)
    s_own = tie(s_own, acts)
    s_other = core_swap(s_own)
    br = branch_part(merged, act_own, act_other, s_own, s_other, acts)
    group = [[2 * p + c for p in range(8)] for c in range(2)]
    br_sum = lax.psum_scatter(br, "tensor", scatter_dimension=0, axis_index_groups=group, tiled=True)

    gout, gm_own, gm_other, gh_own, gh_other, g2_other, up_sum_own, up_sum_other = grad_in(
        cot, s_own, s_other, slope_own, slope_other, merged, act_other, br
    )
    g2_received = core_swap(g2_other)
    gq_own, gq_other, g1_other, attn_sums = attn_bwd(
        qkv_own, qkv_other, lse, gm_own, gm_other, tables, acts, gh_other, gout
    )
    g1_received = core_swap(g1_other)
    g2_up, g2_down, g2_0, g2_1, g2_3, g2_4 = second_grad(merged, act_own, gout, g2_received, gq_own)
    g2_u, g2_d = y_up(g2_up), y_down(g2_down)
    (gn_up, gn_down, gn_0, gn_1, gn_3, gn_4), vec, vec_send = gnormed_part(
        gq_own, gh_own, gq_other, gh_other, acts, f_own, f_other, g2_0, cot_sum, attn_sums, up_sum_own, up_sum_other
    )
    gn_u, gn_d = x_up(gn_up), x_down(gn_down)
    step = core_swap(vec_send)

    n_one, n_two, m_one, m_two = slice(0, 128), slice(128, 256), slice(0, 256), slice(256, 512)
    one, two, last = slice(0, 640), slice(640, 1280), slice(64, 128)
    vec, g2_4, g2_3 = adds((vec, step), (g2_4, (g2_u, one)), (g2_3, (g2_d, one)), deps=(gn_0,), name="early_adds")
    step = zz_swap(vec)
    g2_ua, g2_dz = y_up(g2_4), y_down(g2_3)
    g1_up, g1_down = first_grad((6, 5, 7, 2), 512, gq_own, gh_own, acts, g1_received, g2_4)
    g1_u, g1_d = y_up(g1_up), y_down(g1_down)
    (vec,) = adds((vec, step), deps=(g1_up, g2_ua, g2_dz))
    step = z_swap(vec)
    g1_0, g1_1, g1_3, g1_4 = first_grad((0, 1, 3, 4), 256, gq_own, gh_own, acts, g1_received, vec)
    br_sum = tie(br_sum, g1_0)
    br_received = core_swap(br_sum[64:])
    layer_out = post_out(tokens, br_sum, br_received, (dense_bias + down_bias)[None, :])
    gn_4, gn_3, vec, g2_1 = adds(
        (gn_4, (gn_u, n_one)),
        (gn_3, (gn_d, n_one)),
        (vec, (step, "top")),
        (g2_1, (g2_u, two), g2_dz),
        deps=(layer_out,),
        name="early_adds",
    )
    gn_ua, gn_dz = x_up(gn_4), x_down(gn_3)
    step, g2_z = y_pair(vec), zz_swap(g2_1)
    g1_4, g1_3 = adds((g1_4, (g1_u, m_one)), (g1_3, (g1_d, m_one)), deps=(gn_4,))
    g1_ua, g1_dz = y_up(g1_4), y_down(g1_3)
    gn_1, vec = adds((gn_1, (gn_u, n_two), gn_dz), (vec, step), deps=(g1_4, gn_ua, g2_z))
    gn_z = z_swap(gn_1)
    step = y_cross(vec)
    g1_1, vec = adds((g1_1, (g1_u, m_two), g1_dz), (vec, step), deps=(gn_1, g1_ua))
    g1_z = zz_swap(g1_1)
    step = x_pair(vec)
    dense_grad, down_grad, attn_bias_grad, up_bias_grad = finish_second(g2_0, g2_ua, g2_d, g2_z, vec, vec)
    gn_send, vec = adds(
        ((gn_0, last), (gn_ua, last), (gn_d, slice(192, 256)), (gn_z, last)), (vec, (step, "top")), deps=(dense_grad,)
    )
    gn_received, step = core_swap(gn_send), x_cross(vec)
    grad_tokens = post_grad(tokens, cotangent, (gn_0, gn_ua, gn_d, gn_z), gn_received, gain_row)
    out_bias_grad, norm_gain_grad, norm_bias_grad = finish_vector(
        (vec, step), norm_bias[None, :], norm_gain[None, :], grad_tokens
    )
    attn_grad, up_grad = finish_first(g1_0, g1_ua, g1_d, g1_z, out_bias_grad)
    out_bias_grad = out_bias_grad[0]
    return (
        layer_out,
        grad_tokens,
        attn_grad,
        attn_bias_grad[0],
        dense_grad,
        out_bias_grad,
        up_grad,
        up_bias_grad[0],
        down_grad,
        out_bias_grad,
        norm_gain_grad[0],
        norm_bias_grad[0],
    )


def solution(mesh):
    in_specs = (
        P("dp", "tensor", None),
        P("dp", "tensor"),
        P("tensor"),
        P("tensor", "dp"),
        P(),
        P("dp", "tensor"),
        P("tensor"),
        P("tensor", "dp"),
        P(),
        P(),
        P(),
        P("dp", "tensor", None),
    )
    out_specs = (
        P("dp", "tensor", None),
        P("dp", "tensor", None),
        P("dp", "tensor"),
        P("tensor"),
        P("tensor", "dp"),
        P(),
        P("dp", "tensor"),
        P("tensor"),
        P("tensor", "dp"),
        P(),
        P(),
        P(),
    )
    return jax.shard_map(shards, mesh=mesh, in_specs=in_specs, out_specs=out_specs, check_vma=False)
```

```python
import functools

import jax
import jax.numpy as jnp
import numpy as np
from jax import lax
from jax.experimental import pallas as pl
from jax.experimental.pallas import tpu as pltpu
from jax.sharding import PartitionSpec as P

HEAD_DIM = 64
ROT = 32
EPS = 1e-05
BF = jnp.bfloat16
LIMIT = 60
F32 = jnp.float32

OFFSETS = (0, -1, 1, 2)


def tensor_index(x, zlo, core):
    return (x % 4) * 4 + (zlo % 2) * 2 + core % 2


def dp_index(zhi, y):
    return (zhi % 2) * 4 + y % 4


def tensor_move(dx, dz, dc):
    return [
        (tensor_index(x, z, c), tensor_index(x + dx, z + dz, c + dc))
        for x in range(4)
        for z in range(2)
        for c in range(2)
    ]


def dp_move(dz, dy):
    return [(dp_index(z, y), dp_index(z + dz, y + dy)) for z in range(2) for y in range(4)]


def x_up(a):
    return lax.ppermute(a, "tensor", tensor_move(1, 0, 0))


def x_down(a):
    return lax.ppermute(a, "tensor", tensor_move(-1, 0, 0))


def z_swap(a):
    return lax.ppermute(a, "tensor", tensor_move(0, 1, 0))


def core_swap(a):
    return lax.ppermute(a, "tensor", tensor_move(0, 0, 1))


def y_up(a):
    return lax.ppermute(a, "dp", dp_move(0, 1))


def y_down(a):
    return lax.ppermute(a, "dp", dp_move(0, -1))


def zz_swap(a):
    return lax.ppermute(a, "dp", dp_move(1, 0))


def tie_body(*refs):
    pass


def tie(value, *others):
    anywhere = pl.BlockSpec(memory_space=pl.ANY)
    return pl.pallas_call(
        tie_body,
        in_specs=[anywhere] * (1 + len(others)),
        out_specs=anywhere,
        out_shape=jax.ShapeDtypeStruct(value.shape, value.dtype),
        input_output_aliases={0: 0},
        compiler_params=pltpu.CompilerParams(),
        cost_estimate=pl.CostEstimate(flops=0, bytes_accessed=0, transcendentals=0),
        name="tie",
    )(value, *others)


def join_body(own, received, *outs):
    rows = own.shape[0]
    for out in outs:
        out[:rows, :], out[rows:, :] = own[...], received[...]


def join(own, received):
    rows, width = own.shape
    return call(join_body, vmem(2), vmem(1), [shape((2 * rows, width))], (own, received), "join")[0]


def x_pair(a):
    return lax.ppermute(a, "tensor", [(i, tensor_index(i // 4 ^ 1, i // 2 % 2, i % 2)) for i in range(16)])


def x_cross(a):
    return lax.ppermute(a, "tensor", [(i, tensor_index(3 - i // 4, i // 2 % 2, i % 2)) for i in range(16)])


def y_pair(a):
    return lax.ppermute(a, "dp", [(i, dp_index(i // 4, i % 4 ^ 1)) for i in range(8)])


def y_cross(a):
    return lax.ppermute(a, "dp", [(i, dp_index(i // 4, 3 - i % 4)) for i in range(8)])


def vmem(count):
    return [pl.BlockSpec(memory_space=pltpu.VMEM)] * count


def feature_blocks():
    d, t = lax.axis_index("dp"), lax.axis_index("tensor")
    zhi, y = d // 4, d % 4
    return [((zhi + j) % 2) * 4 + (y + o) % 4 for o in OFFSETS for j in range(2)] + [t % 2]


def row_blocks():
    t = lax.axis_index("tensor")
    x, zlo, core = t // 4, (t // 2) % 2, t % 2
    return [
        4 * ((x + o) % 4) + 2 * ((zlo + j) % 2) + (core + k) % 2
        for o in OFFSETS
        for j in range(2)
        for k in range(2)
    ]


def anywhere(count=1):
    return [pl.BlockSpec(memory_space=pl.ANY)] * count


def params(limit=LIMIT):
    return pltpu.CompilerParams(vmem_limit_bytes=limit * 1024 * 1024)


TIMES = dict(
    project=17, attn_fwd=10, branch_part=11, grad_in=17, attn_bwd=20, second_grad=60, gnormed_part=15, first_grad=40,
    adds=0, early_adds=0, finish=0, post_out=0, post_grad=0, pre=0, join=0,
)
FLOPS = 200_000_000
LARGE = ("pre", "early_adds", "project", "attn_fwd", "branch_part", "grad_in", "attn_bwd", "second_grad", "gnormed_part", "first_grad")


def call(body, in_specs, out_specs, out_shape, args, name, scratch=(), **kwargs):
    return pl.pallas_call(
        body,
        in_specs=in_specs,
        out_specs=out_specs,
        out_shape=out_shape,
        scratch_shapes=list(scratch),
        compiler_params=params(LIMIT if name in LARGE else 16),
        cost_estimate=pl.CostEstimate(flops=TIMES[name] * FLOPS + 1, bytes_accessed=1, transcendentals=0),
        name=name,
        **kwargs,
    )(*args)


def shape(dims, dtype=BF):
    return jax.ShapeDtypeStruct(dims, dtype)


class Copy:
    def __init__(self, src, dst, sem):
        self.copy, self.waited = pltpu.make_async_copy(src, dst, sem), False
        self.copy.start()

    def wait(self):
        if not self.waited:
            self.copy.wait()
        self.waited = True


def copier(sems):
    used = iter(range(sems.shape[0]))
    return lambda src, dst: Copy(src, dst, sems.at[next(used)])


def wait(copies):
    for copy in copies:
        copy.wait()


def adds_body(groups, count, *refs):
    sizes = [len(group) for group in groups]
    ins, outs, sems = refs[: sum(sizes)], refs[count : count + len(groups)], refs[-1]
    holds = refs[count + len(groups) : -1]
    start = copier(sems)
    rows = [r for group in groups for r in group]
    copies = [start(a.at[r, :] if isinstance(r, slice) else a, b) for a, r, b in zip(ins, rows, holds)]
    at = 0
    for size, out in zip(sizes, outs):
        wait(copies[at : at + size])
        total = holds[at][...].astype(F32)
        for k in range(at + 1, at + size):
            term = holds[k][...].astype(F32)
            if rows[k] == "top":
                term = jnp.where(lax.broadcasted_iota(jnp.int32, term.shape, 0) < 3, term, 0.0)
            total = total + term
        out[...] = total.astype(out.dtype)
        at += size


def adds(*groups, deps=(), name="adds"):
    groups = [[a if isinstance(a, tuple) else (a, None) for a in group] for group in groups]
    flat_groups = [a for group in groups for a in group]
    dims = [(r.stop - r.start if isinstance(r, slice) else a.shape[0], a.shape[1]) for a, r in flat_groups]
    rows = tuple(tuple(r for _, r in group) for group in groups)
    firsts = [sum(len(group) for group in groups[:k]) for k in range(len(groups))]
    return call(
        functools.partial(adds_body, rows, len(flat_groups) + len(deps)),
        anywhere(len(flat_groups) + len(deps)),
        vmem(len(groups)),
        [shape(dims[k], flat_groups[k][0].dtype) for k in firsts],
        (*(a for a, _ in flat_groups), *deps),
        name,
        [pltpu.VMEM(dim, a.dtype) for dim, (a, _) in zip(dims, flat_groups)]
        + [pltpu.SemaphoreType.DMA((len(flat_groups),))],
    )


def finish_first_body(a, b, c, d, attn_out, up_out, p0, p1, p2, p3, sems):
    start = copier(sems)
    wait([start(a, p0), start(b, p1), start(c.at[256:, :], p2), start(d, p3)])
    total = sum(p[...].astype(F32) for p in (p0, p1, p2, p3))
    by_head = [total[:, (2 * k + h) * 64 : (2 * k + h) * 64 + 64] for h in range(2) for k in range(3)]
    attn_out[...] = jnp.concatenate(by_head, axis=1)
    up_out[...] = total[:, 384:]


def finish_first(a, b, c, d, dep):
    return call(
        lambda a, b, c, d, dep, *refs: finish_first_body(a, b, c, d, *refs),
        anywhere(5),
        vmem(2),
        [shape((256, 384), F32), shape((256, 512), F32)],
        (a, b, c, d, dep),
        "finish",
        [pltpu.VMEM((256, 896), BF)] * 4 + [pltpu.SemaphoreType.DMA((4,))],
    )


def finish_second_body(a, b, c, d, vec, dep, dense_out, down_out, attn_bias, up_bias, p0, p1, p2, p3, sems):
    start = copier(sems)
    copies = [start(a, p0), start(b, p1), start(c.at[640:, :], p2), start(d, p3)]
    row = vec[3:4, :]
    by_head = [row[:, (2 * k + h) * 64 : (2 * k + h) * 64 + 64] for h in range(2) for k in range(3)]
    attn_bias[...] = jnp.concatenate(by_head, axis=1)
    up_bias[...] = row[:, 384:896]
    wait(copies)
    total = sum(p[...].astype(F32) for p in (p0, p1, p2, p3))
    dense_out[...], down_out[...] = total[:128, :], total[128:, :]


def finish_second(a, b, c, d, vec, dep):
    return call(
        finish_second_body,
        anywhere(4) + vmem(1) + anywhere(),
        vmem(4),
        [shape((128, 256), F32), shape((512, 256), F32), shape((1, 384), F32), shape((1, 512), F32)],
        (a, b, c, d, vec, dep),
        "finish",
        [pltpu.VMEM((640, 256), BF)] * 4 + [pltpu.SemaphoreType.DMA((4,))],
    )


def finish_vector_body(a, b, norm_bias, norm_gain, dep, out_bias, gain_out, bias_out):
    total = a[...] + b[...]
    out_bias[...] = total[0:1, :]
    bias_out[...] = total[1:2, :]
    gain_out[...] = (total[2:3, :] - norm_bias[...] * total[1:2, :]) / norm_gain[...]


def finish_vector(parts, norm_bias, norm_gain, dep):
    return call(
        finish_vector_body,
        vmem(4) + anywhere(),
        vmem(3),
        [shape((1, 2048), F32)] * 3,
        (*parts, norm_bias, norm_gain, dep),
        "finish",
    )


def pre_body(
    tok_in, cot_in, gain, bias, attn_in, up, dense, down,
    acts_out, acts_send, cotsum, first, second, tok, cot, attn, hold, sems,
):
    sc = feature_blocks()
    start = copier(sems)
    in_attn = start(attn_in, attn)
    in_tok = start(tok_in, tok)
    in_cot = start(cot_in, cot)
    rest = [start(up, first.at[:, 384:]), start(dense, second.at[:128, :]), start(down, second.at[128:, :])]
    by_kind = lambda a: jnp.concatenate(
        [a[:, (3 * h + k) * 64 : (3 * h + k) * 64 + 64] for k in range(3) for h in range(2)], axis=1
    )
    in_attn.wait()
    first[:, :384] = by_kind(attn[...])
    in_tok.wait()
    in_cot.wait()
    total = jnp.zeros(cotsum.shape, F32)
    for s in range(2):
        seq = sc[8] if s == 0 else 1 - sc[8]
        xin = tok[seq].astype(F32)
        centred = xin - jnp.mean(xin, axis=-1, keepdims=True)
        spread = jnp.mean(centred * centred, axis=-1, keepdims=True)
        hold[...] = (centred * lax.rsqrt(spread + EPS) * gain[...] + bias[...]).astype(BF)
        total = total + jnp.sum(cot[seq].astype(F32), axis=0, keepdims=True)
        for r in range(8):
            cols = pl.ds(pl.multiple_of(sc[r] * 256, 256), 256)
            to = slice(r * 256, (r + 1) * 256)
            (acts_out, acts_send)[s][:, to] = hold[:, cols]
    cotsum[...] = total
    wait(rest)


def pre(tok, cot, gain, bias, attn, *rest):
    rows, width = tok.shape[1:]
    return call(
        pre_body,
        anywhere(2) + vmem(2) + anywhere(4),
        vmem(5),
        [
            shape((rows, width)),
            shape((rows, width)),
            shape((1, width), F32),
            shape((256, 896)),
            shape((640, 256)),
        ],
        (tok, cot, gain, bias, attn, *rest),
        "pre",
        [pltpu.VMEM(tok.shape, BF), pltpu.VMEM(tok.shape, BF), pltpu.VMEM(attn.shape, BF)]
        + [pltpu.VMEM((rows, width), BF), pltpu.SemaphoreType.DMA((6,))],
    )


def own_rows(sc, parts, received, hold):
    for s in range(2):
        rows = sum(ref[...].astype(F32) for ref in parts) if s == 0 else received[...].astype(F32)
        for r in range(8):
            cols = pl.ds(pl.multiple_of(sc[r] * 256, 256), 256)
            hold[s, :, cols] = rows[:, r * 256 : (r + 1) * 256]


def post_out_body(tok, part, received, extra, out):
    sc = feature_blocks()
    for s in range(2):
        seq = sc[8] if s == 0 else 1 - sc[8]
        rows = (part[:64, :] if s == 0 else received[...]).astype(F32)
        out[seq] = (tok[seq].astype(F32) + rows + extra[...]).astype(BF)


def post_out(tok, part, received, extra):
    return call(
        post_out_body,
        vmem(4),
        pl.BlockSpec(memory_space=pltpu.VMEM),
        shape(tok.shape),
        (tok, part, received, extra),
        "post_out",
    )


def post_grad_body(tok_in, cot_in, a, b, c, d, received, gain, out, tok, cot, hold, p0, p1, p2, p3, p4, sems):
    sc = feature_blocks()
    start = copier(sems)
    ins = [start(ref.at[:64, :], p) for ref, p in zip((a, b, c.at[128:, :], d, received), (p0, p1, p2, p3, p4))]
    wait(ins + [start(tok_in, tok), start(cot_in, cot)])
    own_rows(sc, (p0, p1, p2, p3), p4, hold)
    for s in range(2):
        seq = sc[8] if s == 0 else 1 - sc[8]
        xin = tok[seq].astype(F32)
        centred = xin - jnp.mean(xin, axis=-1, keepdims=True)
        scale = lax.rsqrt(jnp.mean(centred * centred, axis=-1, keepdims=True) + EPS)
        xhat = centred * scale
        e = hold[s] * gain[...]
        mean_e = jnp.mean(e, axis=-1, keepdims=True)
        mean_x = jnp.mean(e * xhat, axis=-1, keepdims=True)
        out[seq] = cot[seq].astype(F32) + (e - mean_e - xhat * mean_x) * scale


def post_grad(tok, cot, parts, received, gain):
    rows = tok.shape[1:]
    return call(
        post_grad_body,
        anywhere(7) + vmem(1),
        pl.BlockSpec(memory_space=pltpu.VMEM),
        shape(tok.shape, F32),
        (tok, cot, *parts, received, gain),
        "post_grad",
        [pltpu.VMEM(tok.shape, BF)] * 2
        + [pltpu.VMEM(tok.shape, F32)]
        + [pltpu.VMEM(rows, BF)] * 5
        + [pltpu.SemaphoreType.DMA((7,))],
    )


def turn(u, cosine, sine_low, sine_high):
    return (
        u * cosine
        + pltpu.roll(u, u.shape[-1] - ROT // 2, 1) * sine_low
        + pltpu.roll(u, ROT // 2, 1) * sine_high
    )


def turn_back(u, cosine, sine_low, sine_high):
    return (
        u * cosine
        - pltpu.roll(u, u.shape[-1] - ROT // 2, 1) * sine_low
        - pltpu.roll(u, ROT // 2, 1) * sine_high
    )


def dot(a, b):
    return lax.dot_general(a, b, (((1,), (0,)), ((), ())), preferred_element_type=F32)


def dot_nt(a, b):
    return lax.dot_general(a, b, (((1,), (1,)), ((), ())), preferred_element_type=F32)


def dot_tn(a, b):
    return lax.dot_general(a, b, (((0,), (0,)), ((), ())), preferred_element_type=F32)


QB = 256


def diagonal(size):
    keys = lax.broadcasted_iota(jnp.int32, (size, size), 0)
    queries = lax.broadcasted_iota(jnp.int32, (size, size), 1)
    return keys <= queries


def attn_fwd_body(*refs):
    sc = row_blocks()
    dep, merged, lse, out_t, out_abs, q_in, k_in, v_in, sems = refs[6:]
    start = copier(sems)
    wait([start(refs[3 * h + k], held.at[h]) for h in range(2) for k, held in enumerate((q_in, k_in, v_in))])
    for h in range(2):
        attn_fwd_half(h, sc, merged, lse, out_t, out_abs, q_in, k_in, v_in)


def attn_fwd_half(h, sc, merged, lse, out_t, out_abs, q_in, k_in, v_in):
    keys = k_in[h]
    values_t = v_in[h].T
    lane = lax.broadcasted_iota(jnp.int32, (QB, 128), 1)
    allowed = diagonal(QB)
    for b in range(1024 // QB):
        begin, end = b * QB, (b + 1) * QB
        query = q_in[h, begin:end, :]
        for a in range(2):
            heads = slice(a * HEAD_DIM, (a + 1) * HEAD_DIM)
            only = jnp.where(lane // HEAD_DIM == a, query, jnp.zeros_like(query))
            scores = dot_nt(keys[:end], only)
            low = jnp.where(allowed, scores[begin:], -jnp.inf)
            top = jnp.max(low, axis=0, keepdims=True)
            if b > 0:
                top = jnp.maximum(top, jnp.max(scores[:begin], axis=0, keepdims=True))
            weights = jnp.exp(low - top)
            total = jnp.sum(weights, axis=0, keepdims=True)
            out = dot(values_t[:, begin:end], weights.astype(BF))
            if b > 0:
                weights = jnp.exp(scores[:begin] - top)
                total = total + jnp.sum(weights, axis=0, keepdims=True)
                out = out + dot(values_t[:, :begin], weights.astype(BF))
            out_t[heads, begin:end] = (out * (1.0 / total))[heads, :]
            lse[2 * h + a : 2 * h + a + 1, begin:end] = top + jnp.log(total)
    for r in range(1024 // 128):
        here = slice(128 * r, 128 * r + 128)
        out_abs[here, :] = out_t[:, here].T.astype(BF)
    for r in range(1024 // 64):
        there = pl.ds(pl.multiple_of(sc[r] * 64, 64), 64)
        merged[64 * r : 64 * r + 64, 128 * h : 128 * h + 128] = out_abs[there, :]


def attn_fwd(own, other, dep):
    length = own[0].shape[0]
    return call(
        attn_fwd_body,
        anywhere(7),
        vmem(2),
        [shape((length, 256)), shape((4, length), F32)],
        (*own, *other, dep),
        "attn_fwd",
        [pltpu.VMEM((128, length), F32), pltpu.VMEM((length, 128), BF)]
        + [pltpu.VMEM((2, length, 128), BF)] * 3
        + [pltpu.SemaphoreType.DMA((6,))],
    )


def attn_bwd_body(*refs):
    sc = row_blocks()
    lse, tables_in, (acts_in, gh_in, dep) = refs[8], refs[9:12], refs[12:15]
    outs, g1_out, colsum = refs[15:17], refs[17], refs[18]
    gqkv, gm_hold, dq_t, dq, dk, dv, q_in, k_in, v_in, gm_in = refs[19:29]
    tables, (acts, rhs, g1, sems) = refs[29:32], refs[32:]
    start = copier(sems)
    held = (gm_in, k_in, q_in, v_in)
    ins = [start(refs[4 * h + k], a.at[h]) for h in (1, 0) for k, a in enumerate(held)]
    ins += [start(a, b) for a, b in zip(tables_in, tables)]
    rest = [start(gh_in, rhs.at[:, 384:]), start(acts_in, acts)]
    wait(ins)
    copies = []
    for h in (1, 0):
        attn_bwd_half(h, sc, lse, *tables, gqkv, colsum, gm_hold, dq_t, dq, dk, dv, q_in, k_in, v_in, gm_in)
        copies.append(start(gqkv.at[h], outs[h]))
    wait(rest)
    rhs[:, :384] = gqkv[1]
    for rows in blocks_of(512, 4):
        g1[rows, :] = dot_tn(acts[:, rows], rhs[...]).astype(BF)
        copies.append(start(g1.at[rows, :], g1_out.at[rows, :]))
    wait(copies)


def attn_bwd_half(
    h, sc, lse, cos_t, low_t, high_t, gqkv, colsum, gm_hold, dq_t, dq, dk, dv, q_in, k_in, v_in, gm_in
):
    for r in range(1024 // 64):
        there = pl.ds(pl.multiple_of(sc[r] * 64, 64), 64)
        gm_hold[there, :] = gm_in[h, 64 * r : 64 * r + 64, :]
    keys = k_in[h]
    values = v_in[h]
    keys_t = keys.T
    lane = lax.broadcasted_iota(jnp.int32, (QB, 128), 1)
    allowed = diagonal(QB)
    for b in reversed(range(1024 // QB)):
        begin, end = b * QB, (b + 1) * QB
        query = q_in[h, begin:end, :]
        grad = gm_hold[begin:end, :]
        add_v, add_k = 0.0, 0.0
        for a in range(2):
            heads = slice(a * HEAD_DIM, (a + 1) * HEAD_DIM)
            mine = lane // HEAD_DIM == a
            only = jnp.where(mine, query, jnp.zeros_like(query))
            grad_only = jnp.where(mine, grad, jnp.zeros_like(grad))
            shift = lse[2 * h + a : 2 * h + a + 1, begin:end]
            scores = dot_nt(keys[:end], only)
            dprobs = dot_nt(values[:end], grad_only)
            low_p = jnp.where(allowed, jnp.exp(scores[begin:] - shift), 0.0)
            probs = low_p if b == 0 else jnp.concatenate([jnp.exp(scores[:begin] - shift), low_p], axis=0)
            delta = jnp.sum(probs * dprobs, axis=0, keepdims=True)
            gscores = (probs * (dprobs - delta)).astype(BF)
            add_v = add_v + dot(probs.astype(BF), grad_only)
            add_k = add_k + dot(gscores, only)
            dq_t[heads, begin:end] = dot(keys_t[:, :end], gscores)[heads, :]
        if end == 1024:
            dv[...], dk[...] = add_v, add_k
        else:
            dv[:end, :] += add_v
            dk[:end, :] += add_k
    for r in range(1024 // 128):
        here = slice(128 * r, 128 * r + 128)
        dq[here, :] = dq_t[:, here].T
    total = jnp.zeros((1, 384), F32)
    for r in range(1024 // 64):
        here = slice(64 * r, 64 * r + 64)
        there = pl.ds(pl.multiple_of(sc[r] * 64, 64), 64)
        tables = (cos_t[there, :], low_t[there, :], high_t[there, :])
        gq = turn_back(dq[there, :] * (HEAD_DIM**-0.5), *tables)
        gk = turn_back(dk[there, :], *tables)
        rows = jnp.concatenate([gq, gk, dv[there, :]], axis=1).astype(BF)
        gqkv[h, here, :] = rows
        total = total + jnp.sum(rows.astype(F32), axis=0, keepdims=True)
    colsum[h] = total


def attn_bwd(own, other, lse, gm_own, gm_other, tables, acts, gh_other, dep):
    length = gm_own.shape[0]
    ins = []
    for (q, k, v), gm in ((own, gm_own), (other, gm_other)):
        ins += [gm, k, q, v]
    return call(
        attn_bwd_body,
        anywhere(8) + vmem(1) + anywhere(6),
        anywhere(3) + vmem(1),
        [shape((length, 384))] * 2 + [shape((2048, 896)), shape((2, 1, 384), F32)],
        (*ins, lse, *tables, acts, gh_other, dep),
        "attn_bwd",
        [pltpu.VMEM((2, length, 384), BF), pltpu.VMEM((length, 128), BF), pltpu.VMEM((128, length), F32)]
        + [pltpu.VMEM((length, 128), F32)] * 3
        + [pltpu.VMEM((2, length, 128), BF)] * 4
        + [pltpu.VMEM((length, 128), F32)] * 3
        + [pltpu.VMEM((1024, 2048), BF), pltpu.VMEM((1024, 896), BF), pltpu.VMEM((2048, 896), BF)]
        + [pltpu.SemaphoreType.DMA((32,))],
    )


ROWS = 256
HUGE = (pltpu.SemaphoreType.DMA((176,)),)


def blocks_of(size=256, count=8):
    return [slice(size * r, size * r + size) for r in range(count)]


def message_places(outs, rows):
    up, down, own_a, own_z, left_z, right_a = outs
    one, two = slice(0, rows), slice(rows, 2 * rows)
    return [own_a, own_z, down.at[two, :], left_z, right_a, up.at[two, :], up.at[one, :], down.at[one, :]]


def flat(groups):
    return [copy for group in groups for copy in group]


def project_body(*refs):
    sc = row_blocks()
    pieces, w_own, w_other = refs[:8], refs[8:16], refs[16:24]
    b_own, b_other, tables_in = refs[24], refs[25], refs[26:29]
    acts_out, qkv_out = refs[29], refs[30:36]
    act_out, slope_out = refs[36:38], refs[38:40]
    acts, w, cos_t, low_t, high_t = refs[40:45]
    qkv, act, slope, sems = refs[45:51], refs[51:53], refs[53:55], refs[55]
    start = copier(sems)

    def tile(j):
        group = []
        for r, rows in enumerate(blocks_of()):
            if j < 6:
                cols = slice(256 * (j % 3), 256 * (j % 3) + 256)
                group.append(((w_own, w_other)[j // 3][r].at[:, cols], w.at[j, rows, :]))
            else:
                group.append((w_own[r].at[:, 768:], w.at[j, rows, :128]))
                group.append((w_other[r].at[:, 768:], w.at[j, rows, 128:]))
        return group

    def rows_in(m):
        return [(pieces[r], acts.at[128 * r : 128 * r + 128, :]) for r in (2 * m, 2 * m + 1)]

    def begin(group):
        return [start(a, b) for a, b in group]

    acts_in = [begin(rows_in(0))]
    w_in = {j: begin(tile(j)) for j in (1, 2, 0)}
    rest = begin(zip(tables_in, (cos_t, low_t, high_t)))
    acts_in += [begin(rows_in(m)) for m in range(1, 4)]
    w_in.update({j: begin(tile(j)) for j in range(3, 7)})
    root = (2.0 / np.pi) ** 0.5
    outs = []
    strips = [[(j // 3, 2 * (j % 3) + k) for k in range(2)] for j in range(6)] + [[(0, 6), (1, 6)]]
    steps = [(m, j) for m in range(4) for j in (1, 2, 0)] + [(m, j) for m in range(4) for j in range(3, 7)]
    for m, j in steps:
        rows = slice(ROWS * m, ROWS * m + ROWS)
        if j == 1 and m == 0:
            wait(acts_in[0] + w_in[1] + w_in[2])
        if j == 0 and m == 0:
            wait(w_in[0] + rest)
        if j == 1 and m == 1:
            wait(flat(acts_in[1:]))
            outs.append(start(acts, acts_out))
        if j == 3 and m == 0:
            wait(flat(w_in[k] for k in range(3, 7)))
        result = dot(acts[rows, :], w[j])
        for k, (core, strip) in enumerate(strips[j]):
            cols = slice(128 * strip, 128 * strip + 128)
            h = result[:, 128 * k : 128 * k + 128] + (b_own, b_other)[core][:, cols]
            if strip < 3:
                for b in range(ROWS // 64):
                    there = pl.ds(pl.multiple_of(sc[4 * m + b] * 64, 64), 64)
                    u = h[64 * b : 64 * b + 64, :]
                    if strip < 2:
                        u = turn(u, cos_t[there, :], low_t[there, :], high_t[there, :])
                    if strip == 0:
                        u = u * (HEAD_DIM**-0.5)
                    qkv[3 * core + strip][there, :] = u.astype(BF)
                continue
            cols = slice(128 * (strip - 3), 128 * (strip - 3) + 128)
            square = h * h
            th = jnp.tanh(root * (h + 0.044715 * (square * h)))
            half = 0.5 + 0.5 * th
            act[core][rows, cols] = (h * half).astype(BF)
            slope[core][rows, cols] = (
                half + (0.5 * h) * (1.0 - th * th) * (root + (3 * 0.044715 * root) * square)
            ).astype(BF)
        if j == 6:
            for a, b in zip((*act, *slope), (*act_out, *slope_out)):
                outs.append(start(a.at[rows, :], b.at[rows, :]))
    for a, b in zip(qkv, qkv_out):
        outs.append(start(a, b))
    wait(outs)


def project(pieces, w_own, w_other, b_own, b_other, tables):
    small, wide, whole = (1024, 128), (1024, 512), (1024, 2048)
    return call(
        project_body,
        anywhere(24) + vmem(2) + anywhere(3),
        anywhere(11),
        [shape(whole)] + [shape(small)] * 6 + [shape(wide)] * 4,
        (*pieces, *w_own, *w_other, b_own, b_other, *tables),
        "project",
        [pltpu.VMEM(whole, BF), pltpu.VMEM((7, 2048, 256), BF)]
        + [pltpu.VMEM(small, F32)] * 3
        + [pltpu.VMEM(small, BF)] * 6
        + [pltpu.VMEM(wide, BF)] * 4
        + [*HUGE],
    )


def branch_body(merged, act_own, act_other, w_own, w_other, dep, out, lhs, w, stage, sems):
    sc = row_blocks()
    start = copier(sems)
    parts = ((merged.at[:, :128], 0, 128), (act_own, 128, 512), (merged.at[:, 128:], 640, 128), (act_other, 768, 512))
    lhs_in = [start(a, lhs.at[:, c : c + n]) for a, c, n in parts]
    w_in = [[start(w_own.at[r], w.at[r, :640, :]), start(w_other.at[r], w.at[r, 640:, :])] for r in range(8)]
    copies = []
    for half in (range(3), range(3, 8)):
        wait(lhs_in + flat(w_in[r] for r in half))
        for m in range(4):
            rows = slice(ROWS * m, ROWS * m + ROWS)
            for r in half:
                stage[rows, 256 * r : 256 * r + 256] = dot(lhs[rows, :], w[r]).astype(BF)
            if 7 in half:
                for p in (2 * m, 2 * m + 1):
                    to = pl.ds(pl.multiple_of(sc[2 * p] // 2 * 128, 128), 128)
                    copies.append(start(stage.at[128 * p : 128 * p + 128, :], out.at[to, :]))
    wait(copies)


def branch_part(merged, act_own, act_other, w_own, w_other, dep):
    return call(
        branch_body,
        anywhere(6),
        pl.BlockSpec(memory_space=pl.ANY),
        shape((1024, 2048)),
        (merged, act_own, act_other, w_own, w_other, dep),
        "branch_part",
        [pltpu.VMEM((1024, 1280), BF), pltpu.VMEM((8, 1280, 256), BF), pltpu.VMEM((1024, 2048), BF), *HUGE],
    )


def grad_in_body(cot, w_own, w_other, *refs):
    core, rows_sc = feature_blocks()[8], row_blocks()
    slope_in, (merged, act, dep) = refs[:2], refs[2:5]
    gout_out, gm_out, gh_out, g2_out, colsum = refs[5], refs[6:8], refs[8:10], refs[10], refs[11:13]
    gout, w, slope, gm, gh, lhs, stage, sems = refs[13], refs[14], refs[15:17], refs[17:19], refs[19:21], *refs[21:]
    start = copier(sems)

    def tile(j):
        copies = []
        for r, cols in enumerate(blocks_of()):
            for first, source, at in ((0, w_own, 256 * j), (640, w_other, 256 * j - 640)):
                lo, hi = max(at, 0), min(at + 256, 640)
                if lo < hi:
                    copies.append(start(source.at[r, lo:hi, :], w.at[lo + first : hi + first, cols]))
        return copies

    gout_in = [start(cot.at[rows_sc[r], core], gout.at[64 * r : 64 * r + 64, :]) for r in range(16)]
    w_in = [tile(0)]
    slope_copies = [start(a, b) for a, b in zip(slope_in, slope)]
    w_in += [tile(j) for j in range(1, 5)]
    lhs_in = [start(merged.at[:, 128:], lhs.at[:, :128]), start(act, lhs.at[:, 128:])]
    totals = [[jnp.zeros((1, 128), F32)] * 4 for _ in range(2)]
    copies = []
    for j in range(5):
        if j == 0:
            wait(gout_in + w_in[0] + slope_copies)
            copies.append(start(gout, gout_out))
        if j == 1:
            wait(flat(w_in) + lhs_in)
        for m in range(4):
            rows = slice(ROWS * m, ROWS * m + ROWS)
            result = dot_nt(gout[rows, :], w[256 * j : 256 * j + 256, :])
            for k in range(2):
                half, strip = (2 * j + k) // 5, (2 * j + k) % 5
                part = result[:, 128 * k : 128 * k + 128]
                if strip == 0:
                    gm[half][rows, :] = part.astype(BF)
                    continue
                cols = slice(128 * (strip - 1), 128 * strip)
                part = (part * slope[half][rows, cols].astype(F32)).astype(BF)
                gh[half][rows, cols] = part
                totals[half][strip - 1] += jnp.sum(part.astype(F32), axis=0, keepdims=True)
    for core in range(2):
        for strip in range(4):
            colsum[core][:, 128 * strip : 128 * strip + 128] = totals[core][strip]
    for a, b in zip((*gm, *gh), (*gm_out, *gh_out)):
        copies.append(start(a, b))
    for cols in blocks_of(512, 4):
        stage[:, cols] = dot_tn(lhs[...], gout[:, cols]).astype(BF)
        copies.append(start(stage.at[:, cols], g2_out.at[:, cols]))
    wait(copies)


def grad_in(cot, w_own, w_other, slope_own, slope_other, merged, act_other, dep):
    small, wide, whole = (1024, 128), (1024, 512), (1024, 2048)
    return call(
        grad_in_body,
        anywhere(8),
        anywhere(6) + vmem(2),
        [shape(whole)] + [shape(small)] * 2 + [shape(wide)] * 2 + [shape((640, 2048))] + [shape((1, 512), F32)] * 2,
        (cot, w_own, w_other, slope_own, slope_other, merged, act_other, dep),
        "grad_in",
        [pltpu.VMEM(whole, BF), pltpu.VMEM((1280, 2048), BF)]
        + [pltpu.VMEM(wide, BF)] * 2
        + [pltpu.VMEM(small, BF)] * 2
        + [pltpu.VMEM(wide, BF)] * 2
        + [pltpu.VMEM((1024, 640), BF), pltpu.VMEM((640, 2048), BF), *HUGE],
    )


def gnormed_body(q_own, gh_own, q_other, gh_other, acts_in, *refs):
    sc = feature_blocks()
    w_own, w_other, dep, cot_sum, attn_sums, up_own, up_other = refs[:8], refs[8:16], *refs[16:21]
    outs, vec_own, vec_send, (lhs, w, acts, stage, sems) = refs[21:27], refs[27], refs[28], refs[29:]
    places = message_places(outs, 128)
    start = copier(sems)
    parts = ((q_own, 0), (gh_own, 384), (q_other, 896), (gh_other, 1280))

    def rows_in(m):
        rows = slice(ROWS * m, ROWS * m + ROWS)
        copies = [start(a.at[rows, :], lhs.at[rows, c : c + a.shape[1]]) for a, c in parts]
        return copies + [start(acts_in.at[rows, :], acts.at[rows, :])]

    def tile(r):
        rows = slice(256 * r, 256 * r + 256)
        return [start(w_own[r], w.at[rows, :896]), start(w_other[r], w.at[rows, 896:])]

    lhs_in = {3: rows_in(3)}
    w_in = [tile(r) for r in range(8)]
    lhs_in.update({m: rows_in(m) for m in range(3)})
    totals = [[jnp.zeros((1, 256), F32)] * 8 for _ in range(2)]
    copies = []
    for m, first, last in ((3, 0, 3), (3, 3, 8), (0, 0, 8), (1, 0, 8), (2, 0, 8)):
        rows = slice(ROWS * m, ROWS * m + ROWS)
        if m == 3:
            wait(lhs_in[3] + flat(w_in[first:last]))
        if m == 0:
            wait(lhs_in[0] + lhs_in[1] + lhs_in[2])
        for r in range(first, last):
            cols = slice(256 * r, 256 * r + 256)
            result = dot_nt(lhs[rows, :], w[cols, :])
            totals[0][r] += jnp.sum(result, axis=0, keepdims=True)
            totals[1][r] += jnp.sum(result * acts[rows, cols].astype(F32), axis=0, keepdims=True)
            stage[rows, cols] = result.astype(BF)
        if last == 8:
            for p in (2 * m, 2 * m + 1):
                copies.append(start(stage.at[128 * p : 128 * p + 128, :], places[p]))
    for vec, half, up in ((vec_own, 0, up_own), (vec_send, 1, up_other)):
        vec[0:1, :] = cot_sum[...]
        for k in range(2):
            for r in range(8):
                vec[k + 1 : k + 2, pl.ds(pl.multiple_of(sc[r] * 256, 256), 256)] = totals[k][r]
        vec[3:4, :384], vec[3:4, 384:896] = attn_sums[half], up[...]
        vec[3:4, 896:] = jnp.zeros((1, 2048 - 896), F32)
    wait(copies)


def gnormed_part(q_own, gh_own, q_other, gh_other, acts, w_own, w_other, dep, *vectors):
    whole, piece = (1024, 2048), shape((128, 2048))
    *outs, vec_own, vec_send = call(
        gnormed_body,
        anywhere(22) + vmem(4),
        anywhere(6) + vmem(2),
        [shape((256, 2048))] * 2 + [piece] * 4 + [shape((4, 2048), F32)] * 2,
        (q_own, gh_own, q_other, gh_other, acts, *w_own, *w_other, dep, *vectors),
        "gnormed_part",
        [pltpu.VMEM((1024, 1792), BF), pltpu.VMEM((2048, 1792), BF), pltpu.VMEM(whole, BF), pltpu.VMEM(whole, BF), *HUGE],
    )
    return outs, vec_own, vec_send


def second_body(merged, act, gout, received, dep, *refs):
    sc = feature_blocks()
    places, (lhs, rhs, held, stage, sems) = message_places(refs[:6], 640), refs[6:]
    start = copier(sems)
    lhs_in = [start(merged.at[:, :128], lhs.at[:, :128]), start(act, lhs.at[:, 128:])]
    ins = []
    for r in range(8):
        cols = pl.ds(pl.multiple_of(sc[r] * 256, 256), 256)
        ins.append([start(gout.at[:, cols], rhs.at[r]), start(received.at[:, cols], held.at[r])])
    copies = []
    for r in range(8):
        if r == 0:
            wait(lhs_in + flat(ins[:3]))
        if r == 3:
            wait(flat(ins))
        result = dot_tn(lhs[...], rhs[r])
        stage[r] = (result + held[r].astype(F32)).astype(BF)
        copies.append(start(stage.at[r], places[r]))
    wait(copies)


def second_grad(merged, act, gout, received, dep):
    return call(
        second_body,
        anywhere(5),
        anywhere(6),
        [shape((1280, 256))] * 2 + [shape((640, 256))] * 4,
        (merged, act, gout, received, dep),
        "second_grad",
        [pltpu.VMEM((1024, 640), BF), pltpu.VMEM((8, 1024, 256), BF)]
        + [pltpu.VMEM((8, 640, 256), BF)] * 2
        + [*HUGE],
    )


def first_body(blocks, count, gqkv, gh, acts, received, *refs):
    outs, (lhs, rhs, held, stage, sems) = refs[count - 4 : -5], refs[-5:]
    places = [out.at[256 * k : 256 * k + 256, :] for out in outs for k in range(out.shape[0] // 256)]
    start = copier(sems)
    rhs_in = [start(gqkv, rhs.at[:, :384]), start(gh, rhs.at[:, 384:])]
    ins = []
    for k, r in enumerate(blocks):
        rows = slice(256 * r, 256 * r + 256)
        ins.append([start(acts.at[:, rows], lhs.at[k]), start(received.at[rows, :], held.at[k])])
    copies = []
    for k in range(4):
        if k == 0:
            wait(rhs_in + ins[0])
        if k == 1:
            wait(flat(ins))
        result = dot_tn(lhs[k], rhs[...])
        stage[k] = (result + held[k].astype(F32)).astype(BF)
        copies.append(start(stage.at[k], places[k]))
    wait(copies)


def first_grad(blocks, rows, *args):
    return call(
        functools.partial(first_body, blocks, len(args)),
        anywhere(len(args)),
        anywhere(1024 // rows),
        [shape((rows, 896))] * (1024 // rows),
        args,
        "first_grad",
        [pltpu.VMEM((4, 1024, 256), BF), pltpu.VMEM((1024, 896), BF)]
        + [pltpu.VMEM((4, 256, 896), BF)] * 2
        + [*HUGE],
    )


def rotary_tables(length):
    frequency = np.float32(10000.0) ** (-(np.arange(ROT // 2, dtype=np.float32) * 2.0 / ROT))
    angles = np.arange(length, dtype=np.float32)[:, None] * frequency.astype(np.float32)[None, :]
    cosine, sine = np.cos(angles), np.sin(angles)
    one = np.ones((length, HEAD_DIM - ROT), np.float32)
    zero_half, zero = np.zeros_like(sine), np.zeros_like(one)
    cos_t = np.concatenate([cosine, cosine, one] * 2, axis=1)
    low_t = np.concatenate([-sine, zero_half, zero] * 2, axis=1)
    high_t = np.concatenate([zero_half, sine, zero] * 2, axis=1)
    return tuple(jnp.asarray(a, F32) for a in (cos_t, low_t, high_t))


def by_kind(a):
    return jnp.swapaxes(a.reshape(2, 3, HEAD_DIM), 0, 1).reshape(384)


def shards(
    tokens,
    attn_weight,
    attn_bias,
    dense_weight,
    dense_bias,
    up_weight,
    up_bias,
    down_weight,
    down_bias,
    norm_gain,
    norm_bias,
    cotangent,
):
    tables = rotary_tables(16 * tokens.shape[1])
    gain_row, bias_row = norm_gain[None, :], norm_bias[None, :]

    cot = lax.all_gather(cotangent, "tensor", axis=0)
    acts_own, acts_send, cot_sum, f0, s0 = pre(
        tokens, cotangent, gain_row, bias_row, attn_weight, up_weight, dense_weight, down_weight
    )
    swapped = core_swap(acts_send)
    f1, f2, f4, f0x = zz_swap(f0), y_up(f0), y_down(f0), core_swap(f0)
    s_own = lax.all_gather(s0, "dp", axis=0)
    a0 = join(acts_own, swapped)
    a2, a4, a1 = x_up(a0), x_down(a0), z_swap(a0)
    f1 = tie(f1, f2, f4, a0)
    f3, f5, f1x = y_up(f1), y_down(f1), core_swap(f1)
    f2 = tie(f2, f1)
    f6, f2x, f4x = y_up(f2), core_swap(f2), core_swap(f4)
    a2 = tie(a2, a4, f2)
    a6 = x_up(a2)
    a1 = tie(a1, a2, f3, f5)
    a3, a5 = x_up(a1), x_down(a1)
    f5 = tie(f5, a1)
    f7, f5x = y_down(f5), core_swap(f5)
    a5 = tie(a5, f6)
    a7 = x_down(a5)
    f3 = tie(f3, a5, a6)
    f3x = core_swap(f3)
    f6 = tie(f6, f7, a3, f3)
    f6x, f7x = core_swap(f6), core_swap(f7)
    biases = tie(jnp.concatenate([by_kind(attn_bias), up_bias])[None, :], f1)
    other_biases = core_swap(biases)
    f_own, f_other = [f0, f1, f2, f3, f4, f5, f6, f7], [f0x, f1x, f2x, f3x, f4x, f5x, f6x, f7x]

    acts, *rest = project([a0, a1, a2, a3, a4, a5, a6, a7], f_own, f_other, biases, other_biases, tables)
    qkv_own, qkv_other, (act_own, act_other), (slope_own, slope_other) = rest[:3], rest[3:6], rest[6:8], rest[8:]
    merged, lse = attn_fwd(qkv_own, qkv_other, acts)
    s_own = tie(s_own, acts)
    s_other = core_swap(s_own)
    br = branch_part(merged, act_own, act_other, s_own, s_other, acts)
    group = [[2 * p + c for p in range(8)] for c in range(2)]
    br_sum = lax.psum_scatter(br, "tensor", scatter_dimension=0, axis_index_groups=group, tiled=True)

    gout, gm_own, gm_other, gh_own, gh_other, g2_other, up_sum_own, up_sum_other = grad_in(
        cot, s_own, s_other, slope_own, slope_other, merged, act_other, br
    )
    g2_received = core_swap(g2_other)
    gq_own, gq_other, g1_other, attn_sums = attn_bwd(
        qkv_own, qkv_other, lse, gm_own, gm_other, tables, acts, gh_other, gout
    )
    g1_received = core_swap(g1_other)
    g2_up, g2_down, g2_0, g2_1, g2_3, g2_4 = second_grad(merged, act_own, gout, g2_received, gq_own)
    g2_u, g2_d = y_up(g2_up), y_down(g2_down)
    (gn_up, gn_down, gn_0, gn_1, gn_3, gn_4), vec, vec_send = gnormed_part(
        gq_own, gh_own, gq_other, gh_other, acts, f_own, f_other, g2_0, cot_sum, attn_sums, up_sum_own, up_sum_other
    )
    gn_u, gn_d = x_up(gn_up), x_down(gn_down)
    step = core_swap(vec_send)

    n_one, n_two, m_one, m_two = slice(0, 128), slice(128, 256), slice(0, 256), slice(256, 512)
    one, two, last = slice(0, 640), slice(640, 1280), slice(64, 128)
    vec, g2_4, g2_3 = adds((vec, step), (g2_4, (g2_u, one)), (g2_3, (g2_d, one)), deps=(gn_0,), name="early_adds")
    step = zz_swap(vec)
    g2_ua, g2_dz = y_up(g2_4), y_down(g2_3)
    g1_up, g1_down = first_grad((6, 5, 7, 2), 512, gq_own, gh_own, acts, g1_received, g2_4)
    g1_u, g1_d = y_up(g1_up), y_down(g1_down)
    (vec,) = adds((vec, step), deps=(g1_up, g2_ua, g2_dz))
    step = z_swap(vec)
    g1_0, g1_1, g1_3, g1_4 = first_grad((0, 1, 3, 4), 256, gq_own, gh_own, acts, g1_received, vec)
    br_sum = tie(br_sum, g1_0)
    br_received = core_swap(br_sum[64:])
    layer_out = post_out(tokens, br_sum, br_received, (dense_bias + down_bias)[None, :])
    gn_4, gn_3, vec, g2_1 = adds(
        (gn_4, (gn_u, n_one)),
        (gn_3, (gn_d, n_one)),
        (vec, (step, "top")),
        (g2_1, (g2_u, two), g2_dz),
        deps=(layer_out,),
        name="early_adds",
    )
    gn_ua, gn_dz = x_up(gn_4), x_down(gn_3)
    step, g2_z = y_pair(vec), zz_swap(g2_1)
    g1_4, g1_3 = adds((g1_4, (g1_u, m_one)), (g1_3, (g1_d, m_one)), deps=(gn_4,))
    g1_ua, g1_dz = y_up(g1_4), y_down(g1_3)
    gn_1, vec = adds((gn_1, (gn_u, n_two), gn_dz), (vec, step), deps=(g1_4, gn_ua, g2_z))
    gn_z = z_swap(gn_1)
    step = y_cross(vec)
    g1_1, vec = adds((g1_1, (g1_u, m_two), g1_dz), (vec, step), deps=(gn_1, g1_ua))
    g1_z = zz_swap(g1_1)
    step = x_pair(vec)
    dense_grad, down_grad, attn_bias_grad, up_bias_grad = finish_second(g2_0, g2_ua, g2_d, g2_z, vec, vec)
    gn_send, vec = adds(
        ((gn_0, last), (gn_ua, last), (gn_d, slice(192, 256)), (gn_z, last)), (vec, (step, "top")), deps=(dense_grad,)
    )
    gn_received, step = core_swap(gn_send), x_cross(vec)
    grad_tokens = post_grad(tokens, cotangent, (gn_0, gn_ua, gn_d, gn_z), gn_received, gain_row)
    out_bias_grad, norm_gain_grad, norm_bias_grad = finish_vector(
        (vec, step), norm_bias[None, :], norm_gain[None, :], grad_tokens
    )
    attn_grad, up_grad = finish_first(g1_0, g1_ua, g1_d, g1_z, out_bias_grad)
    out_bias_grad = out_bias_grad[0]
    return (
        layer_out,
        grad_tokens,
        attn_grad,
        attn_bias_grad[0],
        dense_grad,
        out_bias_grad,
        up_grad,
        up_bias_grad[0],
        down_grad,
        out_bias_grad,
        norm_gain_grad[0],
        norm_bias_grad[0],
    )


def solution(mesh):
    in_specs = (
        P("dp", "tensor", None),
        P("dp", "tensor"),
        P("tensor"),
        P("tensor", "dp"),
        P(),
        P("dp", "tensor"),
        P("tensor"),
        P("tensor", "dp"),
        P(),
        P(),
        P(),
        P("dp", "tensor", None),
    )
    out_specs = (
        P("dp", "tensor", None),
        P("dp", "tensor", None),
        P("dp", "tensor"),
        P("tensor"),
        P("tensor", "dp"),
        P(),
        P("dp", "tensor"),
        P("tensor"),
        P("tensor", "dp"),
        P(),
        P(),
        P(),
    )
    return jax.shard_map(shards, mesh=mesh, in_specs=in_specs, out_specs=out_specs, check_vma=False)
```
